768 devices in a mesh: lat: 96 (over z, y), lon: 8 (over x, core).
Axes of the slice: x: 4, y: 8, z: 12, core: 2. Of those that a mesh axis runs over, the one named last changes fastest.
Arguments:
- tracers: float32 [4, 8, 1536, 3072], P(None, None, 'lat', 'lon'), may hold values from -6 to 6
- east_velocity: float32 [8, 1536, 3072], P(None, 'lat', 'lon'), may hold values from -0.2 to 0.2
- north_velocity: float32 [8, 1536, 3072], P(None, 'lat', 'lon'), may hold values from -0.2 to 0.2
- diffusivity: float32 [8, 1536, 3072], P(None, 'lat', 'lon'), may hold values from 0.02 to 0.12
- cross_diffusivity: float32 [8, 1536, 3072], P(None, 'lat', 'lon'), may hold values from -0.2 to 0.2
- depth_levels: int32 [1536, 3072], P('lat', 'lon'), may hold values from 0 to 8
- land_mask: int32 [36864], P(('lat', 'lon')), may hold values 0 or 1
- ocean_state: bfloat16 [36864, 8, 128], P(('lat', 'lon')), may hold values from -5.5 to 5.5
- atm_state: float32 [36864, 8, 128], P(('lat', 'lon')), may hold values from -6 to 6
- exchange_coef: float32 [36864, 128], P(('lat', 'lon')), may hold values from 0.1 to 9
- sunlight: float32 [36864, 128], P(('lat', 'lon')), may hold values from 0.5 to 2
- mixing: float32 [8, 8], replicated, may hold values from -2 to 2
- o2a_dest: int32 [36864], P(('lat', 'lon')), may hold values from 0 to 767, as said below
- o2a_slot: int32 [36864], P(('lat', 'lon')), may hold values from 0 to 47, as said below
- a2o_source: int32 [36864], P(('lat', 'lon')), may hold values from 0 to 767, as said below
- a2o_tile: int32 [36864], P(('lat', 'lon')), may hold values from 0 to 47
Outputs:
- new_tracers: float32 [4, 8, 1536, 3072], P(None, None, 'lat', 'lon')
- ocean_flux: bfloat16 [36864, 8, 128], P(('lat', 'lon'))
The draws below stay inside these ranges and needn't reach their ends.
Inputs may be any that keep to these rules, and one draw needn't show every extreme that they name: `o2a_dest`: its lat index is the source device's lat index plus -1, 0 or 1 modulo 96. Exactly 16 tiles of every device go to each of these three rows, at most 6 to one device, and in each of those rows one device receives exactly 6 of them. `o2a_slot`: the tiles that one device receives fill its places 0 to 47 once each. a2o_source and a2o_tile name, for each place, the ocean tile that o2a_dest and o2a_slot send there.
All inputs are finite; a program needn't handle non-finite values. No bound on the sum of `land_mask` on one device may be relied on, other than what follows from the above.
Results may differ from the reference program's by a relative error of at most 0.002.
The reference program's roundings to bfloat16 on the way count: a program that leaves them out, or rounds other values in their place, can miss the bound.
Values may be sent and summed in bfloat16 or wider, within the bound.
No kernel may reach another device: no remote copies, remote signals or barrier semaphores. Data moves between devices by JAX's collectives and lax.ppermute only.
A program may use at most 32 MiB of HBM per device.

```python
import math
import jax
import jax.numpy as jnp
from jax import lax

BLOCK_ROWS = 16
BLOCK_COLS = 384
LEVELS = 8
TRACERS = 4
FIELDS = 8
TILE = 128
DEV_TILES = 48
ROW_TILES = 16
PAIR_MOST = 6
TILES_ALL = 36864
NY = 1536
NX = 3072
N_LAT = 96
N_LON = 8


def lon_step(rank_values, lane_count):
    return jnp.where(rank_values < PAIR_MOST, 0, 1 + (rank_values - PAIR_MOST) % lane_count)


def build_maps(key):
    devices_total = N_LAT * N_LON
    key_tiles, key_turn, key_slots = jax.random.split(key, 3)
    tile_ranks = jax.vmap(lambda subkey: jax.random.permutation(subkey, DEV_TILES))(jax.random.split(key_tiles, devices_total)).astype(jnp.int32)
    row_offset = tile_ranks // ROW_TILES
    group_rank = tile_ranks % ROW_TILES
    lane_count = N_LON - 1
    step_values = lon_step(group_rank, lane_count)
    sources = jnp.arange(devices_total, dtype=jnp.int32)
    source_lat = (sources // N_LON)[:, None]
    source_lon = (sources % N_LON)[:, None]
    turns = jax.random.randint(key_turn, (N_LAT, 3), 0, N_LON, dtype=jnp.int32)
    turn_value = turns[source_lat, row_offset]
    dest_lat = (source_lat + row_offset - 1) % N_LAT
    dest_lon = (source_lon + turn_value + step_values) % N_LON
    destination = (dest_lat * N_LON + dest_lon).astype(jnp.int32)
    others = jnp.arange(N_LON, dtype=jnp.int32)
    profile = jnp.sum((lon_step(jnp.arange(ROW_TILES, dtype=jnp.int32), lane_count)[:, None] == others[None, :]).astype(jnp.int32), axis=0)
    earlier_counts = profile[(dest_lon[..., None] - others - turn_value[..., None]) % N_LON] * (others < source_lon[..., None]).astype(jnp.int32)
    offset_in = jnp.sum(earlier_counts, axis=-1)
    within = jnp.where(step_values == 0, group_rank, (group_rank - PAIR_MOST) // lane_count)
    canonical = row_offset * ROW_TILES + offset_in + within
    slot_perms = jax.vmap(lambda subkey: jax.random.permutation(subkey, DEV_TILES))(jax.random.split(key_slots, devices_total)).astype(jnp.int32)
    slots = slot_perms[destination, canonical].astype(jnp.int32)
    flat_index = (destination * DEV_TILES + slots).reshape(-1)
    tile_ids = jnp.broadcast_to(jnp.arange(DEV_TILES, dtype=jnp.int32)[None, :], (devices_total, DEV_TILES)).reshape(-1)
    owners = jnp.broadcast_to(sources[:, None], (devices_total, DEV_TILES)).reshape(-1)
    a2o_source = jnp.zeros((devices_total * DEV_TILES,), jnp.int32).at[flat_index].set(owners)
    a2o_tile = jnp.zeros((devices_total * DEV_TILES,), jnp.int32).at[flat_index].set(tile_ids)
    return (destination.reshape(-1), slots.reshape(-1), a2o_source, a2o_tile)


def draw_o2a_dest(key, part):
    result = build_maps(key)
    return result[0]


def draw_o2a_slot(key, part):
    result = build_maps(key)
    return result[1]


def draw_a2o_source(key, part):
    result = build_maps(key)
    return result[2]


def draw_a2o_tile(key, part):
    result = build_maps(key)
    return result[3]


def draw_ocean_state(key, part):
    key = jax.random.fold_in(key, 21)
    key_base, key_noise = jax.random.split(key)
    blocks = TILES_ALL // DEV_TILES
    field_offset = jax.random.uniform(key_base, (blocks, FIELDS), jnp.float32, -1.5, 1.5)
    shape = (TILES_ALL, FIELDS, TILE)
    jitter = jnp.clip(jax.random.normal(key_noise, shape, jnp.float32), -4.0, 4.0)
    block_base = jnp.repeat(field_offset, DEV_TILES, axis=0)[:, :, None]
    return (block_base + jitter).astype(jnp.bfloat16)


def draw_exchange_coef(key, part):
    key = jax.random.fold_in(key, 31)
    band_row = jnp.arange(TILES_ALL) // DEV_TILES // N_LON
    latitude_share = band_row.astype(jnp.float32) / (N_LAT - 1)
    spread_part = jnp.exp(jax.random.uniform(key, (TILES_ALL, TILE), jnp.float32, jnp.log(0.1), 0.0))
    gradient = 1.0 + 2.0 * latitude_share
    return spread_part * gradient[:, None]


def touch_ends(values, rng, least, largest):
    index_at = [jax.random.randint(jax.random.fold_in(rng, axis), (), 0, length) for axis, length in enumerate(values.shape)]
    longest = values.shape.index(max(values.shape))
    neighbour = index_at[:longest] + [(index_at[longest] + 1) % values.shape[longest]] + index_at[longest + 1:]
    return values.at[tuple(index_at)].set(least).at[tuple(neighbour)].set(largest)


def level_of(stream_key, shape, cuts, smallest, high):
    level = 1.0
    for position, blocks in cuts:
        steps = jax.random.uniform(jax.random.fold_in(jax.random.fold_in(stream_key, 6), position), (blocks,), jnp.float32, smallest / len(cuts), high / len(cuts))
        level = level * jnp.repeat(jnp.exp(steps), shape[position] // blocks).reshape((-1,) + (1,) * (len(shape) - 1 - position))
    return level


def bell_draw(stream_key, shape, deviation, bound, pieces=(), kind=jnp.bfloat16):
    values = jax.random.normal(stream_key, shape, jnp.float32) * deviation
    if len(pieces) > 0:
        values = level_of(stream_key, shape, pieces, -0.22, 0.18) * values
    return jnp.clip(values, min=-bound, max=bound).astype(kind)


def setup_inputs(seed: int = 0) -> dict:
    splits = jax.random.split(jax.random.key(seed), 17)
    return {
        "tracers": bell_draw(splits[0], (TRACERS, LEVELS, NY, NX), 1.0, 6.0, ((2, 96), (3, 8)), jnp.float32),
        "east_velocity": jnp.clip(jax.random.uniform(splits[1], (LEVELS, NY, NX), jnp.float32, -0.2, 0.2) * level_of(splits[1], (LEVELS, NY, NX), ((1, 96), (2, 8)), -0.4, 0.0), -0.2, 0.2),
        "north_velocity": jnp.clip(jax.random.uniform(splits[2], (LEVELS, NY, NX), jnp.float32, -0.2, 0.2) * level_of(splits[2], (LEVELS, NY, NX), ((1, 96), (2, 8)), -0.4, 0.0), -0.2, 0.2),
        "diffusivity": jnp.clip(jnp.exp(math.log(0.12) - 1.7917595 * jax.random.uniform(splits[3], (LEVELS, NY, NX), jnp.float32) ** level_of(splits[3], (LEVELS, NY, NX), ((1, 96), (2, 8)), -0.2, 0.2)), 0.02, 0.12),
        "cross_diffusivity": jnp.clip(jax.random.uniform(splits[4], (LEVELS, NY, NX), jnp.float32, -0.2, 0.2) * level_of(splits[4], (LEVELS, NY, NX), ((1, 96), (2, 8)), -0.4, 0.0), -0.2, 0.2),
        "depth_levels": touch_ends(jax.random.randint(splits[5], (NY, NX), 0, LEVELS + 1), jax.random.fold_in(splits[5], 1), 0, LEVELS).astype(jnp.int32),
        "land_mask": touch_ends((jax.random.randint(splits[6], (TILES_ALL,), 0, 4) < 3).astype(jnp.int32), jax.random.fold_in(splits[6], 1), 0, 1),
        "ocean_state": draw_ocean_state(jax.random.fold_in(splits[16], 71), 0),
        "atm_state": bell_draw(splits[8], (TILES_ALL, FIELDS, TILE), 1.0, 6.0, ((0, 768),), jnp.float32),
        "exchange_coef": draw_exchange_coef(jax.random.fold_in(splits[16], 71), 0),
        "sunlight": jnp.clip(jnp.exp(math.log(2.0) - 1.3862944 * jax.random.uniform(splits[10], (TILES_ALL, TILE), jnp.float32) ** level_of(splits[10], (TILES_ALL, TILE), ((0, 768),), -0.2, 0.2)), 0.5, 2.0),
        "mixing": bell_draw(splits[11], (FIELDS, FIELDS), FIELDS ** -0.5, 2.0, (), jnp.float32),
        "o2a_dest": draw_o2a_dest(jax.random.fold_in(splits[16], 71), 0),
        "o2a_slot": draw_o2a_slot(jax.random.fold_in(splits[16], 71), 0),
        "a2o_source": draw_a2o_source(jax.random.fold_in(splits[16], 71), 0),
        "a2o_tile": draw_a2o_tile(jax.random.fold_in(splits[16], 71), 0),
    }


surface_gain = 0.5


def face_flux(left_value, right_value, velocity, left_kappa, right_kappa, left_mask, right_mask):
    upwind = jnp.where(velocity > 0.0, left_value, right_value)
    kappa_face = 0.5 * (left_kappa + right_kappa)
    return left_mask * right_mask * (velocity * upwind - kappa_face * (right_value - left_value))


def window(values, row_shift, column_shift):
    rows_total = values.shape[-2]
    cols_total = values.shape[-1]
    return values[..., 1 + row_shift:rows_total - 1 + row_shift, 1 + column_shift:cols_total - 1 + column_shift]


def advance(padded, east_pad, north_pad, kappa_pad, mask_pad, cross, forcing, top_flag):
    center = window(padded, 0, 0)
    kappa_center = window(kappa_pad, 0, 0)
    mask_center = window(mask_pad, 0, 0)
    east_flux = face_flux(center, window(padded, 0, 1), window(east_pad, 0, 0), kappa_center, window(kappa_pad, 0, 1), mask_center, window(mask_pad, 0, 1))
    west_flux = face_flux(window(padded, 0, -1), center, window(east_pad, 0, -1), window(kappa_pad, 0, -1), kappa_center, window(mask_pad, 0, -1), mask_center)
    north_flux = face_flux(center, window(padded, 1, 0), window(north_pad, 0, 0), kappa_center, window(kappa_pad, 1, 0), mask_center, window(mask_pad, 1, 0))
    south_flux = face_flux(window(padded, -1, 0), center, window(north_pad, -1, 0), window(kappa_pad, -1, 0), kappa_center, window(mask_pad, -1, 0), mask_center)
    corners = (window(mask_pad, 1, 1) * window(padded, 1, 1) - window(mask_pad, 1, -1) * window(padded, 1, -1)
               - window(mask_pad, -1, 1) * window(padded, -1, 1) + window(mask_pad, -1, -1) * window(padded, -1, -1))
    tendency = -(east_flux - west_flux) - (north_flux - south_flux) + cross * mask_center * corners
    updated = center + mask_center * tendency
    return updated + ((mask_center * surface_gain) * forcing) * top_flag


def couple(received, atm_state, exchange_coef, sunlight, mixing):
    ocean_values = received.astype(jnp.float32)
    weights = exchange_coef[:, None, :]
    band_mean = jnp.sum(weights * ocean_values, axis=(0, 2)) / jnp.sum(exchange_coef)
    drive = atm_state + band_mean[None, :, None] - 2.0 * ocean_values
    mixed = jnp.einsum("fg,tgp->tfp", mixing, drive, precision=lax.Precision.HIGHEST)
    fluxes = weights * mixed
    fluxes = fluxes.at[:, 0, :].add(exchange_coef * sunlight)
    return fluxes.astype(jnp.bfloat16)


def pad_grid(values):
    wrapped = jnp.concatenate([values[..., -1:], values, values[..., :1]], axis=-1)
    widths = [(0, 0)] * (values.ndim - 2) + [(1, 1), (0, 0)]
    return jnp.pad(wrapped, widths)


def tiles_to_grid(tiles):
    per_row = BLOCK_COLS // TILE
    channels = tiles.shape[1]
    shaped = tiles.reshape(N_LAT, N_LON, BLOCK_ROWS, per_row, channels, TILE)
    return shaped.transpose(4, 0, 2, 1, 3, 5).reshape(channels, NY, NX)


def reference(tracers, east_velocity, north_velocity, diffusivity, cross_diffusivity, depth_levels, land_mask, ocean_state, atm_state, exchange_coef, sunlight, mixing, o2a_dest, o2a_slot, a2o_source, a2o_tile):
    devices_total = N_LAT * N_LON
    sea_tiles = land_mask.astype(jnp.bfloat16)[:, None, None]
    masked = ocean_state * sea_tiles
    target = (o2a_dest * DEV_TILES + o2a_slot).astype(jnp.int32)
    received = jnp.zeros_like(masked).at[target].set(masked)
    fluxes = jax.vmap(couple, in_axes=(0, 0, 0, 0, None))(
        received.reshape(devices_total, DEV_TILES, FIELDS, TILE),
        atm_state.reshape(devices_total, DEV_TILES, FIELDS, TILE),
        exchange_coef.reshape(devices_total, DEV_TILES, TILE),
        sunlight.reshape(devices_total, DEV_TILES, TILE),
        mixing)
    fluxes = fluxes.reshape(TILES_ALL, FIELDS, TILE)
    anchor = (a2o_source * DEV_TILES + a2o_tile).astype(jnp.int32)
    returned = jnp.zeros_like(fluxes).at[anchor].set(fluxes)
    ocean_flux = returned * sea_tiles
    heat_total = jnp.sum(ocean_flux[:, 0, :].astype(jnp.float32))
    correction = heat_total / (TILES_ALL * TILE)
    forcing = tiles_to_grid(ocean_flux[:, :TRACERS, :].astype(jnp.float32))
    forcing = forcing.at[0].add(-correction)
    sea_cells = tiles_to_grid(jnp.broadcast_to(land_mask.astype(jnp.float32)[:, None, None], (TILES_ALL, 1, TILE)))[0]
    bottom = depth_levels.astype(jnp.float32) * sea_cells
    levels_axis = jnp.arange(LEVELS, dtype=jnp.float32)[:, None, None]
    ocean_mask = (levels_axis < bottom[None]).astype(jnp.float32)
    top_flags = (jnp.arange(LEVELS) == 0).astype(jnp.float32)

    def one_level(level_inputs):
        tracer_level, east_level, north_level, kappa_level, mask_level, cross_level, top_flag = level_inputs
        return advance(pad_grid(tracer_level), pad_grid(east_level), pad_grid(north_level), pad_grid(kappa_level), pad_grid(mask_level), cross_level, forcing, top_flag)

    stacked = lax.map(one_level, (jnp.moveaxis(tracers, 1, 0), east_velocity, north_velocity, diffusivity, ocean_mask, cross_diffusivity, top_flags))
    new_tracers = jnp.moveaxis(stacked, 0, 1)
    return new_tracers, ocean_flux
```

```python
import functools

import jax
import jax.numpy as jnp
from jax import lax
from jax.experimental import pallas as pl
from jax.experimental.pallas import tpu as pltpu
from jax.sharding import PartitionSpec as P

F32 = jnp.float32
BF16 = jnp.bfloat16
PAIR = 6
SLOTS = 20
LAND = 2.0**100
LAND_TEST = 2.0**90
VMEM = pl.BlockSpec(memory_space=pltpu.VMEM)
SMEM = pl.BlockSpec(memory_space=pltpu.SMEM)


def iota(shape, dim):
    return lax.broadcasted_iota(jnp.int32, shape, dim)


def block_of(ref, block):
    return ref[..., 128 * block : 128 * block + 128]


def tile_column(land_ref, block):
    rows = iota((16, 128), 0)
    out = jnp.zeros((16, 128), F32)
    for r in range(16):
        out = jnp.where(rows == r, land_ref[3 * r + block].astype(F32), out)
    return out


def pack_kernel(lats, dest_ref, land_ref, state_ref, tracer_ref, east_ref, kappa_ref, depth_ref,
                out_ref, code_ref, count_ref):
    lat = lax.axis_index("lat")
    lon = lax.axis_index("lon")
    lons = 8
    for i in range(24):
        count_ref[i] = 0
    for t in range(48):
        dest = dest_ref[t]
        off = lax.shift_right_logical(dest, 3) - lat + 1
        off = jnp.where(off < 0, off + lats, jnp.where(off >= lats, off - lats, off))
        dlon = lax.bitwise_and(dest, 7)
        key = off * 8 + dlon
        rank = count_ref[key]
        count_ref[key] = rank + 1
        code_ref[t] = key * 8 + rank
        value = state_ref[t].astype(F32)
        value = jnp.where(land_ref[t] > 0, value, LAND)
        out_ref[dlon * SLOTS + off * PAIR + rank] = value.astype(BF16)
    lanes = iota((16, 128), 1)
    for block, lane, shift in ((2, 127, 1), (0, 0, lons - 1)):
        packed = jnp.zeros((16, 128), F32)
        for i in range(32):
            packed = jnp.where(lanes == i, block_of(tracer_ref, block)[i][:, lane : lane + 1], packed)
        for i in range(8):
            if block == 2:
                packed = jnp.where(lanes == 32 + i, block_of(east_ref, block)[i][:, lane : lane + 1], packed)
            packed = jnp.where(lanes == 40 + i, block_of(kappa_ref, block)[i][:, lane : lane + 1], packed)
        bottom = block_of(depth_ref, block)[...].astype(F32) * tile_column(land_ref, block)
        packed = jnp.where(lanes == 48, bottom[:, lane : lane + 1], packed)
        target = lax.rem(lon + shift, lons)
        out_ref[target * SLOTS + 18] = packed[:8].astype(BF16)
        out_ref[target * SLOTS + 19] = packed[8:].astype(BF16)


def rows_kernel(land_ref, came_ref, tracer_ref, north_ref, kappa_ref, depth_ref, up_ref, down_ref):
    lon = lax.axis_index("lon")
    west = lax.rem(lon + 7, 8)
    east = lax.rem(lon + 1, 8)
    subs = iota((8, 128), 0)
    for out_ref, first, row in ((up_ref, 12, 15), (down_ref, 0, 0)):
        for s in range(8):
            for k in range(PAIR):
                out_ref[s * PAIR + k] = came_ref[s * SLOTS + first + k]
        half, sub = (19, 7) if row else (18, 0)
        corners = (
            came_ref[west * SLOTS + half].astype(F32)[sub : sub + 1],
            None,
            came_ref[east * SLOTS + half].astype(F32)[sub : sub + 1],
        )
        for j in range(3):
            cols = slice(128 * j, 128 * j + 128)
            for k in range(4):
                out_ref[48 + 3 * k + j] = tracer_ref[8 * k : 8 * k + 8, row, cols].astype(BF16)
            if row:
                out_ref[48 + 12 + j] = north_ref[:, row, cols].astype(BF16)
            else:
                out_ref[48 + 12 + j] = jnp.zeros((8, 128), BF16)
            out_ref[48 + 15 + j] = kappa_ref[:, row, cols].astype(BF16)
            bottom = depth_ref[row : row + 1, cols].astype(F32) * land_ref[3 * row + j].astype(F32)
            last = jnp.where(subs == 0, bottom, 0.0)
            if j != 1:
                last = jnp.where(subs == 1, corners[j], last)
            out_ref[48 + 18 + j] = last.astype(BF16)


def couple_kernel(place_ref, came_ref, low_ref, high_ref, atm_ref, coef_ref, sun_ref, mixing_ref,
                  out_ref, got_ref):
    total = jnp.zeros((8, 128), F32)
    for q in range(48):
        code = place_ref[q]
        rank = lax.bitwise_and(code, 7)
        slon = lax.bitwise_and(lax.shift_right_logical(code, 3), 7)
        off = lax.shift_right_logical(code, 6)
        at = slon * PAIR + rank
        own = came_ref[slon * SLOTS + PAIR + rank].astype(F32)
        low = low_ref[at].astype(F32)
        high = high_ref[at].astype(F32)
        value = jnp.where(off == 1, own, jnp.where(off == 2, low, high))
        got_ref[q] = value
        total = total + coef_ref[q : q + 1, :] * jnp.where(value < LAND_TEST, value, 0.0)
    weight = jnp.sum(jnp.sum(coef_ref[...], axis=0, keepdims=True), axis=1, keepdims=True)
    band_mean = jnp.sum(total, axis=1, keepdims=True) / weight
    mixing = mixing_ref[...]
    columns = [jnp.broadcast_to(mixing[:, g : g + 1], (8, 128)) for g in range(8)]
    heat = jnp.zeros((8, 128), F32)
    first = iota((8, 128), 0) == 0
    for q in range(48):
        code = place_ref[q]
        rank = lax.bitwise_and(code, 7)
        slon = lax.bitwise_and(lax.shift_right_logical(code, 3), 7)
        off = lax.shift_right_logical(code, 6)
        value = got_ref[q]
        wet = value < LAND_TEST
        drive = atm_ref[q] + band_mean - 2.0 * jnp.where(wet, value, 0.0)
        mixed = columns[0] * drive[0:1]
        for g in range(1, 8):
            mixed = mixed + columns[g] * drive[g : g + 1]
        coef = coef_ref[q : q + 1, :]
        flux = coef * mixed
        flux = flux + jnp.where(first, coef * sun_ref[q : q + 1, :], 0.0)
        rounded = flux.astype(BF16)
        out_ref[slon * SLOTS + off * PAIR + rank] = rounded
        heat = heat + jnp.where(wet, rounded.astype(F32), 0.0)
    subs = iota((8, 128), 0)
    row = jnp.broadcast_to(heat[0:1], (8, 128))
    one = row.astype(BF16).astype(F32)
    two = (row - one).astype(BF16).astype(F32)
    three = row - one - two
    parts = jnp.where(subs == 0, one, jnp.where(subs == 1, two, jnp.where(subs == 2, three, 0.0)))
    for s in range(8):
        out_ref[s * SLOTS + 18] = parts.astype(BF16)


def split_kernel(lats, back_ref, to_south_ref, to_north_ref, heat_ref):
    heat = jnp.zeros((8, 128), F32)
    for s in range(8):
        heat = heat + back_ref[s * SLOTS + 18].astype(F32)
        for k in range(PAIR):
            to_south_ref[s * PAIR + k] = back_ref[s * SLOTS + 12 + k]
            to_north_ref[s * PAIR + k] = back_ref[s * SLOTS + k]
    row = jnp.sum(heat, axis=0, keepdims=True)
    heat_ref[...] = jnp.broadcast_to(row[None], (lats, 1, 128))


def stencil_kernel(lats, land_ref, came_ref, low_ref, high_ref, tracer_ref, east_ref, north_ref,
                   kappa_ref, cross_ref, depth_ref, out_ref, rows_ref, diag_ref, bottom_ref):
    lat = lax.axis_index("lat")
    lon = lax.axis_index("lon")
    west = lax.rem(lon + 7, 8)
    east = lax.rem(lon + 1, 8)
    full = (16, 384)
    lanes = iota(full, 1)
    subs = iota(full, 0)
    at_west, at_east = lanes == 0, lanes == 383
    at_south, at_north = subs == 0, subs == 15
    small = iota((8, 384), 1)
    lane8, sub8 = iota((8, 128), 1), iota((8, 128), 0)

    def columns_of(side):
        return jnp.concatenate(
            [came_ref[side * SLOTS + 18].astype(F32), came_ref[side * SLOTS + 19].astype(F32)], axis=0
        )

    def from_west(v, column):
        return jnp.where(at_west, column, pltpu.roll(v, 1, 1))

    def from_east(v, column):
        return jnp.where(at_east, column, pltpu.roll(v, 383, 1))

    def from_south(v, row):
        return jnp.where(at_south, row, pltpu.roll(v, 1, 0))

    def from_north(v, row):
        return jnp.where(at_north, row, pltpu.roll(v, 15, 0))

    col_west, col_east = columns_of(west), columns_of(east)
    for side, ref in enumerate((low_ref, high_ref)):
        inside = jnp.where(lat == (0, lats - 1)[side], 0.0, 1.0)
        for k in range(7):
            for j in range(3):
                tile = ref[48 + 3 * k + j].astype(F32)
                if k == 6:
                    tile = jnp.where(sub8 == 0, tile * inside, tile)
                rows_ref[side, 8 * k : 8 * k + 8, 128 * j : 128 * j + 128] = tile
    for j in range(3):
        cols = slice(128 * j, 128 * j + 128)
        bottom_ref[0, :, cols] = depth_ref[:, cols].astype(F32) * tile_column(land_ref, j)
    bottom = bottom_ref[0]
    bottom_ref[1] = from_east(bottom, col_east[:, 48:49])
    bottom_ref[2] = from_west(bottom, col_west[:, 48:49])
    bottom_ref[3] = from_north(bottom, rows_ref[1, 48:49, :])
    bottom_ref[4] = from_south(bottom, rows_ref[0, 48:49, :])

    level8 = iota((8, 384), 0).astype(F32)
    for side in range(2):
        inside = jnp.where(lat == (0, lats - 1)[side], 0.0, 1.0)
        corner_w = jnp.broadcast_to(rows_ref[side, 49:50, 0:128], (8, 128))
        corner_e = jnp.broadcast_to(rows_ref[side, 49:50, 256:384], (8, 128))
        edge = jnp.broadcast_to(rows_ref[side, 48:49, :], (8, 384))
        edge_e = jnp.where(small == 383, corner_e[:, 48:49] * inside, pltpu.roll(edge, 383, 1))
        edge_w = jnp.where(small == 0, corner_w[:, 48:49] * inside, pltpu.roll(edge, 1, 1))
        for k in range(4):
            value = rows_ref[side, 8 * k : 8 * k + 8, :]
            pick = lane8 == sub8 + 8 * k
            value_e = jnp.sum(jnp.where(pick, corner_e, 0.0), axis=1, keepdims=True)
            value_w = jnp.sum(jnp.where(pick, corner_w, 0.0), axis=1, keepdims=True)
            value_e = jnp.where(small == 383, value_e, pltpu.roll(value, 383, 1))
            value_w = jnp.where(small == 0, value_w, pltpu.roll(value, 1, 1))
            diag_ref[side, 8 * k : 8 * k + 8, :] = jnp.where(level8 < edge_e, value_e, 0.0) - jnp.where(
                level8 < edge_w, value_w, 0.0
            )

    def level_step(l, carry):
        lf = l.astype(F32)
        cw = pltpu.roll(col_west, lax.rem(128 - l, 128), 1)
        ce = pltpu.roll(col_east, lax.rem(128 - l, 128), 1)
        masks = [(lf < bottom_ref[i]).astype(F32) for i in range(5)]
        mask, mask_e, mask_w, mask_n, mask_s = masks
        kappa = kappa_ref[l]
        velocity = east_ref[l]
        kap = 0.5 * (kappa + from_east(kappa, ce[:, 40:41]))
        open_face = mask * mask_e
        out_e = open_face * (jnp.maximum(velocity, 0.0) + kap)
        in_e = open_face * (kap - jnp.minimum(velocity, 0.0))
        velocity = from_west(velocity, cw[:, 32:33])
        kap = 0.5 * (kappa + from_west(kappa, cw[:, 40:41]))
        open_face = mask * mask_w
        in_w = open_face * (jnp.maximum(velocity, 0.0) + kap)
        out_w = open_face * (kap - jnp.minimum(velocity, 0.0))
        velocity = north_ref[l]
        kap = 0.5 * (kappa + from_north(kappa, rows_ref[1, pl.ds(40 + l, 1), :]))
        open_face = mask * mask_n
        out_n = open_face * (jnp.maximum(velocity, 0.0) + kap)
        in_n = open_face * (kap - jnp.minimum(velocity, 0.0))
        velocity = from_south(velocity, rows_ref[0, pl.ds(32 + l, 1), :])
        kap = 0.5 * (kappa + from_south(kappa, rows_ref[0, pl.ds(40 + l, 1), :]))
        open_face = mask * mask_s
        in_s = open_face * (jnp.maximum(velocity, 0.0) + kap)
        out_s = open_face * (kap - jnp.minimum(velocity, 0.0))
        keep = 1.0 - (out_e + out_w + out_n + out_s)
        cross = cross_ref[l] * mask
        for t in range(4):
            i = 8 * t + l
            c = tracer_ref[i]
            c_e = from_east(c, ce[:, 8 * t : 8 * t + 1])
            c_w = from_west(c, cw[:, 8 * t : 8 * t + 1])
            c_n = from_north(c, rows_ref[1, pl.ds(i, 1), :])
            c_s = from_south(c, rows_ref[0, pl.ds(i, 1), :])
            diag = mask_e * c_e - mask_w * c_w
            diag_n = from_north(diag, diag_ref[1, pl.ds(i, 1), :])
            diag_s = from_south(diag, diag_ref[0, pl.ds(i, 1), :])
            out_ref[i] = (
                keep * c + in_e * c_e + in_w * c_w + in_n * c_n + in_s * c_s + cross * (diag_n - diag_s)
            )
        return carry

    lax.fori_loop(0, 8, level_step, 0)


def finish_kernel(points, code_ref, land_ref, back_ref, from_north_ref, from_south_ref, heat_ref, depth_ref,
                  step_ref, flux_ref, out_ref, wide_ref):
    for t in range(48):
        code = code_ref[t]
        rank = lax.bitwise_and(code, 7)
        dlon = lax.bitwise_and(lax.shift_right_logical(code, 3), 7)
        off = lax.shift_right_logical(code, 6)
        at = dlon * PAIR + rank
        own = back_ref[dlon * SLOTS + PAIR + rank].astype(F32)
        north = from_north_ref[at].astype(F32)
        south = from_south_ref[at].astype(F32)
        value = jnp.where(off == 1, own, jnp.where(off == 2, north, south))
        value = jnp.where(land_ref[t] > 0, value, 0.0)
        flux_ref[t] = value.astype(BF16)
        wide_ref[8 * t : 8 * t + 8, :] = value
    heat = jnp.sum(jnp.sum(heat_ref[...], axis=0), axis=1, keepdims=True)
    correction = heat / points
    for j in range(3):
        cols = slice(128 * j, 128 * j + 128)
        wet = depth_ref[:, cols].astype(F32) * tile_column(land_ref, j)
        gain = jnp.where(wet > 0.0, 0.5, 0.0)
        for t in range(4):
            force = wide_ref[pl.ds(8 * j + t, 16, stride=24), :]
            if t == 0:
                force = force - correction
            out_ref[t, 0, :, cols] = step_ref[t, 0, :, cols] + gain * force


def call(kernel, name, in_specs, out_shape, out_specs, scratch=(), **more):
    return pl.pallas_call(
        kernel,
        out_shape=out_shape,
        in_specs=in_specs,
        out_specs=out_specs,
        scratch_shapes=list(scratch),
        name=name,
        **more,
    )


def shape(dims, dtype):
    return jax.ShapeDtypeStruct(dims, dtype)


def shards(
    tracers,
    east_velocity,
    north_velocity,
    diffusivity,
    cross_diffusivity,
    depth_levels,
    land_mask,
    ocean_state,
    atm_state,
    exchange_coef,
    sunlight,
    mixing,
    o2a_dest,
    o2a_slot,
    a2o_source,
    a2o_tile,
):
    lats = lax.axis_size("lat")
    lons = lax.axis_size("lon")
    lat = lax.axis_index("lat")
    north_pairs = [(i, (i + 1) % lats) for i in range(lats)]
    south_pairs = [(j, i) for i, j in north_pairs]
    flat = (8 * SLOTS, 8, 128)

    def turn(values):
        values = values.reshape(8, SLOTS, 8, 128)
        return lax.all_to_all(values, "lon", 0, 0, tiled=True).reshape(flat)

    tracers_l = tracers.reshape(32, 16, 384)

    outgoing, code = call(
        functools.partial(pack_kernel, lats),
        "pack",
        [SMEM, SMEM, VMEM, VMEM, VMEM, VMEM, VMEM],
        (shape(flat, BF16), shape((48,), jnp.int32)),
        (VMEM, SMEM),
        [pltpu.SMEM((24,), jnp.int32)],
    )(o2a_dest, land_mask, ocean_state, tracers_l, east_velocity, diffusivity, depth_levels)

    source_off = (lat - a2o_source // lons + 1) % lats
    same = a2o_source[:, None] == a2o_source[None, :]
    earlier = a2o_tile[None, :] < a2o_tile[:, None]
    source_rank = jnp.sum((same & earlier).astype(jnp.int32), axis=1)
    place = source_off * 64 + (a2o_source % lons) * 8 + source_rank

    came = turn(outgoing)
    row_shape = shape((69, 8, 128), BF16)
    up, down = call(
        rows_kernel,
        "rows",
        [SMEM, VMEM, VMEM, VMEM, VMEM, VMEM],
        (row_shape, row_shape),
        (VMEM, VMEM),
    )(
        land_mask,
        came,
        tracers_l,
        north_velocity,
        diffusivity,
        depth_levels,
    )
    low = lax.ppermute(up, "lat", north_pairs)
    high = lax.ppermute(down, "lat", south_pairs)

    backward = call(
        couple_kernel,
        "couple",
        [SMEM] + [VMEM] * 7,
        shape(flat, BF16),
        VMEM,
        [pltpu.VMEM((48, 8, 128), F32)],
    )(place, came, low, high, atm_state, exchange_coef, sunlight, mixing)
    back = turn(backward)

    step = call(
        functools.partial(stencil_kernel, lats),
        "stencil",
        [SMEM] + [VMEM] * 9,
        shape((32, 16, 384), F32),
        VMEM,
        [pltpu.VMEM((2, 56, 384), F32), pltpu.VMEM((2, 32, 384), F32), pltpu.VMEM((5, 16, 384), F32)],
        cost_estimate=pl.CostEstimate(flops=8000000, bytes_accessed=3000000, transcendentals=0),
    )(
        land_mask,
        came,
        low,
        high,
        tracers_l,
        east_velocity,
        north_velocity,
        diffusivity,
        cross_diffusivity,
        depth_levels,
    )

    to_south, to_north, heat = call(
        functools.partial(split_kernel, lats),
        "split",
        [VMEM],
        (shape((48, 8, 128), BF16), shape((48, 8, 128), BF16), shape((lats, 1, 128), F32)),
        (VMEM, VMEM, VMEM),
    )(back)
    heat = lax.all_to_all(heat, "lat", 0, 0, tiled=True)
    back_north = lax.ppermute(to_south, "lat", south_pairs)
    back_south = lax.ppermute(to_north, "lat", north_pairs)

    points = float(48 * 128 * lats * lons)
    top = pl.BlockSpec((4, 1, 16, 384), lambda i: (0, 0, 0, 0))
    ocean_flux, new_tracers = call(
        functools.partial(finish_kernel, points),
        "finish",
        [SMEM, SMEM, VMEM, VMEM, VMEM, VMEM, VMEM, top],
        (shape((48, 8, 128), BF16), shape((4, 8, 16, 384), F32)),
        (VMEM, top),
        [pltpu.VMEM((384, 128), F32)],
        grid=(1,),
        input_output_aliases={7: 1},
    )(code, land_mask, back, back_north, back_south, heat, depth_levels, step.reshape(4, 8, 16, 384))
    return (new_tracers, ocean_flux)


def solution(mesh):
    return jax.shard_map(
        shards,
        mesh=mesh,
        in_specs=(
            P(None, None, "lat", "lon"),
            P(None, "lat", "lon"),
            P(None, "lat", "lon"),
            P(None, "lat", "lon"),
            P(None, "lat", "lon"),
            P("lat", "lon"),
            P(("lat", "lon")),
            P(("lat", "lon"), None, None),
            P(("lat", "lon"), None, None),
            P(("lat", "lon"), None),
            P(("lat", "lon"), None),
            P(),
            P(("lat", "lon")),
            P(("lat", "lon")),
            P(("lat", "lon")),
            P(("lat", "lon")),
        ),
        out_specs=(P(None, None, "lat", "lon"), P(("lat", "lon"), None, None)),
        check_vma=False,
    )
```

```python
import functools

import jax
import jax.numpy as jnp
from jax import lax
from jax.experimental import pallas as pl
from jax.experimental.pallas import tpu as pltpu
from jax.sharding import PartitionSpec as P

F32 = jnp.float32
BF16 = jnp.bfloat16
PAIR = 6
SLOTS = 20
LAND = 2.0**100
LAND_TEST = 2.0**90
VMEM = pl.BlockSpec(memory_space=pltpu.VMEM)
SMEM = pl.BlockSpec(memory_space=pltpu.SMEM)
ANY = pl.BlockSpec(memory_space=pl.ANY)
SMALL = 16 * 1024 * 1024


def iota(shape, dim):
    return lax.broadcasted_iota(jnp.int32, shape, dim)


def block_of(ref, block):
    return ref[..., 128 * block : 128 * block + 128]


def tile_column(land_ref, block):
    rows = iota((16, 128), 0)
    out = jnp.zeros((16, 128), F32)
    for r in range(16):
        out = jnp.where(rows == r, land_ref[3 * r + block].astype(F32), out)
    return out


def pack_kernel(lats, dest_ref, land_ref, state_ref, tracer_ref, east_ref, kappa_ref, depth_ref,
                out_ref, code_ref, count_ref):
    lat = lax.axis_index("lat")
    lon = lax.axis_index("lon")
    lons = 8
    for i in range(24):
        count_ref[i] = 0
    for t in range(48):
        dest = dest_ref[t]
        off = lax.shift_right_logical(dest, 3) - lat + 1
        off = jnp.where(off < 0, off + lats, jnp.where(off >= lats, off - lats, off))
        dlon = lax.bitwise_and(dest, 7)
        key = off * 8 + dlon
        rank = count_ref[key]
        count_ref[key] = rank + 1
        code_ref[t] = key * 8 + rank
        value = state_ref[t].astype(F32)
        value = jnp.where(land_ref[t] > 0, value, LAND)
        out_ref[dlon * SLOTS + off * PAIR + rank] = value.astype(BF16)
    lanes = iota((16, 128), 1)
    for block, lane, shift in ((2, 127, 1), (0, 0, lons - 1)):
        packed = jnp.zeros((16, 128), F32)
        for i in range(32):
            packed = jnp.where(lanes == i, block_of(tracer_ref, block)[i][:, lane : lane + 1], packed)
        for i in range(8):
            if block == 2:
                packed = jnp.where(lanes == 32 + i, block_of(east_ref, block)[i][:, lane : lane + 1], packed)
            packed = jnp.where(lanes == 40 + i, block_of(kappa_ref, block)[i][:, lane : lane + 1], packed)
        bottom = block_of(depth_ref, block)[...].astype(F32) * tile_column(land_ref, block)
        packed = jnp.where(lanes == 48, bottom[:, lane : lane + 1], packed)
        target = lax.rem(lon + shift, lons)
        out_ref[target * SLOTS + 18] = packed[:8].astype(BF16)
        out_ref[target * SLOTS + 19] = packed[8:].astype(BF16)


def rows_kernel(land_ref, came_ref, tracer_ref, north_ref, kappa_ref, depth_ref, up_ref, down_ref):
    lon = lax.axis_index("lon")
    west = lax.rem(lon + 7, 8)
    east = lax.rem(lon + 1, 8)
    subs = iota((8, 128), 0)
    for out_ref, first, row in ((up_ref, 12, 15), (down_ref, 0, 0)):
        for s in range(8):
            for k in range(PAIR):
                out_ref[s * PAIR + k] = came_ref[s * SLOTS + first + k]
        half, sub = (19, 7) if row else (18, 0)
        corners = (
            came_ref[west * SLOTS + half].astype(F32)[sub : sub + 1],
            None,
            came_ref[east * SLOTS + half].astype(F32)[sub : sub + 1],
        )
        for j in range(3):
            cols = slice(128 * j, 128 * j + 128)
            for k in range(4):
                out_ref[48 + 3 * k + j] = tracer_ref[8 * k : 8 * k + 8, row, cols].astype(BF16)
            if row:
                out_ref[48 + 12 + j] = north_ref[:, row, cols].astype(BF16)
            else:
                out_ref[48 + 12 + j] = jnp.zeros((8, 128), BF16)
            out_ref[48 + 15 + j] = kappa_ref[:, row, cols].astype(BF16)
            bottom = depth_ref[row : row + 1, cols].astype(F32) * land_ref[3 * row + j].astype(F32)
            last = jnp.where(subs == 0, bottom, 0.0)
            if j != 1:
                last = jnp.where(subs == 1, corners[j], last)
            out_ref[48 + 18 + j] = last.astype(BF16)


def couple_kernel(place_ref, came_ref, low_ref, high_ref, atm_ref, coef_ref, sun_ref, mixing_ref,
                  out_ref, got_ref):
    total = jnp.zeros((8, 128), F32)
    for q in range(48):
        code = place_ref[q]
        rank = lax.bitwise_and(code, 7)
        slon = lax.bitwise_and(lax.shift_right_logical(code, 3), 7)
        off = lax.shift_right_logical(code, 6)
        at = slon * PAIR + rank
        own = came_ref[slon * SLOTS + PAIR + rank].astype(F32)
        low = low_ref[at].astype(F32)
        high = high_ref[at].astype(F32)
        value = jnp.where(off == 1, own, jnp.where(off == 2, low, high))
        got_ref[q] = value
        total = total + coef_ref[q : q + 1, :] * jnp.where(value < LAND_TEST, value, 0.0)
    weight = jnp.sum(jnp.sum(coef_ref[...], axis=0, keepdims=True), axis=1, keepdims=True)
    band_mean = jnp.sum(total, axis=1, keepdims=True) / weight
    mixing = mixing_ref[...]
    columns = [jnp.broadcast_to(mixing[:, g : g + 1], (8, 128)) for g in range(8)]
    heat = jnp.zeros((8, 128), F32)
    first = iota((8, 128), 0) == 0
    for q in range(48):
        code = place_ref[q]
        rank = lax.bitwise_and(code, 7)
        slon = lax.bitwise_and(lax.shift_right_logical(code, 3), 7)
        off = lax.shift_right_logical(code, 6)
        value = got_ref[q]
        wet = value < LAND_TEST
        drive = atm_ref[q] + band_mean - 2.0 * jnp.where(wet, value, 0.0)
        mixed = columns[0] * drive[0:1]
        for g in range(1, 8):
            mixed = mixed + columns[g] * drive[g : g + 1]
        coef = coef_ref[q : q + 1, :]
        flux = coef * mixed
        flux = flux + jnp.where(first, coef * sun_ref[q : q + 1, :], 0.0)
        rounded = flux.astype(BF16)
        out_ref[slon * SLOTS + off * PAIR + rank] = rounded
        heat = heat + jnp.where(wet, rounded.astype(F32), 0.0)
    subs = iota((8, 128), 0)
    row = jnp.broadcast_to(heat[0:1], (8, 128))
    one = row.astype(BF16).astype(F32)
    two = (row - one).astype(BF16).astype(F32)
    three = row - one - two
    parts = jnp.where(subs == 0, one, jnp.where(subs == 1, two, jnp.where(subs == 2, three, 0.0)))
    for s in range(8):
        out_ref[s * SLOTS + 18] = parts.astype(BF16)


def split_kernel(lats, back_ref, done_ref, to_south_ref, to_north_ref, heat_ref):
    heat = jnp.zeros((8, 128), F32)
    for s in range(8):
        heat = heat + back_ref[s * SLOTS + 18].astype(F32)
        for k in range(PAIR):
            to_south_ref[s * PAIR + k] = back_ref[s * SLOTS + 12 + k]
            to_north_ref[s * PAIR + k] = back_ref[s * SLOTS + k]
    row = jnp.sum(heat, axis=0, keepdims=True)
    heat_ref[...] = jnp.broadcast_to(row[None], (lats, 1, 128))


def stencil_kernel(lats, land_ref, came_ref, low_ref, high_ref, tracer_ref, east_ref, north_ref,
                   kappa_ref, cross_ref, depth_ref, after_ref, out_ref, done_ref, rows_ref, diag_ref, bottom_ref):
    lat = lax.axis_index("lat")
    lon = lax.axis_index("lon")
    west = lax.rem(lon + 7, 8)
    east = lax.rem(lon + 1, 8)
    full = (16, 384)
    lanes = iota(full, 1)
    subs = iota(full, 0)
    at_west, at_east = lanes == 0, lanes == 383
    at_south, at_north = subs == 0, subs == 15
    small = iota((8, 384), 1)
    lane8, sub8 = iota((8, 128), 1), iota((8, 128), 0)

    def columns_of(side):
        return jnp.concatenate(
            [came_ref[side * SLOTS + 18].astype(F32), came_ref[side * SLOTS + 19].astype(F32)], axis=0
        )

    def from_west(v, column):
        return jnp.where(at_west, column, pltpu.roll(v, 1, 1))

    def from_east(v, column):
        return jnp.where(at_east, column, pltpu.roll(v, 383, 1))

    def from_south(v, row):
        return jnp.where(at_south, row, pltpu.roll(v, 1, 0))

    def from_north(v, row):
        return jnp.where(at_north, row, pltpu.roll(v, 15, 0))

    col_west, col_east = columns_of(west), columns_of(east)
    for side, ref in enumerate((low_ref, high_ref)):
        inside = jnp.where(lat == (0, lats - 1)[side], 0.0, 1.0)
        for k in range(7):
            for j in range(3):
                tile = ref[48 + 3 * k + j].astype(F32)
                if k == 6:
                    tile = jnp.where(sub8 == 0, tile * inside, tile)
                rows_ref[side, 8 * k : 8 * k + 8, 128 * j : 128 * j + 128] = tile
    for j in range(3):
        cols = slice(128 * j, 128 * j + 128)
        bottom_ref[0, :, cols] = depth_ref[:, cols].astype(F32) * tile_column(land_ref, j)
    bottom = bottom_ref[0]
    bottom_ref[1] = from_east(bottom, col_east[:, 48:49])
    bottom_ref[2] = from_west(bottom, col_west[:, 48:49])
    bottom_ref[3] = from_north(bottom, rows_ref[1, 48:49, :])
    bottom_ref[4] = from_south(bottom, rows_ref[0, 48:49, :])

    level8 = iota((8, 384), 0).astype(F32)
    for side in range(2):
        inside = jnp.where(lat == (0, lats - 1)[side], 0.0, 1.0)
        corner_w = jnp.broadcast_to(rows_ref[side, 49:50, 0:128], (8, 128))
        corner_e = jnp.broadcast_to(rows_ref[side, 49:50, 256:384], (8, 128))
        edge = jnp.broadcast_to(rows_ref[side, 48:49, :], (8, 384))
        edge_e = jnp.where(small == 383, corner_e[:, 48:49] * inside, pltpu.roll(edge, 383, 1))
        edge_w = jnp.where(small == 0, corner_w[:, 48:49] * inside, pltpu.roll(edge, 1, 1))
        for k in range(4):
            value = rows_ref[side, 8 * k : 8 * k + 8, :]
            pick = lane8 == sub8 + 8 * k
            value_e = jnp.sum(jnp.where(pick, corner_e, 0.0), axis=1, keepdims=True)
            value_w = jnp.sum(jnp.where(pick, corner_w, 0.0), axis=1, keepdims=True)
            value_e = jnp.where(small == 383, value_e, pltpu.roll(value, 383, 1))
            value_w = jnp.where(small == 0, value_w, pltpu.roll(value, 1, 1))
            diag_ref[side, 8 * k : 8 * k + 8, :] = jnp.where(level8 < edge_e, value_e, 0.0) - jnp.where(
                level8 < edge_w, value_w, 0.0
            )

    def level_step(l, carry):
        lf = l.astype(F32)
        cw = pltpu.roll(col_west, lax.rem(128 - l, 128), 1)
        ce = pltpu.roll(col_east, lax.rem(128 - l, 128), 1)
        masks = [(lf < bottom_ref[i]).astype(F32) for i in range(5)]
        mask, mask_e, mask_w, mask_n, mask_s = masks
        kappa = kappa_ref[l]
        velocity = east_ref[l]
        kap = 0.5 * (kappa + from_east(kappa, ce[:, 40:41]))
        open_face = mask * mask_e
        out_e = open_face * (jnp.maximum(velocity, 0.0) + kap)
        in_e = open_face * (kap - jnp.minimum(velocity, 0.0))
        velocity = from_west(velocity, cw[:, 32:33])
        kap = 0.5 * (kappa + from_west(kappa, cw[:, 40:41]))
        open_face = mask * mask_w
        in_w = open_face * (jnp.maximum(velocity, 0.0) + kap)
        out_w = open_face * (kap - jnp.minimum(velocity, 0.0))
        velocity = north_ref[l]
        kap = 0.5 * (kappa + from_north(kappa, rows_ref[1, pl.ds(40 + l, 1), :]))
        open_face = mask * mask_n
        out_n = open_face * (jnp.maximum(velocity, 0.0) + kap)
        in_n = open_face * (kap - jnp.minimum(velocity, 0.0))
        velocity = from_south(velocity, rows_ref[0, pl.ds(32 + l, 1), :])
        kap = 0.5 * (kappa + from_south(kappa, rows_ref[0, pl.ds(40 + l, 1), :]))
        open_face = mask * mask_s
        in_s = open_face * (jnp.maximum(velocity, 0.0) + kap)
        out_s = open_face * (kap - jnp.minimum(velocity, 0.0))
        keep = 1.0 - (out_e + out_w + out_n + out_s)
        cross = cross_ref[l] * mask
        for t in range(4):
            i = 8 * t + l
            c = tracer_ref[i]
            c_e = from_east(c, ce[:, 8 * t : 8 * t + 1])
            c_w = from_west(c, cw[:, 8 * t : 8 * t + 1])
            c_n = from_north(c, rows_ref[1, pl.ds(i, 1), :])
            c_s = from_south(c, rows_ref[0, pl.ds(i, 1), :])
            diag = mask_e * c_e - mask_w * c_w
            diag_n = from_north(diag, diag_ref[1, pl.ds(i, 1), :])
            diag_s = from_south(diag, diag_ref[0, pl.ds(i, 1), :])
            out_ref[i] = (
                keep * c + in_e * c_e + in_w * c_w + in_n * c_n + in_s * c_s + cross * (diag_n - diag_s)
            )
        return carry

    lax.fori_loop(0, 8, level_step, 0)
    done_ref[...] = jnp.zeros((8, 128), F32)


def finish_kernel(points, code_ref, land_ref, back_ref, from_north_ref, from_south_ref, heat_ref, depth_ref,
                  step_ref, flux_ref, out_ref, wide_ref):
    for t in range(48):
        code = code_ref[t]
        rank = lax.bitwise_and(code, 7)
        dlon = lax.bitwise_and(lax.shift_right_logical(code, 3), 7)
        off = lax.shift_right_logical(code, 6)
        at = dlon * PAIR + rank
        own = back_ref[dlon * SLOTS + PAIR + rank].astype(F32)
        north = from_north_ref[at].astype(F32)
        south = from_south_ref[at].astype(F32)
        value = jnp.where(off == 1, own, jnp.where(off == 2, north, south))
        value = jnp.where(land_ref[t] > 0, value, 0.0)
        flux_ref[t] = value.astype(BF16)
        wide_ref[8 * t : 8 * t + 8, :] = value
    heat = jnp.sum(jnp.sum(heat_ref[...], axis=0), axis=1, keepdims=True)
    correction = heat / points
    for j in range(3):
        cols = slice(128 * j, 128 * j + 128)
        wet = depth_ref[:, cols].astype(F32) * tile_column(land_ref, j)
        gain = jnp.where(wet > 0.0, 0.5, 0.0)
        for t in range(4):
            force = wide_ref[pl.ds(8 * j + t, 16, stride=24), :]
            if t == 0:
                force = force - correction
            out_ref[t, 0, :, cols] = step_ref[t, 0, :, cols] + gain * force


def call(kernel, name, in_specs, out_shape, out_specs, scratch=(), limit=SMALL, **more):
    return pl.pallas_call(
        kernel,
        out_shape=out_shape,
        in_specs=in_specs,
        out_specs=out_specs,
        scratch_shapes=list(scratch),
        name=name,
        compiler_params=pltpu.CompilerParams(vmem_limit_bytes=limit),
        **more,
    )


def shape(dims, dtype):
    return jax.ShapeDtypeStruct(dims, dtype)


def shards(
    tracers,
    east_velocity,
    north_velocity,
    diffusivity,
    cross_diffusivity,
    depth_levels,
    land_mask,
    ocean_state,
    atm_state,
    exchange_coef,
    sunlight,
    mixing,
    o2a_dest,
    o2a_slot,
    a2o_source,
    a2o_tile,
):
    lats = lax.axis_size("lat")
    lons = lax.axis_size("lon")
    lat = lax.axis_index("lat")
    north_pairs = [(i, (i + 1) % lats) for i in range(lats)]
    south_pairs = [(j, i) for i, j in north_pairs]
    flat = (8 * SLOTS, 8, 128)

    def turn(values):
        values = values.reshape(8, SLOTS, 8, 128)
        return lax.all_to_all(values, "lon", 0, 0, tiled=True).reshape(flat)

    tracers_l = tracers.reshape(32, 16, 384)

    outgoing, code = call(
        functools.partial(pack_kernel, lats),
        "pack",
        [SMEM, SMEM, VMEM, VMEM, VMEM, VMEM, VMEM],
        (shape(flat, BF16), shape((48,), jnp.int32)),
        (VMEM, SMEM),
        [pltpu.SMEM((24,), jnp.int32)],
        limit=60 * 1024 * 1024,
    )(o2a_dest, land_mask, ocean_state, tracers_l, east_velocity, diffusivity, depth_levels)

    source_off = (lat - a2o_source // lons + 1) % lats
    same = a2o_source[:, None] == a2o_source[None, :]
    earlier = a2o_tile[None, :] < a2o_tile[:, None]
    source_rank = jnp.sum((same & earlier).astype(jnp.int32), axis=1)
    place = source_off * 64 + (a2o_source % lons) * 8 + source_rank

    came = turn(outgoing)
    row_shape = shape((69, 8, 128), BF16)
    up, down = call(
        rows_kernel,
        "rows",
        [SMEM, VMEM, VMEM, VMEM, VMEM, VMEM],
        (row_shape, row_shape),
        (VMEM, VMEM),
    )(
        land_mask,
        came,
        tracers_l,
        north_velocity,
        diffusivity,
        depth_levels,
    )
    low = lax.ppermute(up, "lat", north_pairs)
    high = lax.ppermute(down, "lat", south_pairs)

    backward = call(
        couple_kernel,
        "couple",
        [SMEM] + [VMEM] * 7,
        shape(flat, BF16),
        VMEM,
        [pltpu.VMEM((48, 8, 128), F32)],
    )(place, came, low, high, atm_state, exchange_coef, sunlight, mixing)
    back = turn(backward)

    step, done = call(
        functools.partial(stencil_kernel, lats),
        "stencil",
        [SMEM] + [VMEM] * 9 + [ANY],
        (shape((32, 16, 384), F32), shape((8, 128), F32)),
        (VMEM, VMEM),
        [pltpu.VMEM((2, 56, 384), F32), pltpu.VMEM((2, 32, 384), F32), pltpu.VMEM((5, 16, 384), F32)],
        cost_estimate=pl.CostEstimate(flops=8000000, bytes_accessed=3000000, transcendentals=0),
    )(
        land_mask,
        came,
        low,
        high,
        tracers_l,
        east_velocity,
        north_velocity,
        diffusivity,
        cross_diffusivity,
        depth_levels,
        backward,
    )

    to_south, to_north, heat = call(
        functools.partial(split_kernel, lats),
        "split",
        [VMEM, ANY],
        (shape((48, 8, 128), BF16), shape((48, 8, 128), BF16), shape((lats, 1, 128), F32)),
        (VMEM, VMEM, VMEM),
    )(back, done)
    heat = lax.all_to_all(heat, "lat", 0, 0, tiled=True)
    back_north = lax.ppermute(to_south, "lat", south_pairs)
    back_south = lax.ppermute(to_north, "lat", north_pairs)

    points = float(48 * 128 * lats * lons)
    top = pl.BlockSpec((4, 1, 16, 384), lambda i: (0, 0, 0, 0))
    ocean_flux, new_tracers = call(
        functools.partial(finish_kernel, points),
        "finish",
        [SMEM, SMEM, VMEM, VMEM, VMEM, VMEM, VMEM, top],
        (shape((48, 8, 128), BF16), shape((4, 8, 16, 384), F32)),
        (VMEM, top),
        [pltpu.VMEM((384, 128), F32)],
        grid=(1,),
        input_output_aliases={7: 1},
    )(code, land_mask, back, back_north, back_south, heat, depth_levels, step.reshape(4, 8, 16, 384))
    return (new_tracers, ocean_flux)


def solution(mesh):
    return jax.shard_map(
        shards,
        mesh=mesh,
        in_specs=(
            P(None, None, "lat", "lon"),
            P(None, "lat", "lon"),
            P(None, "lat", "lon"),
            P(None, "lat", "lon"),
            P(None, "lat", "lon"),
            P("lat", "lon"),
            P(("lat", "lon")),
            P(("lat", "lon"), None, None),
            P(("lat", "lon"), None, None),
            P(("lat", "lon"), None),
            P(("lat", "lon"), None),
            P(),
            P(("lat", "lon")),
            P(("lat", "lon")),
            P(("lat", "lon")),
            P(("lat", "lon")),
        ),
        out_specs=(P(None, None, "lat", "lon"), P(("lat", "lon"), None, None)),
        check_vma=False,
    )
```

```python
import functools

import jax
import jax.numpy as jnp
from jax import lax
from jax.experimental import pallas as pl
from jax.experimental.pallas import tpu as pltpu
from jax.sharding import PartitionSpec as P

F32 = jnp.float32
BF16 = jnp.bfloat16
PAIR = 6
SLOTS = 20
LAND = 2.0**100
LAND_TEST = 2.0**90
VMEM = pl.BlockSpec(memory_space=pltpu.VMEM)
SMEM = pl.BlockSpec(memory_space=pltpu.SMEM)
ANY = pl.BlockSpec(memory_space=pl.ANY)
HBM = pl.BlockSpec(memory_space=pltpu.HBM)
SMALL = 16 * 1024 * 1024


def iota(shape, dim):
    return lax.broadcasted_iota(jnp.int32, shape, dim)


def block_of(ref, block):
    return ref[..., 128 * block : 128 * block + 128]


def tile_column(land_ref, block):
    rows = iota((16, 128), 0)
    out = jnp.zeros((16, 128), F32)
    for r in range(16):
        out = jnp.where(rows == r, land_ref[3 * r + block].astype(F32), out)
    return out


def pack_kernel(lats, dest_hbm, land_hbm, state_hbm, tracer_hbm, east_hbm, kappa_hbm, depth_hbm,
                out_ref, code_ref, count_ref, dest_ref, land_ref, state_ref, tracer_ref, east_ref,
                kappa_ref, depth_ref, sems):
    first, last = pl.ds(0, 128), pl.ds(256, 128)
    copies = [
        pltpu.make_async_copy(source, target, sems.at[n])
        for n, (source, target) in enumerate(
            (
                (dest_hbm, dest_ref),
                (land_hbm, land_ref),
                (state_hbm, state_ref),
                (depth_hbm, depth_ref),
                (tracer_hbm.at[:, :, last], tracer_ref.at[0]),
                (tracer_hbm.at[:, :, first], tracer_ref.at[1]),
                (kappa_hbm.at[:, :, last], kappa_ref.at[0]),
                (kappa_hbm.at[:, :, first], kappa_ref.at[1]),
                (east_hbm.at[:, :, last], east_ref),
            )
        )
    ]
    for copy in copies:
        copy.start()
    lat = lax.axis_index("lat")
    lon = lax.axis_index("lon")
    lons = 8
    for i in range(24):
        count_ref[i] = 0
    for copy in copies[:3]:
        copy.wait()
    for t in range(48):
        dest = dest_ref[t]
        off = lax.shift_right_logical(dest, 3) - lat + 1
        off = jnp.where(off < 0, off + lats, jnp.where(off >= lats, off - lats, off))
        dlon = lax.bitwise_and(dest, 7)
        key = off * 8 + dlon
        rank = count_ref[key]
        count_ref[key] = rank + 1
        code_ref[t] = key * 8 + rank
        value = state_ref[t].astype(F32)
        value = jnp.where(land_ref[t] > 0, value, LAND)
        out_ref[dlon * SLOTS + off * PAIR + rank] = value.astype(BF16)
    for copy in copies[3:]:
        copy.wait()
    lanes = iota((16, 128), 1)
    for side, block, lane, shift in ((0, 2, 127, 1), (1, 0, 0, lons - 1)):
        packed = jnp.zeros((16, 128), F32)
        for i in range(32):
            packed = jnp.where(lanes == i, tracer_ref[side, i][:, lane : lane + 1], packed)
        for i in range(8):
            if side == 0:
                packed = jnp.where(lanes == 32 + i, east_ref[i][:, lane : lane + 1], packed)
            packed = jnp.where(lanes == 40 + i, kappa_ref[side, i][:, lane : lane + 1], packed)
        bottom = block_of(depth_ref, block)[...].astype(F32) * tile_column(land_ref, block)
        packed = jnp.where(lanes == 48, bottom[:, lane : lane + 1], packed)
        target = lax.rem(lon + shift, lons)
        out_ref[target * SLOTS + 18] = packed[:8].astype(BF16)
        out_ref[target * SLOTS + 19] = packed[8:].astype(BF16)


def by_parity(body, cross, inner):
    odd = lax.rem(lax.axis_index("lat"), 2)

    @pl.when(odd == 1)
    def _():
        body(cross, inner)

    @pl.when(odd == 0)
    def _():
        body(inner, cross)


def rows_kernel(land_ref, came_ref, tracer_ref, north_ref, kappa_ref, depth_ref, cross_ref, inner_ref):
    inputs = (land_ref, came_ref, tracer_ref, north_ref, kappa_ref, depth_ref)
    by_parity(functools.partial(fill_rows, *inputs), cross_ref, inner_ref)


def fill_rows(land_ref, came_ref, tracer_ref, north_ref, kappa_ref, depth_ref, up_ref, down_ref):
    lon = lax.axis_index("lon")
    west = lax.rem(lon + 7, 8)
    east = lax.rem(lon + 1, 8)
    subs = iota((8, 128), 0)
    for out_ref, first, row in ((up_ref, 12, 15), (down_ref, 0, 0)):
        for s in range(8):
            for k in range(PAIR):
                out_ref[s * PAIR + k] = came_ref[s * SLOTS + first + k]
        half, sub = (19, 7) if row else (18, 0)
        corners = (
            came_ref[west * SLOTS + half].astype(F32)[sub : sub + 1],
            None,
            came_ref[east * SLOTS + half].astype(F32)[sub : sub + 1],
        )
        for j in range(3):
            cols = slice(128 * j, 128 * j + 128)
            for k in range(4):
                out_ref[48 + 3 * k + j] = tracer_ref[8 * k : 8 * k + 8, row, cols].astype(BF16)
            if row:
                out_ref[48 + 12 + j] = north_ref[:, row, cols].astype(BF16)
            else:
                out_ref[48 + 12 + j] = jnp.zeros((8, 128), BF16)
            out_ref[48 + 15 + j] = kappa_ref[:, row, cols].astype(BF16)
            bottom = depth_ref[row : row + 1, cols].astype(F32) * land_ref[3 * row + j].astype(F32)
            last = jnp.where(subs == 0, bottom, 0.0)
            if j != 1:
                last = jnp.where(subs == 1, corners[j], last)
            out_ref[48 + 18 + j] = last.astype(BF16)


def couple_kernel(place_ref, came_ref, cross_ref, inner_ref, atm_ref, coef_ref, sun_ref, mixing_ref,
                  out_ref, got_ref):
    odd = lax.rem(lax.axis_index("lat"), 2)
    cross_off = jnp.where(odd == 1, 0, 2)
    total = jnp.zeros((8, 128), F32)
    for q in range(48):
        code = place_ref[q]
        rank = lax.bitwise_and(code, 7)
        slon = lax.bitwise_and(lax.shift_right_logical(code, 3), 7)
        off = lax.shift_right_logical(code, 6)
        at = slon * PAIR + rank
        own = came_ref[slon * SLOTS + PAIR + rank].astype(F32)
        cross = cross_ref[at].astype(F32)
        inner = inner_ref[at].astype(F32)
        value = jnp.where(off == 1, own, jnp.where(off == cross_off, cross, inner))
        got_ref[q] = value
        total = total + coef_ref[q : q + 1, :] * jnp.where(value < LAND_TEST, value, 0.0)
    weight = jnp.sum(jnp.sum(coef_ref[...], axis=0, keepdims=True), axis=1, keepdims=True)
    band_mean = jnp.sum(total, axis=1, keepdims=True) / weight
    mixing = mixing_ref[...]
    columns = [jnp.broadcast_to(mixing[:, g : g + 1], (8, 128)) for g in range(8)]
    heat = jnp.zeros((8, 128), F32)
    first = iota((8, 128), 0) == 0
    for q in range(48):
        code = place_ref[q]
        rank = lax.bitwise_and(code, 7)
        slon = lax.bitwise_and(lax.shift_right_logical(code, 3), 7)
        off = lax.shift_right_logical(code, 6)
        value = got_ref[q]
        wet = value < LAND_TEST
        drive = atm_ref[q] + band_mean - 2.0 * jnp.where(wet, value, 0.0)
        mixed = columns[0] * drive[0:1]
        for g in range(1, 8):
            mixed = mixed + columns[g] * drive[g : g + 1]
        coef = coef_ref[q : q + 1, :]
        flux = coef * mixed
        flux = flux + jnp.where(first, coef * sun_ref[q : q + 1, :], 0.0)
        rounded = flux.astype(BF16)
        out_ref[slon * SLOTS + off * PAIR + rank] = rounded
        heat = heat + jnp.where(wet, rounded.astype(F32), 0.0)
    subs = iota((8, 128), 0)
    row = jnp.broadcast_to(heat[0:1], (8, 128))
    one = row.astype(BF16).astype(F32)
    two = (row - one).astype(BF16).astype(F32)
    three = row - one - two
    parts = jnp.where(subs == 0, one, jnp.where(subs == 1, two, jnp.where(subs == 2, three, 0.0)))
    for s in range(8):
        out_ref[s * SLOTS + 18] = parts.astype(BF16)


def split_kernel(lats, back_ref, done_ref, cross_ref, inner_ref, heat_ref):
    odd = lax.rem(lax.axis_index("lat"), 2)
    cross_at = jnp.where(odd == 1, 0, 12)
    inner_at = 12 - cross_at
    heat = jnp.zeros((8, 128), F32)
    for s in range(8):
        heat = heat + back_ref[s * SLOTS + 18].astype(F32)
        for k in range(PAIR):
            cross_ref[s * PAIR + k] = back_ref[s * SLOTS + cross_at + k]
            inner_ref[s * PAIR + k] = back_ref[s * SLOTS + inner_at + k]
    row = jnp.sum(heat, axis=0, keepdims=True)
    heat_ref[...] = jnp.broadcast_to(row[None], (lats, 1, 128))


def stencil_kernel(lats, land_ref, came_ref, cross_halo_ref, inner_halo_ref, tracer_ref, east_ref, north_ref,
                   kappa_ref, cross_ref, depth_ref, code_ref, after_ref, out_ref, top_ref, done_ref, rows_ref,
                   diag_ref, bottom_ref):
    lat = lax.axis_index("lat")
    lon = lax.axis_index("lon")
    west = lax.rem(lon + 7, 8)
    east = lax.rem(lon + 1, 8)
    full = (16, 384)
    lanes = iota(full, 1)
    subs = iota(full, 0)
    at_west, at_east = lanes == 0, lanes == 383
    at_south, at_north = subs == 0, subs == 15
    small = iota((8, 384), 1)
    lane8, sub8 = iota((8, 128), 1), iota((8, 128), 0)

    def columns_of(side):
        return jnp.concatenate(
            [came_ref[side * SLOTS + 18].astype(F32), came_ref[side * SLOTS + 19].astype(F32)], axis=0
        )

    def from_west(v, column):
        return jnp.where(at_west, column, pltpu.roll(v, 1, 1))

    def from_east(v, column):
        return jnp.where(at_east, column, pltpu.roll(v, 383, 1))

    def from_south(v, row):
        return jnp.where(at_south, row, pltpu.roll(v, 1, 0))

    def from_north(v, row):
        return jnp.where(at_north, row, pltpu.roll(v, 15, 0))

    col_west, col_east = columns_of(west), columns_of(east)

    def unpack_rows(high_ref, low_ref):
        for side, ref in enumerate((low_ref, high_ref)):
            inside = jnp.where(lat == (0, lats - 1)[side], 0.0, 1.0)
            for k in range(7):
                for j in range(3):
                    tile = ref[48 + 3 * k + j].astype(F32)
                    if k == 6:
                        tile = jnp.where(sub8 == 0, tile * inside, tile)
                    rows_ref[side, 8 * k : 8 * k + 8, 128 * j : 128 * j + 128] = tile

    by_parity(unpack_rows, cross_halo_ref, inner_halo_ref)
    for j in range(3):
        cols = slice(128 * j, 128 * j + 128)
        bottom_ref[0, :, cols] = depth_ref[:, cols].astype(F32) * tile_column(land_ref, j)
    bottom = bottom_ref[0]
    bottom_ref[1] = from_east(bottom, col_east[:, 48:49])
    bottom_ref[2] = from_west(bottom, col_west[:, 48:49])
    bottom_ref[3] = from_north(bottom, rows_ref[1, 48:49, :])
    bottom_ref[4] = from_south(bottom, rows_ref[0, 48:49, :])

    level8 = iota((8, 384), 0).astype(F32)
    for side in range(2):
        inside = jnp.where(lat == (0, lats - 1)[side], 0.0, 1.0)
        corner_w = jnp.broadcast_to(rows_ref[side, 49:50, 0:128], (8, 128))
        corner_e = jnp.broadcast_to(rows_ref[side, 49:50, 256:384], (8, 128))
        edge = jnp.broadcast_to(rows_ref[side, 48:49, :], (8, 384))
        edge_e = jnp.where(small == 383, corner_e[:, 48:49] * inside, pltpu.roll(edge, 383, 1))
        edge_w = jnp.where(small == 0, corner_w[:, 48:49] * inside, pltpu.roll(edge, 1, 1))
        for k in range(4):
            value = rows_ref[side, 8 * k : 8 * k + 8, :]
            pick = lane8 == sub8 + 8 * k
            value_e = jnp.sum(jnp.where(pick, corner_e, 0.0), axis=1, keepdims=True)
            value_w = jnp.sum(jnp.where(pick, corner_w, 0.0), axis=1, keepdims=True)
            value_e = jnp.where(small == 383, value_e, pltpu.roll(value, 383, 1))
            value_w = jnp.where(small == 0, value_w, pltpu.roll(value, 1, 1))
            diag_ref[side, 8 * k : 8 * k + 8, :] = jnp.where(level8 < edge_e, value_e, 0.0) - jnp.where(
                level8 < edge_w, value_w, 0.0
            )

    def level_step(l, carry):
        lf = l.astype(F32)
        cw = pltpu.roll(col_west, lax.rem(128 - l, 128), 1)
        ce = pltpu.roll(col_east, lax.rem(128 - l, 128), 1)
        masks = [(lf < bottom_ref[i]).astype(F32) for i in range(5)]
        mask, mask_e, mask_w, mask_n, mask_s = masks
        kappa = kappa_ref[l]
        velocity = east_ref[l]
        kap = 0.5 * (kappa + from_east(kappa, ce[:, 40:41]))
        open_face = mask * mask_e
        out_e = open_face * (jnp.maximum(velocity, 0.0) + kap)
        in_e = open_face * (kap - jnp.minimum(velocity, 0.0))
        velocity = from_west(velocity, cw[:, 32:33])
        kap = 0.5 * (kappa + from_west(kappa, cw[:, 40:41]))
        open_face = mask * mask_w
        in_w = open_face * (jnp.maximum(velocity, 0.0) + kap)
        out_w = open_face * (kap - jnp.minimum(velocity, 0.0))
        velocity = north_ref[l]
        kap = 0.5 * (kappa + from_north(kappa, rows_ref[1, pl.ds(40 + l, 1), :]))
        open_face = mask * mask_n
        out_n = open_face * (jnp.maximum(velocity, 0.0) + kap)
        in_n = open_face * (kap - jnp.minimum(velocity, 0.0))
        velocity = from_south(velocity, rows_ref[0, pl.ds(32 + l, 1), :])
        kap = 0.5 * (kappa + from_south(kappa, rows_ref[0, pl.ds(40 + l, 1), :]))
        open_face = mask * mask_s
        in_s = open_face * (jnp.maximum(velocity, 0.0) + kap)
        out_s = open_face * (kap - jnp.minimum(velocity, 0.0))
        keep = 1.0 - (out_e + out_w + out_n + out_s)
        cross = cross_ref[l] * mask
        for t in range(4):
            i = 8 * t + l
            c = tracer_ref[i]
            c_e = from_east(c, ce[:, 8 * t : 8 * t + 1])
            c_w = from_west(c, cw[:, 8 * t : 8 * t + 1])
            c_n = from_north(c, rows_ref[1, pl.ds(i, 1), :])
            c_s = from_south(c, rows_ref[0, pl.ds(i, 1), :])
            diag = mask_e * c_e - mask_w * c_w
            diag_n = from_north(diag, diag_ref[1, pl.ds(i, 1), :])
            diag_s = from_south(diag, diag_ref[0, pl.ds(i, 1), :])
            out_ref[i] = (
                keep * c + in_e * c_e + in_w * c_w + in_n * c_n + in_s * c_s + cross * (diag_n - diag_s)
            )
        return carry

    lax.fori_loop(0, 8, level_step, 0)
    for t in range(4):
        top_ref[t] = out_ref[8 * t]
    for t in range(48):
        done_ref[t] = code_ref[t]


def finish_kernel(points, code_ref, land_ref, back_ref, cross_ref, inner_ref, heat_ref, depth_ref,
                  top_ref, step_hbm, flux_hbm, out_hbm, flux_ref, sum_ref, wide_ref, sems):
    odd = lax.rem(lax.axis_index("lat"), 2)
    cross_off = jnp.where(odd == 1, 2, 0)
    for t in range(48):
        code = code_ref[t]
        rank = lax.bitwise_and(code, 7)
        dlon = lax.bitwise_and(lax.shift_right_logical(code, 3), 7)
        off = lax.shift_right_logical(code, 6)
        at = dlon * PAIR + rank
        own = back_ref[dlon * SLOTS + PAIR + rank].astype(F32)
        cross = cross_ref[at].astype(F32)
        inner = inner_ref[at].astype(F32)
        value = jnp.where(off == 1, own, jnp.where(off == cross_off, cross, inner))
        value = jnp.where(land_ref[t] > 0, value, 0.0)
        flux_ref[t] = value.astype(BF16)
        wide_ref[8 * t : 8 * t + 8, :] = value
    flux_copy = pltpu.make_async_copy(flux_ref, flux_hbm, sems.at[0])
    flux_copy.start()
    heat = jnp.sum(jnp.sum(heat_ref[...], axis=0), axis=1, keepdims=True)
    correction = heat / points
    for j in range(3):
        cols = slice(128 * j, 128 * j + 128)
        wet = depth_ref[:, cols].astype(F32) * tile_column(land_ref, j)
        gain = jnp.where(wet > 0.0, 0.5, 0.0)
        for t in range(4):
            force = wide_ref[pl.ds(8 * j + t, 16, stride=24), :]
            if t == 0:
                force = force - correction
            sum_ref[t, :, cols] = top_ref[t, :, cols] + gain * force
    top_copy = pltpu.make_async_copy(sum_ref, out_hbm.at[:, 0], sems.at[1])
    top_copy.start()
    flux_copy.wait()
    top_copy.wait()


def call(kernel, name, in_specs, out_shape, out_specs, scratch=(), limit=SMALL, **more):
    return pl.pallas_call(
        kernel,
        out_shape=out_shape,
        in_specs=in_specs,
        out_specs=out_specs,
        scratch_shapes=list(scratch),
        name=name,
        compiler_params=pltpu.CompilerParams(vmem_limit_bytes=limit),
        **more,
    )


def shape(dims, dtype):
    return jax.ShapeDtypeStruct(dims, dtype)


def shards(
    tracers,
    east_velocity,
    north_velocity,
    diffusivity,
    cross_diffusivity,
    depth_levels,
    land_mask,
    ocean_state,
    atm_state,
    exchange_coef,
    sunlight,
    mixing,
    o2a_dest,
    o2a_slot,
    a2o_source,
    a2o_tile,
):
    lats = lax.axis_size("lat")
    lons = lax.axis_size("lon")
    lat = lax.axis_index("lat")
    cross_pairs, inner_pairs = [], []
    for i in range(0, lats, 2):
        north, south = i + 1, (i + lats - 1) % lats
        inner_pairs += [(i, north), (north, i)]
        cross_pairs += [(i, south), (south, i)]
    flat = (8 * SLOTS, 8, 128)

    def turn(values):
        values = values.reshape(8, SLOTS, 8, 128)
        return lax.all_to_all(values, "lon", 0, 0, tiled=True).reshape(flat)

    tracers_l = tracers.reshape(32, 16, 384)

    outgoing, code = call(
        functools.partial(pack_kernel, lats),
        "pack",
        [HBM] * 7,
        (shape(flat, BF16), shape((48,), jnp.int32)),
        (VMEM, SMEM),
        [
            pltpu.SMEM((24,), jnp.int32),
            pltpu.SMEM((48,), jnp.int32),
            pltpu.SMEM((48,), jnp.int32),
            pltpu.VMEM((48, 8, 128), BF16),
            pltpu.VMEM((2, 32, 16, 128), F32),
            pltpu.VMEM((8, 16, 128), F32),
            pltpu.VMEM((2, 8, 16, 128), F32),
            pltpu.VMEM((16, 384), jnp.int32),
            pltpu.SemaphoreType.DMA((9,)),
        ],
        limit=60 * 1024 * 1024,
    )(o2a_dest, land_mask, ocean_state, tracers_l, east_velocity, diffusivity, depth_levels)

    source_off = (lat - a2o_source // lons + 1) % lats
    same = a2o_source[:, None] == a2o_source[None, :]
    earlier = a2o_tile[None, :] < a2o_tile[:, None]
    source_rank = jnp.sum((same & earlier).astype(jnp.int32), axis=1)
    place = source_off * 64 + (a2o_source % lons) * 8 + source_rank

    came = turn(outgoing)
    row_shape = shape((69, 8, 128), BF16)
    cross, inner = call(
        rows_kernel,
        "rows",
        [SMEM, VMEM, VMEM, VMEM, VMEM, VMEM],
        (row_shape, row_shape),
        (VMEM, VMEM),
    )(
        land_mask,
        came,
        tracers_l,
        north_velocity,
        diffusivity,
        depth_levels,
    )
    cross = lax.ppermute(cross, "lat", cross_pairs)
    inner = lax.ppermute(inner, "lat", inner_pairs)

    backward = call(
        couple_kernel,
        "couple",
        [SMEM] + [VMEM] * 7,
        shape(flat, BF16),
        VMEM,
        [pltpu.VMEM((48, 8, 128), F32)],
    )(place, came, cross, inner, atm_state, exchange_coef, sunlight, mixing)
    back = turn(backward)

    step, top, done = call(
        functools.partial(stencil_kernel, lats),
        "stencil",
        [SMEM] + [VMEM] * 9 + [SMEM, ANY],
        (shape((32, 16, 384), F32), shape((4, 16, 384), F32), shape((48,), jnp.int32)),
        (VMEM, VMEM, SMEM),
        [pltpu.VMEM((2, 56, 384), F32), pltpu.VMEM((2, 32, 384), F32), pltpu.VMEM((5, 16, 384), F32)],
        cost_estimate=pl.CostEstimate(flops=8000000, bytes_accessed=3000000, transcendentals=0),
    )(
        land_mask,
        came,
        cross,
        inner,
        tracers_l,
        east_velocity,
        north_velocity,
        diffusivity,
        cross_diffusivity,
        depth_levels,
        code,
        backward,
    )

    back_cross, back_inner, heat = call(
        functools.partial(split_kernel, lats),
        "split",
        [VMEM, ANY],
        (shape((48, 8, 128), BF16), shape((48, 8, 128), BF16), shape((lats, 1, 128), F32)),
        (VMEM, VMEM, VMEM),
    )(back, done)
    heat = lax.all_to_all(heat, "lat", 0, 0, tiled=True)
    back_cross = lax.ppermute(back_cross, "lat", cross_pairs)
    back_inner = lax.ppermute(back_inner, "lat", inner_pairs)

    points = float(48 * 128 * lats * lons)
    ocean_flux, new_tracers = call(
        functools.partial(finish_kernel, points),
        "finish",
        [SMEM, SMEM, VMEM, VMEM, VMEM, VMEM, VMEM, VMEM, ANY],
        (shape((48, 8, 128), BF16), shape((4, 8, 16, 384), F32)),
        (ANY, ANY),
        [
            pltpu.VMEM((48, 8, 128), BF16),
            pltpu.VMEM((4, 16, 384), F32),
            pltpu.VMEM((384, 128), F32),
            pltpu.SemaphoreType.DMA((2,)),
        ],
        input_output_aliases={8: 1},
    )(done, land_mask, back, back_cross, back_inner, heat, depth_levels, top, step.reshape(4, 8, 16, 384))
    return (new_tracers, ocean_flux)


def solution(mesh):
    return jax.shard_map(
        shards,
        mesh=mesh,
        in_specs=(
            P(None, None, "lat", "lon"),
            P(None, "lat", "lon"),
            P(None, "lat", "lon"),
            P(None, "lat", "lon"),
            P(None, "lat", "lon"),
            P("lat", "lon"),
            P(("lat", "lon")),
            P(("lat", "lon"), None, None),
            P(("lat", "lon"), None, None),
            P(("lat", "lon"), None),
            P(("lat", "lon"), None),
            P(),
            P(("lat", "lon")),
            P(("lat", "lon")),
            P(("lat", "lon")),
            P(("lat", "lon")),
        ),
        out_specs=(P(None, None, "lat", "lon"), P(("lat", "lon"), None, None)),
        check_vma=False,
    )
```

```python
import functools

import jax
import jax.numpy as jnp
from jax import lax
from jax.experimental import pallas as pl
from jax.experimental.pallas import tpu as pltpu
from jax.sharding import PartitionSpec as P

F32 = jnp.float32
BF16 = jnp.bfloat16
PAIR = 6
SLOTS = 20
LAND = 2.0**100
LAND_TEST = 2.0**90
VMEM = pl.BlockSpec(memory_space=pltpu.VMEM)
SMEM = pl.BlockSpec(memory_space=pltpu.SMEM)
ANY = pl.BlockSpec(memory_space=pl.ANY)
HBM = pl.BlockSpec(memory_space=pltpu.HBM)
SMALL = 16 * 1024 * 1024


def iota(shape, dim):
    return lax.broadcasted_iota(jnp.int32, shape, dim)


def block_of(ref, block):
    return ref[..., 128 * block : 128 * block + 128]


def tile_column(land_ref, block):
    rows = iota((16, 128), 0)
    out = jnp.zeros((16, 128), F32)
    for r in range(16):
        out = jnp.where(rows == r, land_ref[3 * r + block].astype(F32), out)
    return out


def pack_kernel(lats, dest_hbm, land_hbm, state_hbm, tracer_hbm, east_hbm, kappa_hbm, depth_hbm,
                out_ref, code_ref, count_ref, dest_ref, land_ref, state_ref, tracer_ref, east_ref,
                kappa_ref, depth_ref, sems):
    first, last = pl.ds(0, 128), pl.ds(256, 128)
    copies = [
        pltpu.make_async_copy(source, target, sems.at[n])
        for n, (source, target) in enumerate(
            (
                (dest_hbm, dest_ref),
                (land_hbm, land_ref),
                (state_hbm, state_ref),
                (depth_hbm, depth_ref),
                (tracer_hbm.at[:, :, last], tracer_ref.at[0]),
                (tracer_hbm.at[:, :, first], tracer_ref.at[1]),
                (kappa_hbm.at[:, :, last], kappa_ref.at[0]),
                (kappa_hbm.at[:, :, first], kappa_ref.at[1]),
                (east_hbm.at[:, :, last], east_ref),
            )
        )
    ]
    for copy in copies:
        copy.start()
    lat = lax.axis_index("lat")
    lon = lax.axis_index("lon")
    lons = 8
    for i in range(24):
        count_ref[i] = 0
    for copy in copies[:3]:
        copy.wait()
    for t in range(48):
        dest = dest_ref[t]
        off = lax.shift_right_logical(dest, 3) - lat + 1
        off = jnp.where(off < 0, off + lats, jnp.where(off >= lats, off - lats, off))
        dlon = lax.bitwise_and(dest, 7)
        key = off * 8 + dlon
        rank = count_ref[key]
        count_ref[key] = rank + 1
        code_ref[t] = key * 8 + rank
        value = state_ref[t].astype(F32)
        value = jnp.where(land_ref[t] > 0, value, LAND)
        out_ref[dlon * SLOTS + off * PAIR + rank] = value.astype(BF16)
    for copy in copies[3:]:
        copy.wait()
    lanes = iota((16, 128), 1)
    for side, block, lane, shift in ((0, 2, 127, 1), (1, 0, 0, lons - 1)):
        packed = jnp.zeros((16, 128), F32)
        for i in range(32):
            packed = jnp.where(lanes == i, tracer_ref[side, i][:, lane : lane + 1], packed)
        for i in range(8):
            if side == 0:
                packed = jnp.where(lanes == 32 + i, east_ref[i][:, lane : lane + 1], packed)
            packed = jnp.where(lanes == 40 + i, kappa_ref[side, i][:, lane : lane + 1], packed)
        bottom = block_of(depth_ref, block)[...].astype(F32) * tile_column(land_ref, block)
        packed = jnp.where(lanes == 48, bottom[:, lane : lane + 1], packed)
        target = lax.rem(lon + shift, lons)
        out_ref[target * SLOTS + 18] = packed[:8].astype(BF16)
        out_ref[target * SLOTS + 19] = packed[8:].astype(BF16)


def by_parity(body, cross, inner):
    odd = lax.rem(lax.axis_index("lat"), 2)

    @pl.when(odd == 1)
    def _():
        body(cross, inner)

    @pl.when(odd == 0)
    def _():
        body(inner, cross)


def rows_kernel(land_ref, came_ref, tracer_ref, north_ref, kappa_ref, depth_ref, cross_ref, inner_ref):
    inputs = (land_ref, came_ref, tracer_ref, north_ref, kappa_ref, depth_ref)
    by_parity(functools.partial(fill_rows, *inputs), cross_ref, inner_ref)


def fill_rows(land_ref, came_ref, tracer_ref, north_ref, kappa_ref, depth_ref, up_ref, down_ref):
    lon = lax.axis_index("lon")
    west = lax.rem(lon + 7, 8)
    east = lax.rem(lon + 1, 8)
    subs = iota((8, 128), 0)
    for out_ref, first, row in ((up_ref, 12, 15), (down_ref, 0, 0)):
        for s in range(8):
            for k in range(PAIR):
                out_ref[s * PAIR + k] = came_ref[s * SLOTS + first + k]
        half, sub = (19, 7) if row else (18, 0)
        corners = (
            came_ref[west * SLOTS + half].astype(F32)[sub : sub + 1],
            None,
            came_ref[east * SLOTS + half].astype(F32)[sub : sub + 1],
        )
        for j in range(3):
            cols = slice(128 * j, 128 * j + 128)
            for k in range(4):
                out_ref[48 + 3 * k + j] = tracer_ref[8 * k : 8 * k + 8, row, cols].astype(BF16)
            if row:
                out_ref[48 + 12 + j] = north_ref[:, row, cols].astype(BF16)
            else:
                out_ref[48 + 12 + j] = jnp.zeros((8, 128), BF16)
            out_ref[48 + 15 + j] = kappa_ref[:, row, cols].astype(BF16)
            bottom = depth_ref[row : row + 1, cols].astype(F32) * land_ref[3 * row + j].astype(F32)
            last = jnp.where(subs == 0, bottom, 0.0)
            if j != 1:
                last = jnp.where(subs == 1, corners[j], last)
            out_ref[48 + 18 + j] = last.astype(BF16)


def couple_kernel(place_ref, came_ref, cross_ref, inner_ref, atm_ref, coef_ref, sun_ref, mixing_ref,
                  back_cross_ref, back_inner_ref, back_own_ref, heat_ref, got_ref, out_ref):
    odd = lax.rem(lax.axis_index("lat"), 2)
    cross_off = jnp.where(odd == 1, 0, 2)
    total = jnp.zeros((8, 128), F32)
    for q in range(48):
        code = place_ref[q]
        rank = lax.bitwise_and(code, 7)
        slon = lax.bitwise_and(lax.shift_right_logical(code, 3), 7)
        off = lax.shift_right_logical(code, 6)
        at = slon * PAIR + rank
        own = came_ref[slon * SLOTS + PAIR + rank].astype(F32)
        cross = cross_ref[at].astype(F32)
        inner = inner_ref[at].astype(F32)
        value = jnp.where(off == 1, own, jnp.where(off == cross_off, cross, inner))
        got_ref[q] = value
        total = total + coef_ref[q : q + 1, :] * jnp.where(value < LAND_TEST, value, 0.0)
    weight = jnp.sum(jnp.sum(coef_ref[...], axis=0, keepdims=True), axis=1, keepdims=True)
    band_mean = jnp.sum(total, axis=1, keepdims=True) / weight
    mixing = mixing_ref[...]
    columns = [jnp.broadcast_to(mixing[:, g : g + 1], (8, 128)) for g in range(8)]
    heat = jnp.zeros((8, 128), F32)
    first = iota((8, 128), 0) == 0
    for q in range(48):
        code = place_ref[q]
        rank = lax.bitwise_and(code, 7)
        slon = lax.bitwise_and(lax.shift_right_logical(code, 3), 7)
        off = lax.shift_right_logical(code, 6)
        value = got_ref[q]
        wet = value < LAND_TEST
        drive = atm_ref[q] + band_mean - 2.0 * jnp.where(wet, value, 0.0)
        mixed = columns[0] * drive[0:1]
        for g in range(1, 8):
            mixed = mixed + columns[g] * drive[g : g + 1]
        coef = coef_ref[q : q + 1, :]
        flux = coef * mixed
        flux = flux + jnp.where(first, coef * sun_ref[q : q + 1, :], 0.0)
        rounded = flux.astype(BF16)
        way = jnp.where(off == 1, 2, jnp.where(off == cross_off, 0, 1))
        out_ref[way * 48 + slon * PAIR + rank] = rounded
        heat = heat + jnp.where(wet, rounded.astype(F32), 0.0)
    for i, ref in enumerate((back_cross_ref, back_inner_ref, back_own_ref)):
        ref[...] = out_ref[48 * i : 48 * i + 48]
    heat_ref[...] = jnp.broadcast_to(heat[0:1][None], heat_ref.shape)


def merge_kernel(cross_ref, inner_ref, own_ref, heat_ref, out_ref):
    odd = lax.rem(lax.axis_index("lat"), 2)
    cross_at = jnp.where(odd == 1, 12, 0)
    inner_at = 12 - cross_at
    subs = iota((8, 128), 0)
    row = jnp.broadcast_to(jnp.sum(heat_ref[...], axis=0), (8, 128))
    one = row.astype(BF16).astype(F32)
    two = (row - one).astype(BF16).astype(F32)
    three = row - one - two
    parts = jnp.where(subs == 0, one, jnp.where(subs == 1, two, jnp.where(subs == 2, three, 0.0)))
    for s in range(8):
        for k in range(PAIR):
            out_ref[s * SLOTS + cross_at + k] = cross_ref[s * PAIR + k]
            out_ref[s * SLOTS + inner_at + k] = inner_ref[s * PAIR + k]
            out_ref[s * SLOTS + PAIR + k] = own_ref[s * PAIR + k]
        out_ref[s * SLOTS + 18] = parts.astype(BF16)


def stencil_kernel(lats, land_ref, came_ref, cross_halo_ref, inner_halo_ref, tracer_ref, east_ref, north_ref,
                   kappa_ref, cross_ref, depth_ref, code_ref, after_ref, out_ref, top_ref, done_ref, rows_ref,
                   diag_ref, bottom_ref):
    lat = lax.axis_index("lat")
    lon = lax.axis_index("lon")
    west = lax.rem(lon + 7, 8)
    east = lax.rem(lon + 1, 8)
    full = (16, 384)
    lanes = iota(full, 1)
    subs = iota(full, 0)
    at_west, at_east = lanes == 0, lanes == 383
    at_south, at_north = subs == 0, subs == 15
    small = iota((8, 384), 1)
    lane8, sub8 = iota((8, 128), 1), iota((8, 128), 0)

    def columns_of(side):
        return jnp.concatenate(
            [came_ref[side * SLOTS + 18].astype(F32), came_ref[side * SLOTS + 19].astype(F32)], axis=0
        )

    def from_west(v, column):
        return jnp.where(at_west, column, pltpu.roll(v, 1, 1))

    def from_east(v, column):
        return jnp.where(at_east, column, pltpu.roll(v, 383, 1))

    def from_south(v, row):
        return jnp.where(at_south, row, pltpu.roll(v, 1, 0))

    def from_north(v, row):
        return jnp.where(at_north, row, pltpu.roll(v, 15, 0))

    col_west, col_east = columns_of(west), columns_of(east)

    def unpack_rows(high_ref, low_ref):
        for side, ref in enumerate((low_ref, high_ref)):
            inside = jnp.where(lat == (0, lats - 1)[side], 0.0, 1.0)
            for k in range(7):
                for j in range(3):
                    tile = ref[48 + 3 * k + j].astype(F32)
                    if k == 6:
                        tile = jnp.where(sub8 == 0, tile * inside, tile)
                    rows_ref[side, 8 * k : 8 * k + 8, 128 * j : 128 * j + 128] = tile

    by_parity(unpack_rows, cross_halo_ref, inner_halo_ref)
    for j in range(3):
        cols = slice(128 * j, 128 * j + 128)
        bottom_ref[0, :, cols] = depth_ref[:, cols].astype(F32) * tile_column(land_ref, j)
    bottom = bottom_ref[0]
    bottom_ref[1] = from_east(bottom, col_east[:, 48:49])
    bottom_ref[2] = from_west(bottom, col_west[:, 48:49])
    bottom_ref[3] = from_north(bottom, rows_ref[1, 48:49, :])
    bottom_ref[4] = from_south(bottom, rows_ref[0, 48:49, :])

    level8 = iota((8, 384), 0).astype(F32)
    for side in range(2):
        inside = jnp.where(lat == (0, lats - 1)[side], 0.0, 1.0)
        corner_w = jnp.broadcast_to(rows_ref[side, 49:50, 0:128], (8, 128))
        corner_e = jnp.broadcast_to(rows_ref[side, 49:50, 256:384], (8, 128))
        edge = jnp.broadcast_to(rows_ref[side, 48:49, :], (8, 384))
        edge_e = jnp.where(small == 383, corner_e[:, 48:49] * inside, pltpu.roll(edge, 383, 1))
        edge_w = jnp.where(small == 0, corner_w[:, 48:49] * inside, pltpu.roll(edge, 1, 1))
        for k in range(4):
            value = rows_ref[side, 8 * k : 8 * k + 8, :]
            pick = lane8 == sub8 + 8 * k
            value_e = jnp.sum(jnp.where(pick, corner_e, 0.0), axis=1, keepdims=True)
            value_w = jnp.sum(jnp.where(pick, corner_w, 0.0), axis=1, keepdims=True)
            value_e = jnp.where(small == 383, value_e, pltpu.roll(value, 383, 1))
            value_w = jnp.where(small == 0, value_w, pltpu.roll(value, 1, 1))
            diag_ref[side, 8 * k : 8 * k + 8, :] = jnp.where(level8 < edge_e, value_e, 0.0) - jnp.where(
                level8 < edge_w, value_w, 0.0
            )

    def level_step(l, carry):
        lf = l.astype(F32)
        cw = pltpu.roll(col_west, lax.rem(128 - l, 128), 1)
        ce = pltpu.roll(col_east, lax.rem(128 - l, 128), 1)
        masks = [(lf < bottom_ref[i]).astype(F32) for i in range(5)]
        mask, mask_e, mask_w, mask_n, mask_s = masks
        kappa = kappa_ref[l]
        velocity = east_ref[l]
        kap = 0.5 * (kappa + from_east(kappa, ce[:, 40:41]))
        open_face = mask * mask_e
        out_e = open_face * (jnp.maximum(velocity, 0.0) + kap)
        in_e = open_face * (kap - jnp.minimum(velocity, 0.0))
        velocity = from_west(velocity, cw[:, 32:33])
        kap = 0.5 * (kappa + from_west(kappa, cw[:, 40:41]))
        open_face = mask * mask_w
        in_w = open_face * (jnp.maximum(velocity, 0.0) + kap)
        out_w = open_face * (kap - jnp.minimum(velocity, 0.0))
        velocity = north_ref[l]
        kap = 0.5 * (kappa + from_north(kappa, rows_ref[1, pl.ds(40 + l, 1), :]))
        open_face = mask * mask_n
        out_n = open_face * (jnp.maximum(velocity, 0.0) + kap)
        in_n = open_face * (kap - jnp.minimum(velocity, 0.0))
        velocity = from_south(velocity, rows_ref[0, pl.ds(32 + l, 1), :])
        kap = 0.5 * (kappa + from_south(kappa, rows_ref[0, pl.ds(40 + l, 1), :]))
        open_face = mask * mask_s
        in_s = open_face * (jnp.maximum(velocity, 0.0) + kap)
        out_s = open_face * (kap - jnp.minimum(velocity, 0.0))
        keep = 1.0 - (out_e + out_w + out_n + out_s)
        cross = cross_ref[l] * mask
        for t in range(4):
            i = 8 * t + l
            c = tracer_ref[i]
            c_e = from_east(c, ce[:, 8 * t : 8 * t + 1])
            c_w = from_west(c, cw[:, 8 * t : 8 * t + 1])
            c_n = from_north(c, rows_ref[1, pl.ds(i, 1), :])
            c_s = from_south(c, rows_ref[0, pl.ds(i, 1), :])
            diag = mask_e * c_e - mask_w * c_w
            diag_n = from_north(diag, diag_ref[1, pl.ds(i, 1), :])
            diag_s = from_south(diag, diag_ref[0, pl.ds(i, 1), :])
            out_ref[i] = (
                keep * c + in_e * c_e + in_w * c_w + in_n * c_n + in_s * c_s + cross * (diag_n - diag_s)
            )
        return carry

    lax.fori_loop(0, 8, level_step, 0)
    for t in range(4):
        top_ref[t] = out_ref[8 * t]
    for t in range(48):
        done_ref[t] = code_ref[t]


def finish_kernel(points, code_ref, land_ref, back_ref, depth_ref, top_ref, step_hbm, flux_hbm, out_hbm,
                  flux_ref, sum_ref, wide_ref, sems):
    for t in range(48):
        code = code_ref[t]
        rank = lax.bitwise_and(code, 7)
        dlon = lax.bitwise_and(lax.shift_right_logical(code, 3), 7)
        off = lax.shift_right_logical(code, 6)
        value = back_ref[dlon * SLOTS + off * PAIR + rank].astype(F32)
        value = jnp.where(land_ref[t] > 0, value, 0.0)
        flux_ref[t] = value.astype(BF16)
        wide_ref[8 * t : 8 * t + 8, :] = value
    flux_copy = pltpu.make_async_copy(flux_ref, flux_hbm, sems.at[0])
    flux_copy.start()
    heat = jnp.zeros((8, 128), F32)
    for i in range(8):
        heat = heat + back_ref[i * SLOTS + 18].astype(F32)
    heat = jnp.sum(jnp.sum(heat, axis=0, keepdims=True), axis=1, keepdims=True)
    correction = heat / points
    for j in range(3):
        cols = slice(128 * j, 128 * j + 128)
        wet = depth_ref[:, cols].astype(F32) * tile_column(land_ref, j)
        gain = jnp.where(wet > 0.0, 0.5, 0.0)
        for t in range(4):
            force = wide_ref[pl.ds(8 * j + t, 16, stride=24), :]
            if t == 0:
                force = force - correction
            sum_ref[t, :, cols] = top_ref[t, :, cols] + gain * force
    top_copy = pltpu.make_async_copy(sum_ref, out_hbm.at[:, 0], sems.at[1])
    top_copy.start()
    flux_copy.wait()
    top_copy.wait()


def call(kernel, name, in_specs, out_shape, out_specs, scratch=(), limit=SMALL, **more):
    return pl.pallas_call(
        kernel,
        out_shape=out_shape,
        in_specs=in_specs,
        out_specs=out_specs,
        scratch_shapes=list(scratch),
        name=name,
        compiler_params=pltpu.CompilerParams(vmem_limit_bytes=limit),
        **more,
    )


def shape(dims, dtype):
    return jax.ShapeDtypeStruct(dims, dtype)


def shards(
    tracers,
    east_velocity,
    north_velocity,
    diffusivity,
    cross_diffusivity,
    depth_levels,
    land_mask,
    ocean_state,
    atm_state,
    exchange_coef,
    sunlight,
    mixing,
    o2a_dest,
    o2a_slot,
    a2o_source,
    a2o_tile,
):
    lats = lax.axis_size("lat")
    lons = lax.axis_size("lon")
    lat = lax.axis_index("lat")
    cross_pairs, inner_pairs = [], []
    for i in range(0, lats, 2):
        north, south = i + 1, (i + lats - 1) % lats
        inner_pairs += [(i, north), (north, i)]
        cross_pairs += [(i, south), (south, i)]
    flat = (8 * SLOTS, 8, 128)

    def turn(values):
        values = values.reshape(8, SLOTS, 8, 128)
        return lax.all_to_all(values, "lon", 0, 0, tiled=True).reshape(flat)

    tracers_l = tracers.reshape(32, 16, 384)

    outgoing, code = call(
        functools.partial(pack_kernel, lats),
        "pack",
        [HBM] * 7,
        (shape(flat, BF16), shape((48,), jnp.int32)),
        (VMEM, SMEM),
        [
            pltpu.SMEM((24,), jnp.int32),
            pltpu.SMEM((48,), jnp.int32),
            pltpu.SMEM((48,), jnp.int32),
            pltpu.VMEM((48, 8, 128), BF16),
            pltpu.VMEM((2, 32, 16, 128), F32),
            pltpu.VMEM((8, 16, 128), F32),
            pltpu.VMEM((2, 8, 16, 128), F32),
            pltpu.VMEM((16, 384), jnp.int32),
            pltpu.SemaphoreType.DMA((9,)),
        ],
        limit=60 * 1024 * 1024,
    )(o2a_dest, land_mask, ocean_state, tracers_l, east_velocity, diffusivity, depth_levels)

    source_off = (lat - a2o_source // lons + 1) % lats
    same = a2o_source[:, None] == a2o_source[None, :]
    earlier = a2o_tile[None, :] < a2o_tile[:, None]
    source_rank = jnp.sum((same & earlier).astype(jnp.int32), axis=1)
    place = source_off * 64 + (a2o_source % lons) * 8 + source_rank

    came = turn(outgoing)
    row_shape = shape((69, 8, 128), BF16)
    cross, inner = call(
        rows_kernel,
        "rows",
        [SMEM, VMEM, VMEM, VMEM, VMEM, VMEM],
        (row_shape, row_shape),
        (VMEM, VMEM),
    )(
        land_mask,
        came,
        tracers_l,
        north_velocity,
        diffusivity,
        depth_levels,
    )
    cross = lax.ppermute(cross, "lat", cross_pairs)
    inner = lax.ppermute(inner, "lat", inner_pairs)

    tiles_shape = shape((48, 8, 128), BF16)
    back_cross, back_inner, back_own, heat = call(
        couple_kernel,
        "couple",
        [SMEM] + [VMEM] * 7,
        (tiles_shape, tiles_shape, tiles_shape, shape((lats, 1, 128), F32)),
        (VMEM, VMEM, VMEM, VMEM),
        [pltpu.VMEM((48, 8, 128), F32), pltpu.VMEM((144, 8, 128), BF16)],
    )(place, came, cross, inner, atm_state, exchange_coef, sunlight, mixing)
    heat = lax.all_to_all(heat, "lat", 0, 0, tiled=True)
    back_cross = lax.ppermute(back_cross, "lat", cross_pairs)
    back_inner = lax.ppermute(back_inner, "lat", inner_pairs)
    backward = call(merge_kernel, "merge", [VMEM] * 4, shape(flat, BF16), VMEM)(
        back_cross, back_inner, back_own, heat
    )
    back = turn(backward)

    step, top, done = call(
        functools.partial(stencil_kernel, lats),
        "stencil",
        [SMEM] + [VMEM] * 9 + [SMEM, ANY],
        (shape((32, 16, 384), F32), shape((4, 16, 384), F32), shape((48,), jnp.int32)),
        (VMEM, VMEM, SMEM),
        [pltpu.VMEM((2, 56, 384), F32), pltpu.VMEM((2, 32, 384), F32), pltpu.VMEM((5, 16, 384), F32)],
        cost_estimate=pl.CostEstimate(flops=8000000, bytes_accessed=3000000, transcendentals=0),
    )(
        land_mask,
        came,
        cross,
        inner,
        tracers_l,
        east_velocity,
        north_velocity,
        diffusivity,
        cross_diffusivity,
        depth_levels,
        code,
        backward,
    )

    points = float(48 * 128 * lats * lons)
    ocean_flux, new_tracers = call(
        functools.partial(finish_kernel, points),
        "finish",
        [SMEM, SMEM, VMEM, VMEM, VMEM, ANY],
        (tiles_shape, shape((4, 8, 16, 384), F32)),
        (ANY, ANY),
        [
            pltpu.VMEM((48, 8, 128), BF16),
            pltpu.VMEM((4, 16, 384), F32),
            pltpu.VMEM((384, 128), F32),
            pltpu.SemaphoreType.DMA((2,)),
        ],
        input_output_aliases={5: 1},
    )(done, land_mask, back, depth_levels, top, step.reshape(4, 8, 16, 384))
    return (new_tracers, ocean_flux)


def solution(mesh):
    return jax.shard_map(
        shards,
        mesh=mesh,
        in_specs=(
            P(None, None, "lat", "lon"),
            P(None, "lat", "lon"),
            P(None, "lat", "lon"),
            P(None, "lat", "lon"),
            P(None, "lat", "lon"),
            P("lat", "lon"),
            P(("lat", "lon")),
            P(("lat", "lon"), None, None),
            P(("lat", "lon"), None, None),
            P(("lat", "lon"), None),
            P(("lat", "lon"), None),
            P(),
            P(("lat", "lon")),
            P(("lat", "lon")),
            P(("lat", "lon")),
            P(("lat", "lon")),
        ),
        out_specs=(P(None, None, "lat", "lon"), P(("lat", "lon"), None, None)),
        check_vma=False,
    )
```

```python
import functools

import jax
import jax.numpy as jnp
from jax import lax
from jax.experimental import pallas as pl
from jax.experimental.pallas import tpu as pltpu
from jax.sharding import PartitionSpec as P

F32 = jnp.float32
BF16 = jnp.bfloat16
PAIR = 6
SLOTS = 20
LAND = 2.0**100
LAND_TEST = 2.0**90
VMEM = pl.BlockSpec(memory_space=pltpu.VMEM)
SMEM = pl.BlockSpec(memory_space=pltpu.SMEM)
ANY = pl.BlockSpec(memory_space=pl.ANY)
HBM = pl.BlockSpec(memory_space=pltpu.HBM)
SMALL = 16 * 1024 * 1024


def iota(shape, dim):
    return lax.broadcasted_iota(jnp.int32, shape, dim)


def block_of(ref, block):
    return ref[..., 128 * block : 128 * block + 128]


def tile_column(land_ref, block):
    rows = iota((16, 128), 0)
    out = jnp.zeros((16, 128), F32)
    for r in range(16):
        out = jnp.where(rows == r, land_ref[3 * r + block].astype(F32), out)
    return out


def pack_kernel(lats, dest_hbm, land_hbm, state_hbm, tracer_hbm, east_hbm, kappa_hbm, depth_hbm,
                out_ref, code_ref, count_ref, dest_ref, land_ref, state_ref, tracer_ref, east_ref,
                kappa_ref, depth_ref, sems):
    first, last = pl.ds(0, 128), pl.ds(256, 128)
    copies = [
        pltpu.make_async_copy(source, target, sems.at[n])
        for n, (source, target) in enumerate(
            (
                (dest_hbm, dest_ref),
                (land_hbm, land_ref),
                (state_hbm, state_ref),
                (depth_hbm, depth_ref),
                (tracer_hbm.at[:, :, last], tracer_ref.at[0]),
                (tracer_hbm.at[:, :, first], tracer_ref.at[1]),
                (kappa_hbm.at[:, :, last], kappa_ref.at[0]),
                (kappa_hbm.at[:, :, first], kappa_ref.at[1]),
                (east_hbm.at[:, :, last], east_ref),
            )
        )
    ]
    for copy in copies:
        copy.start()
    lat = lax.axis_index("lat")
    lon = lax.axis_index("lon")
    lons = 8
    for i in range(24):
        count_ref[i] = 0
    for copy in copies[:3]:
        copy.wait()
    for t in range(48):
        dest = dest_ref[t]
        off = lax.shift_right_logical(dest, 3) - lat + 1
        off = jnp.where(off < 0, off + lats, jnp.where(off >= lats, off - lats, off))
        dlon = lax.bitwise_and(dest, 7)
        key = off * 8 + dlon
        rank = count_ref[key]
        count_ref[key] = rank + 1
        code_ref[t] = key * 8 + rank
        value = state_ref[t].astype(F32)
        value = jnp.where(land_ref[t] > 0, value, LAND)
        out_ref[dlon * SLOTS + off * PAIR + rank] = value.astype(BF16)
    for copy in copies[3:]:
        copy.wait()
    lanes = iota((16, 128), 1)
    for side, block, lane, shift in ((0, 2, 127, 1), (1, 0, 0, lons - 1)):
        packed = jnp.zeros((16, 128), F32)
        for i in range(32):
            packed = jnp.where(lanes == i, tracer_ref[side, i][:, lane : lane + 1], packed)
        for i in range(8):
            if side == 0:
                packed = jnp.where(lanes == 32 + i, east_ref[i][:, lane : lane + 1], packed)
            packed = jnp.where(lanes == 40 + i, kappa_ref[side, i][:, lane : lane + 1], packed)
        bottom = block_of(depth_ref, block)[...].astype(F32) * tile_column(land_ref, block)
        packed = jnp.where(lanes == 48, bottom[:, lane : lane + 1], packed)
        target = lax.rem(lon + shift, lons)
        out_ref[target * SLOTS + 18] = packed[:8].astype(BF16)
        out_ref[target * SLOTS + 19] = packed[8:].astype(BF16)


def by_parity(body, cross, inner):
    odd = lax.rem(lax.axis_index("lat"), 2)

    @pl.when(odd == 1)
    def _():
        body(cross, inner)

    @pl.when(odd == 0)
    def _():
        body(inner, cross)


def rows_kernel(land_ref, came_ref, tracer_ref, north_ref, kappa_ref, depth_ref, cross_ref, inner_ref):
    inputs = (land_ref, came_ref, tracer_ref, north_ref, kappa_ref, depth_ref)
    by_parity(functools.partial(fill_rows, *inputs), cross_ref, inner_ref)


def fill_rows(land_ref, came_ref, tracer_ref, north_ref, kappa_ref, depth_ref, up_ref, down_ref):
    lon = lax.axis_index("lon")
    west = lax.rem(lon + 7, 8)
    east = lax.rem(lon + 1, 8)
    subs = iota((8, 128), 0)
    for out_ref, first, row in ((up_ref, 12, 15), (down_ref, 0, 0)):
        for s in range(8):
            for k in range(PAIR):
                out_ref[s * PAIR + k] = came_ref[s * SLOTS + first + k]
        half, sub = (19, 7) if row else (18, 0)
        corners = (
            came_ref[west * SLOTS + half].astype(F32)[sub : sub + 1],
            None,
            came_ref[east * SLOTS + half].astype(F32)[sub : sub + 1],
        )
        for j in range(3):
            cols = slice(128 * j, 128 * j + 128)
            for k in range(4):
                out_ref[48 + 3 * k + j] = tracer_ref[8 * k : 8 * k + 8, row, cols].astype(BF16)
            if row:
                out_ref[48 + 12 + j] = north_ref[:, row, cols].astype(BF16)
            else:
                out_ref[48 + 12 + j] = jnp.zeros((8, 128), BF16)
            out_ref[48 + 15 + j] = kappa_ref[:, row, cols].astype(BF16)
            bottom = depth_ref[row : row + 1, cols].astype(F32) * land_ref[3 * row + j].astype(F32)
            last = jnp.where(subs == 0, bottom, 0.0)
            if j != 1:
                last = jnp.where(subs == 1, corners[j], last)
            out_ref[48 + 18 + j] = last.astype(BF16)


def couple_kernel(place_ref, came_ref, cross_ref, inner_ref, atm_ref, coef_ref, sun_ref, mixing_ref,
                  out_ref, got_ref):
    odd = lax.rem(lax.axis_index("lat"), 2)
    cross_off = jnp.where(odd == 1, 0, 2)
    total = jnp.zeros((8, 128), F32)
    for q in range(48):
        code = place_ref[q]
        rank = lax.bitwise_and(code, 7)
        slon = lax.bitwise_and(lax.shift_right_logical(code, 3), 7)
        off = lax.shift_right_logical(code, 6)
        at = slon * PAIR + rank
        own = came_ref[slon * SLOTS + PAIR + rank].astype(F32)
        cross = cross_ref[at].astype(F32)
        inner = inner_ref[at].astype(F32)
        value = jnp.where(off == 1, own, jnp.where(off == cross_off, cross, inner))
        got_ref[q] = value
        total = total + coef_ref[q : q + 1, :] * jnp.where(value < LAND_TEST, value, 0.0)
    weight = jnp.sum(jnp.sum(coef_ref[...], axis=0, keepdims=True), axis=1, keepdims=True)
    band_mean = jnp.sum(total, axis=1, keepdims=True) / weight
    mixing = mixing_ref[...]
    columns = [jnp.broadcast_to(mixing[:, g : g + 1], (8, 128)) for g in range(8)]
    heat = jnp.zeros((8, 128), F32)
    first = iota((8, 128), 0) == 0
    for q in range(48):
        code = place_ref[q]
        rank = lax.bitwise_and(code, 7)
        slon = lax.bitwise_and(lax.shift_right_logical(code, 3), 7)
        off = lax.shift_right_logical(code, 6)
        value = got_ref[q]
        wet = value < LAND_TEST
        drive = atm_ref[q] + band_mean - 2.0 * jnp.where(wet, value, 0.0)
        mixed = columns[0] * drive[0:1]
        for g in range(1, 8):
            mixed = mixed + columns[g] * drive[g : g + 1]
        coef = coef_ref[q : q + 1, :]
        flux = coef * mixed
        flux = flux + jnp.where(first, coef * sun_ref[q : q + 1, :], 0.0)
        rounded = flux.astype(BF16)
        out_ref[slon * SLOTS + off * PAIR + rank] = rounded
        heat = heat + jnp.where(wet, rounded.astype(F32), 0.0)
    subs = iota((8, 128), 0)
    row = jnp.broadcast_to(heat[0:1], (8, 128))
    one = row.astype(BF16).astype(F32)
    two = (row - one).astype(BF16).astype(F32)
    three = row - one - two
    parts = jnp.where(subs == 0, one, jnp.where(subs == 1, two, jnp.where(subs == 2, three, 0.0)))
    for s in range(8):
        out_ref[s * SLOTS + 18] = parts.astype(BF16)


def split_kernel(lats, back_ref, done_ref, cross_ref, inner_ref, heat_ref):
    odd = lax.rem(lax.axis_index("lat"), 2)
    cross_at = jnp.where(odd == 1, 0, 12)
    inner_at = 12 - cross_at
    heat = jnp.zeros((8, 128), F32)
    for s in range(8):
        heat = heat + back_ref[s * SLOTS + 18].astype(F32)
        for k in range(PAIR):
            cross_ref[s * PAIR + k] = back_ref[s * SLOTS + cross_at + k]
            inner_ref[s * PAIR + k] = back_ref[s * SLOTS + inner_at + k]
    row = jnp.sum(heat, axis=0, keepdims=True)
    heat_ref[...] = jnp.broadcast_to(row[None], (lats, 1, 128))


def stencil_kernel(lats, land_ref, came_ref, cross_halo_ref, inner_halo_ref, tracer_ref, east_ref, north_ref,
                   kappa_ref, cross_ref, depth_ref, code_ref, after_ref, out_ref, top_ref, done_ref, rows_ref,
                   diag_ref, bottom_ref):
    lat = lax.axis_index("lat")
    lon = lax.axis_index("lon")
    west = lax.rem(lon + 7, 8)
    east = lax.rem(lon + 1, 8)
    full = (16, 384)
    lanes = iota(full, 1)
    subs = iota(full, 0)
    at_west, at_east = lanes == 0, lanes == 383
    at_south, at_north = subs == 0, subs == 15
    small = iota((8, 384), 1)
    lane8, sub8 = iota((8, 128), 1), iota((8, 128), 0)

    def columns_of(side):
        return jnp.concatenate(
            [came_ref[side * SLOTS + 18].astype(F32), came_ref[side * SLOTS + 19].astype(F32)], axis=0
        )

    def from_west(v, column):
        return jnp.where(at_west, column, pltpu.roll(v, 1, 1))

    def from_east(v, column):
        return jnp.where(at_east, column, pltpu.roll(v, 383, 1))

    def from_south(v, row):
        return jnp.where(at_south, row, pltpu.roll(v, 1, 0))

    def from_north(v, row):
        return jnp.where(at_north, row, pltpu.roll(v, 15, 0))

    col_west, col_east = columns_of(west), columns_of(east)

    def unpack_rows(high_ref, low_ref):
        for side, ref in enumerate((low_ref, high_ref)):
            inside = jnp.where(lat == (0, lats - 1)[side], 0.0, 1.0)
            for k in range(7):
                for j in range(3):
                    tile = ref[48 + 3 * k + j].astype(F32)
                    if k == 6:
                        tile = jnp.where(sub8 == 0, tile * inside, tile)
                    rows_ref[side, 8 * k : 8 * k + 8, 128 * j : 128 * j + 128] = tile

    by_parity(unpack_rows, cross_halo_ref, inner_halo_ref)
    for j in range(3):
        cols = slice(128 * j, 128 * j + 128)
        bottom_ref[0, :, cols] = depth_ref[:, cols].astype(F32) * tile_column(land_ref, j)
    bottom = bottom_ref[0]
    bottom_ref[1] = from_east(bottom, col_east[:, 48:49])
    bottom_ref[2] = from_west(bottom, col_west[:, 48:49])
    bottom_ref[3] = from_north(bottom, rows_ref[1, 48:49, :])
    bottom_ref[4] = from_south(bottom, rows_ref[0, 48:49, :])

    level8 = iota((8, 384), 0).astype(F32)
    for side in range(2):
        inside = jnp.where(lat == (0, lats - 1)[side], 0.0, 1.0)
        corner_w = jnp.broadcast_to(rows_ref[side, 49:50, 0:128], (8, 128))
        corner_e = jnp.broadcast_to(rows_ref[side, 49:50, 256:384], (8, 128))
        edge = jnp.broadcast_to(rows_ref[side, 48:49, :], (8, 384))
        edge_e = jnp.where(small == 383, corner_e[:, 48:49] * inside, pltpu.roll(edge, 383, 1))
        edge_w = jnp.where(small == 0, corner_w[:, 48:49] * inside, pltpu.roll(edge, 1, 1))
        for k in range(4):
            value = rows_ref[side, 8 * k : 8 * k + 8, :]
            pick = lane8 == sub8 + 8 * k
            value_e = jnp.sum(jnp.where(pick, corner_e, 0.0), axis=1, keepdims=True)
            value_w = jnp.sum(jnp.where(pick, corner_w, 0.0), axis=1, keepdims=True)
            value_e = jnp.where(small == 383, value_e, pltpu.roll(value, 383, 1))
            value_w = jnp.where(small == 0, value_w, pltpu.roll(value, 1, 1))
            diag_ref[side, 8 * k : 8 * k + 8, :] = jnp.where(level8 < edge_e, value_e, 0.0) - jnp.where(
                level8 < edge_w, value_w, 0.0
            )

    def level_step(l, carry):
        lf = l.astype(F32)
        cw = pltpu.roll(col_west, lax.rem(128 - l, 128), 1)
        ce = pltpu.roll(col_east, lax.rem(128 - l, 128), 1)
        masks = [(lf < bottom_ref[i]).astype(F32) for i in range(5)]
        mask, mask_e, mask_w, mask_n, mask_s = masks
        kappa = kappa_ref[l]
        velocity = east_ref[l]
        kap = 0.5 * (kappa + from_east(kappa, ce[:, 40:41]))
        open_face = mask * mask_e
        out_e = open_face * (jnp.maximum(velocity, 0.0) + kap)
        in_e = open_face * (kap - jnp.minimum(velocity, 0.0))
        velocity = from_west(velocity, cw[:, 32:33])
        kap = 0.5 * (kappa + from_west(kappa, cw[:, 40:41]))
        open_face = mask * mask_w
        in_w = open_face * (jnp.maximum(velocity, 0.0) + kap)
        out_w = open_face * (kap - jnp.minimum(velocity, 0.0))
        velocity = north_ref[l]
        kap = 0.5 * (kappa + from_north(kappa, rows_ref[1, pl.ds(40 + l, 1), :]))
        open_face = mask * mask_n
        out_n = open_face * (jnp.maximum(velocity, 0.0) + kap)
        in_n = open_face * (kap - jnp.minimum(velocity, 0.0))
        velocity = from_south(velocity, rows_ref[0, pl.ds(32 + l, 1), :])
        kap = 0.5 * (kappa + from_south(kappa, rows_ref[0, pl.ds(40 + l, 1), :]))
        open_face = mask * mask_s
        in_s = open_face * (jnp.maximum(velocity, 0.0) + kap)
        out_s = open_face * (kap - jnp.minimum(velocity, 0.0))
        keep = 1.0 - (out_e + out_w + out_n + out_s)
        cross = cross_ref[l] * mask
        for t in range(4):
            i = 8 * t + l
            c = tracer_ref[i]
            c_e = from_east(c, ce[:, 8 * t : 8 * t + 1])
            c_w = from_west(c, cw[:, 8 * t : 8 * t + 1])
            c_n = from_north(c, rows_ref[1, pl.ds(i, 1), :])
            c_s = from_south(c, rows_ref[0, pl.ds(i, 1), :])
            diag = mask_e * c_e - mask_w * c_w
            diag_n = from_north(diag, diag_ref[1, pl.ds(i, 1), :])
            diag_s = from_south(diag, diag_ref[0, pl.ds(i, 1), :])
            out_ref[i] = (
                keep * c + in_e * c_e + in_w * c_w + in_n * c_n + in_s * c_s + cross * (diag_n - diag_s)
            )
        return carry

    lax.fori_loop(0, 8, level_step, 0)
    for t in range(4):
        top_ref[t] = out_ref[8 * t]
    for t in range(48):
        done_ref[t] = code_ref[t]


def finish_kernel(points, code_ref, land_ref, back_ref, cross_ref, inner_ref, heat_ref, depth_ref,
                  top_ref, step_hbm, flux_ref, out_ref, wide_ref):
    odd = lax.rem(lax.axis_index("lat"), 2)
    cross_off = jnp.where(odd == 1, 2, 0)
    for t in range(48):
        code = code_ref[t]
        rank = lax.bitwise_and(code, 7)
        dlon = lax.bitwise_and(lax.shift_right_logical(code, 3), 7)
        off = lax.shift_right_logical(code, 6)
        at = dlon * PAIR + rank
        own = back_ref[dlon * SLOTS + PAIR + rank].astype(F32)
        cross = cross_ref[at].astype(F32)
        inner = inner_ref[at].astype(F32)
        value = jnp.where(off == 1, own, jnp.where(off == cross_off, cross, inner))
        value = jnp.where(land_ref[t] > 0, value, 0.0)
        flux_ref[t] = value.astype(BF16)
        wide_ref[8 * t : 8 * t + 8, :] = value
    heat = jnp.sum(jnp.sum(heat_ref[...], axis=0), axis=1, keepdims=True)
    correction = heat / points
    for j in range(3):
        cols = slice(128 * j, 128 * j + 128)
        wet = depth_ref[:, cols].astype(F32) * tile_column(land_ref, j)
        gain = jnp.where(wet > 0.0, 0.5, 0.0)
        for t in range(4):
            force = wide_ref[pl.ds(8 * j + t, 16, stride=24), :]
            if t == 0:
                force = force - correction
            out_ref[t, 0, :, cols] = top_ref[t, :, cols] + gain * force


def call(kernel, name, in_specs, out_shape, out_specs, scratch=(), limit=SMALL, **more):
    return pl.pallas_call(
        kernel,
        out_shape=out_shape,
        in_specs=in_specs,
        out_specs=out_specs,
        scratch_shapes=list(scratch),
        name=name,
        compiler_params=pltpu.CompilerParams(vmem_limit_bytes=limit),
        **more,
    )


def shape(dims, dtype):
    return jax.ShapeDtypeStruct(dims, dtype)


def shards(
    tracers,
    east_velocity,
    north_velocity,
    diffusivity,
    cross_diffusivity,
    depth_levels,
    land_mask,
    ocean_state,
    atm_state,
    exchange_coef,
    sunlight,
    mixing,
    o2a_dest,
    o2a_slot,
    a2o_source,
    a2o_tile,
):
    lats = lax.axis_size("lat")
    lons = lax.axis_size("lon")
    lat = lax.axis_index("lat")
    cross_pairs, inner_pairs = [], []
    for i in range(0, lats, 2):
        north, south = i + 1, (i + lats - 1) % lats
        inner_pairs += [(i, north), (north, i)]
        cross_pairs += [(i, south), (south, i)]
    flat = (8 * SLOTS, 8, 128)

    def turn(values):
        values = values.reshape(8, SLOTS, 8, 128)
        return lax.all_to_all(values, "lon", 0, 0, tiled=True).reshape(flat)

    tracers_l = tracers.reshape(32, 16, 384)

    outgoing, code = call(
        functools.partial(pack_kernel, lats),
        "pack",
        [HBM] * 7,
        (shape(flat, BF16), shape((48,), jnp.int32)),
        (VMEM, SMEM),
        [
            pltpu.SMEM((24,), jnp.int32),
            pltpu.SMEM((48,), jnp.int32),
            pltpu.SMEM((48,), jnp.int32),
            pltpu.VMEM((48, 8, 128), BF16),
            pltpu.VMEM((2, 32, 16, 128), F32),
            pltpu.VMEM((8, 16, 128), F32),
            pltpu.VMEM((2, 8, 16, 128), F32),
            pltpu.VMEM((16, 384), jnp.int32),
            pltpu.SemaphoreType.DMA((9,)),
        ],
        limit=60 * 1024 * 1024,
    )(o2a_dest, land_mask, ocean_state, tracers_l, east_velocity, diffusivity, depth_levels)

    source_off = (lat - a2o_source // lons + 1) % lats
    same = a2o_source[:, None] == a2o_source[None, :]
    earlier = a2o_tile[None, :] < a2o_tile[:, None]
    source_rank = jnp.sum((same & earlier).astype(jnp.int32), axis=1)
    place = source_off * 64 + (a2o_source % lons) * 8 + source_rank

    came = turn(outgoing)
    row_shape = shape((69, 8, 128), BF16)
    cross, inner = call(
        rows_kernel,
        "rows",
        [SMEM, VMEM, VMEM, VMEM, VMEM, VMEM],
        (row_shape, row_shape),
        (VMEM, VMEM),
    )(
        land_mask,
        came,
        tracers_l,
        north_velocity,
        diffusivity,
        depth_levels,
    )
    cross = lax.ppermute(cross, "lat", cross_pairs)
    inner = lax.ppermute(inner, "lat", inner_pairs)

    backward = call(
        couple_kernel,
        "couple",
        [SMEM] + [VMEM] * 7,
        shape(flat, BF16),
        VMEM,
        [pltpu.VMEM((48, 8, 128), F32)],
    )(place, came, cross, inner, atm_state, exchange_coef, sunlight, mixing)
    back = turn(backward)

    step, top, done = call(
        functools.partial(stencil_kernel, lats),
        "stencil",
        [SMEM] + [VMEM] * 9 + [SMEM, ANY],
        (shape((32, 16, 384), F32), shape((4, 16, 384), F32), shape((48,), jnp.int32)),
        (VMEM, VMEM, SMEM),
        [pltpu.VMEM((2, 56, 384), F32), pltpu.VMEM((2, 32, 384), F32), pltpu.VMEM((5, 16, 384), F32)],
        cost_estimate=pl.CostEstimate(flops=8000000, bytes_accessed=3000000, transcendentals=0),
    )(
        land_mask,
        came,
        cross,
        inner,
        tracers_l,
        east_velocity,
        north_velocity,
        diffusivity,
        cross_diffusivity,
        depth_levels,
        code,
        backward,
    )

    back_cross, back_inner, heat = call(
        functools.partial(split_kernel, lats),
        "split",
        [VMEM, ANY],
        (shape((48, 8, 128), BF16), shape((48, 8, 128), BF16), shape((lats, 1, 128), F32)),
        (VMEM, VMEM, VMEM),
    )(back, done)
    heat = lax.all_to_all(heat, "lat", 0, 0, tiled=True)
    back_cross = lax.ppermute(back_cross, "lat", cross_pairs)
    back_inner = lax.ppermute(back_inner, "lat", inner_pairs)

    points = float(48 * 128 * lats * lons)
    ocean_flux, new_tracers = call(
        functools.partial(finish_kernel, points),
        "finish",
        [SMEM, SMEM, VMEM, VMEM, VMEM, VMEM, VMEM, VMEM, ANY],
        (shape((48, 8, 128), BF16), shape((4, 8, 16, 384), F32)),
        (VMEM, pl.BlockSpec((4, 1, 16, 384), lambda i: (0, 0, 0, 0))),
        [pltpu.VMEM((416, 128), F32)],
        grid=(1,),
        input_output_aliases={8: 1},
    )(done, land_mask, back, back_cross, back_inner, heat, depth_levels, top, step.reshape(4, 8, 16, 384))
    return (new_tracers, ocean_flux)


def solution(mesh):
    return jax.shard_map(
        shards,
        mesh=mesh,
        in_specs=(
            P(None, None, "lat", "lon"),
            P(None, "lat", "lon"),
            P(None, "lat", "lon"),
            P(None, "lat", "lon"),
            P(None, "lat", "lon"),
            P("lat", "lon"),
            P(("lat", "lon")),
            P(("lat", "lon"), None, None),
            P(("lat", "lon"), None, None),
            P(("lat", "lon"), None),
            P(("lat", "lon"), None),
            P(),
            P(("lat", "lon")),
            P(("lat", "lon")),
            P(("lat", "lon")),
            P(("lat", "lon")),
        ),
        out_specs=(P(None, None, "lat", "lon"), P(("lat", "lon"), None, None)),
        check_vma=False,
    )
```

```python
import functools

import jax
import jax.numpy as jnp
from jax import lax
from jax.experimental import pallas as pl
from jax.experimental.pallas import tpu as pltpu
from jax.sharding import PartitionSpec as P

F32 = jnp.float32
BF16 = jnp.bfloat16
PAIR = 6
SLOTS = 19
LAND = 2.0**100
LAND_TEST = 2.0**90
VMEM = pl.BlockSpec(memory_space=pltpu.VMEM)
SMEM = pl.BlockSpec(memory_space=pltpu.SMEM)
ANY = pl.BlockSpec(memory_space=pl.ANY)
HBM = pl.BlockSpec(memory_space=pltpu.HBM)
SMALL = 16 * 1024 * 1024


def iota(shape, dim):
    return lax.broadcasted_iota(jnp.int32, shape, dim)


def block_of(ref, block):
    return ref[..., 128 * block : 128 * block + 128]


def tile_column(land_ref, block):
    rows = iota((16, 128), 0)
    out = jnp.zeros((16, 128), F32)
    for r in range(16):
        out = jnp.where(rows == r, land_ref[3 * r + block].astype(F32), out)
    return out


def pack_kernel(lats, dest_hbm, land_hbm, state_hbm, tracer_hbm, east_hbm, kappa_hbm, depth_hbm,
                out_ref, code_ref, count_ref, dest_ref, land_ref, state_ref, tracer_ref, east_ref,
                kappa_ref, depth_ref, sems):
    first, last = pl.ds(0, 128), pl.ds(256, 128)
    copies = [
        pltpu.make_async_copy(source, target, sems.at[n])
        for n, (source, target) in enumerate(
            (
                (dest_hbm, dest_ref),
                (land_hbm, land_ref),
                (state_hbm, state_ref),
                (depth_hbm, depth_ref),
                (tracer_hbm.at[:, :, last], tracer_ref.at[0]),
                (tracer_hbm.at[:, :, first], tracer_ref.at[1]),
                (kappa_hbm.at[:, :, last], kappa_ref.at[0]),
                (kappa_hbm.at[:, :, first], kappa_ref.at[1]),
                (east_hbm.at[:, :, last], east_ref),
            )
        )
    ]
    for copy in copies:
        copy.start()
    lat = lax.axis_index("lat")
    lon = lax.axis_index("lon")
    lons = 8
    for i in range(24):
        count_ref[i] = 0
    for copy in copies[:3]:
        copy.wait()
    for t in range(48):
        dest = dest_ref[t]
        off = lax.shift_right_logical(dest, 3) - lat + 1
        off = jnp.where(off < 0, off + lats, jnp.where(off >= lats, off - lats, off))
        dlon = lax.bitwise_and(dest, 7)
        key = off * 8 + dlon
        rank = count_ref[key]
        count_ref[key] = rank + 1
        code_ref[t] = key * 8 + rank
        value = state_ref[t].astype(F32)
        value = jnp.where(land_ref[t] > 0, value, LAND)
        out_ref[dlon * SLOTS + off * PAIR + rank] = value.astype(BF16)
    for copy in copies[3:]:
        copy.wait()
    lanes = iota((16, 128), 1)
    for side, block, lane, shift in ((0, 2, 127, 1), (1, 0, 0, lons - 1)):
        packed = jnp.zeros((16, 128), F32)
        for i in range(32):
            packed = jnp.where(lanes == i, tracer_ref[side, i][:, lane : lane + 1], packed)
        for i in range(8):
            if side == 0:
                packed = jnp.where(lanes == 32 + i, east_ref[i][:, lane : lane + 1], packed)
            packed = jnp.where(lanes == 40 + i, kappa_ref[side, i][:, lane : lane + 1], packed)
        bottom = block_of(depth_ref, block)[...].astype(F32) * tile_column(land_ref, block)
        packed = jnp.where(lanes == 48, bottom[:, lane : lane + 1], packed)
        target = lax.rem(lon + shift, lons)
        halo = jnp.where(lanes[:8] < 64, packed[:8], pltpu.roll(packed[8:], 64, 1))
        out_ref[target * SLOTS + 18] = halo.astype(BF16)


def by_parity(body, cross, inner):
    odd = lax.rem(lax.axis_index("lat"), 2)

    @pl.when(odd == 1)
    def _():
        body(cross, inner)

    @pl.when(odd == 0)
    def _():
        body(inner, cross)


def rows_kernel(land_ref, came_ref, tracer_ref, north_ref, kappa_ref, depth_ref, cross_ref, inner_ref):
    inputs = (land_ref, came_ref, tracer_ref, north_ref, kappa_ref, depth_ref)
    by_parity(functools.partial(fill_rows, *inputs), cross_ref, inner_ref)


def fill_rows(land_ref, came_ref, tracer_ref, north_ref, kappa_ref, depth_ref, up_ref, down_ref):
    lon = lax.axis_index("lon")
    west = lax.rem(lon + 7, 8)
    east = lax.rem(lon + 1, 8)
    subs = iota((8, 128), 0)
    for out_ref, first, row in ((up_ref, 12, 15), (down_ref, 0, 0)):
        for s in range(8):
            for k in range(PAIR):
                out_ref[s * PAIR + k] = came_ref[s * SLOTS + first + k]
        corners = [None] * 3
        for j, side in ((0, west), (2, east)):
            halo = came_ref[side * SLOTS + 18].astype(F32)
            corners[j] = pltpu.roll(halo, 64, 1)[7:8] if row else halo[0:1]
        for j in range(3):
            cols = slice(128 * j, 128 * j + 128)
            for k in range(4):
                out_ref[48 + 3 * k + j] = tracer_ref[8 * k : 8 * k + 8, row, cols].astype(BF16)
            if row:
                out_ref[48 + 12 + j] = north_ref[:, row, cols].astype(BF16)
            else:
                out_ref[48 + 12 + j] = jnp.zeros((8, 128), BF16)
            out_ref[48 + 15 + j] = kappa_ref[:, row, cols].astype(BF16)
            bottom = depth_ref[row : row + 1, cols].astype(F32) * land_ref[3 * row + j].astype(F32)
            last = jnp.where(subs == 0, bottom, 0.0)
            if j != 1:
                last = jnp.where(subs == 1, corners[j], last)
            out_ref[48 + 18 + j] = last.astype(BF16)


def couple_kernel(place_ref, came_ref, cross_ref, inner_ref, atm_ref, coef_ref, sun_ref, mixing_ref,
                  out_ref, got_ref):
    odd = lax.rem(lax.axis_index("lat"), 2)
    cross_off = jnp.where(odd == 1, 0, 2)
    total = jnp.zeros((8, 128), F32)
    for q in range(48):
        code = place_ref[q]
        rank = lax.bitwise_and(code, 7)
        slon = lax.bitwise_and(lax.shift_right_logical(code, 3), 7)
        off = lax.shift_right_logical(code, 6)
        at = slon * PAIR + rank
        own = came_ref[slon * SLOTS + PAIR + rank].astype(F32)
        cross = cross_ref[at].astype(F32)
        inner = inner_ref[at].astype(F32)
        value = jnp.where(off == 1, own, jnp.where(off == cross_off, cross, inner))
        got_ref[q] = value
        total = total + coef_ref[q : q + 1, :] * jnp.where(value < LAND_TEST, value, 0.0)
    weight = jnp.sum(jnp.sum(coef_ref[...], axis=0, keepdims=True), axis=1, keepdims=True)
    band_mean = jnp.sum(total, axis=1, keepdims=True) / weight
    mixing = mixing_ref[...]
    columns = [jnp.broadcast_to(mixing[:, g : g + 1], (8, 128)) for g in range(8)]
    heat = jnp.zeros((8, 128), F32)
    first = iota((8, 128), 0) == 0
    for q in range(48):
        code = place_ref[q]
        rank = lax.bitwise_and(code, 7)
        slon = lax.bitwise_and(lax.shift_right_logical(code, 3), 7)
        off = lax.shift_right_logical(code, 6)
        value = got_ref[q]
        wet = value < LAND_TEST
        drive = atm_ref[q] + band_mean - 2.0 * jnp.where(wet, value, 0.0)
        mixed = columns[0] * drive[0:1]
        for g in range(1, 8):
            mixed = mixed + columns[g] * drive[g : g + 1]
        coef = coef_ref[q : q + 1, :]
        flux = coef * mixed
        flux = flux + jnp.where(first, coef * sun_ref[q : q + 1, :], 0.0)
        rounded = flux.astype(BF16)
        out_ref[slon * SLOTS + off * PAIR + rank] = rounded
        heat = heat + jnp.where(wet, rounded.astype(F32), 0.0)
    subs = iota((8, 128), 0)
    row = jnp.broadcast_to(heat[0:1], (8, 128))
    one = row.astype(BF16).astype(F32)
    two = (row - one).astype(BF16).astype(F32)
    three = row - one - two
    parts = jnp.where(subs == 0, one, jnp.where(subs == 1, two, jnp.where(subs == 2, three, 0.0)))
    for s in range(8):
        out_ref[s * SLOTS + 18] = parts.astype(BF16)


def split_kernel(lats, back_ref, done_ref, cross_ref, inner_ref, heat_ref):
    odd = lax.rem(lax.axis_index("lat"), 2)
    cross_at = jnp.where(odd == 1, 0, 12)
    inner_at = 12 - cross_at
    heat = jnp.zeros((8, 128), F32)
    for s in range(8):
        heat = heat + back_ref[s * SLOTS + 18].astype(F32)
        for k in range(PAIR):
            cross_ref[s * PAIR + k] = back_ref[s * SLOTS + cross_at + k]
            inner_ref[s * PAIR + k] = back_ref[s * SLOTS + inner_at + k]
    row = jnp.sum(heat, axis=0, keepdims=True)
    heat_ref[...] = jnp.broadcast_to(row[None], (lats, 1, 128))


def stencil_kernel(lats, land_ref, came_ref, cross_halo_ref, inner_halo_ref, tracer_ref, east_ref, north_ref,
                   kappa_ref, cross_ref, depth_ref, code_ref, after_ref, out_ref, top_ref, done_ref, rows_ref,
                   diag_ref, bottom_ref):
    lat = lax.axis_index("lat")
    lon = lax.axis_index("lon")
    west = lax.rem(lon + 7, 8)
    east = lax.rem(lon + 1, 8)
    full = (16, 384)
    lanes = iota(full, 1)
    subs = iota(full, 0)
    at_west, at_east = lanes == 0, lanes == 383
    at_south, at_north = subs == 0, subs == 15
    small = iota((8, 384), 1)
    lane8, sub8 = iota((8, 128), 1), iota((8, 128), 0)

    def columns_of(side):
        halo = came_ref[side * SLOTS + 18].astype(F32)
        return jnp.concatenate([halo, pltpu.roll(halo, 64, 1)], axis=0)

    def from_west(v, column):
        return jnp.where(at_west, column, pltpu.roll(v, 1, 1))

    def from_east(v, column):
        return jnp.where(at_east, column, pltpu.roll(v, 383, 1))

    def from_south(v, row):
        return jnp.where(at_south, row, pltpu.roll(v, 1, 0))

    def from_north(v, row):
        return jnp.where(at_north, row, pltpu.roll(v, 15, 0))

    col_west, col_east = columns_of(west), columns_of(east)

    def unpack_rows(high_ref, low_ref):
        for side, ref in enumerate((low_ref, high_ref)):
            inside = jnp.where(lat == (0, lats - 1)[side], 0.0, 1.0)
            for k in range(7):
                for j in range(3):
                    tile = ref[48 + 3 * k + j].astype(F32)
                    if k == 6:
                        tile = jnp.where(sub8 == 0, tile * inside, tile)
                    rows_ref[side, 8 * k : 8 * k + 8, 128 * j : 128 * j + 128] = tile

    by_parity(unpack_rows, cross_halo_ref, inner_halo_ref)
    for j in range(3):
        cols = slice(128 * j, 128 * j + 128)
        bottom_ref[0, :, cols] = depth_ref[:, cols].astype(F32) * tile_column(land_ref, j)
    bottom = bottom_ref[0]
    bottom_ref[1] = from_east(bottom, col_east[:, 48:49])
    bottom_ref[2] = from_west(bottom, col_west[:, 48:49])
    bottom_ref[3] = from_north(bottom, rows_ref[1, 48:49, :])
    bottom_ref[4] = from_south(bottom, rows_ref[0, 48:49, :])

    level8 = iota((8, 384), 0).astype(F32)
    for side in range(2):
        inside = jnp.where(lat == (0, lats - 1)[side], 0.0, 1.0)
        corner_w = jnp.broadcast_to(rows_ref[side, 49:50, 0:128], (8, 128))
        corner_e = jnp.broadcast_to(rows_ref[side, 49:50, 256:384], (8, 128))
        edge = jnp.broadcast_to(rows_ref[side, 48:49, :], (8, 384))
        edge_e = jnp.where(small == 383, corner_e[:, 48:49] * inside, pltpu.roll(edge, 383, 1))
        edge_w = jnp.where(small == 0, corner_w[:, 48:49] * inside, pltpu.roll(edge, 1, 1))
        for k in range(4):
            value = rows_ref[side, 8 * k : 8 * k + 8, :]
            pick = lane8 == sub8 + 8 * k
            value_e = jnp.sum(jnp.where(pick, corner_e, 0.0), axis=1, keepdims=True)
            value_w = jnp.sum(jnp.where(pick, corner_w, 0.0), axis=1, keepdims=True)
            value_e = jnp.where(small == 383, value_e, pltpu.roll(value, 383, 1))
            value_w = jnp.where(small == 0, value_w, pltpu.roll(value, 1, 1))
            diag_ref[side, 8 * k : 8 * k + 8, :] = jnp.where(level8 < edge_e, value_e, 0.0) - jnp.where(
                level8 < edge_w, value_w, 0.0
            )

    def level_step(l, carry):
        lf = l.astype(F32)
        cw = pltpu.roll(col_west, lax.rem(128 - l, 128), 1)
        ce = pltpu.roll(col_east, lax.rem(128 - l, 128), 1)
        masks = [(lf < bottom_ref[i]).astype(F32) for i in range(5)]
        mask, mask_e, mask_w, mask_n, mask_s = masks
        kappa = kappa_ref[l]
        velocity = east_ref[l]
        kap = 0.5 * (kappa + from_east(kappa, ce[:, 40:41]))
        open_face = mask * mask_e
        out_e = open_face * (jnp.maximum(velocity, 0.0) + kap)
        in_e = open_face * (kap - jnp.minimum(velocity, 0.0))
        velocity = from_west(velocity, cw[:, 32:33])
        kap = 0.5 * (kappa + from_west(kappa, cw[:, 40:41]))
        open_face = mask * mask_w
        in_w = open_face * (jnp.maximum(velocity, 0.0) + kap)
        out_w = open_face * (kap - jnp.minimum(velocity, 0.0))
        velocity = north_ref[l]
        kap = 0.5 * (kappa + from_north(kappa, rows_ref[1, pl.ds(40 + l, 1), :]))
        open_face = mask * mask_n
        out_n = open_face * (jnp.maximum(velocity, 0.0) + kap)
        in_n = open_face * (kap - jnp.minimum(velocity, 0.0))
        velocity = from_south(velocity, rows_ref[0, pl.ds(32 + l, 1), :])
        kap = 0.5 * (kappa + from_south(kappa, rows_ref[0, pl.ds(40 + l, 1), :]))
        open_face = mask * mask_s
        in_s = open_face * (jnp.maximum(velocity, 0.0) + kap)
        out_s = open_face * (kap - jnp.minimum(velocity, 0.0))
        keep = 1.0 - (out_e + out_w + out_n + out_s)
        cross = cross_ref[l] * mask
        for t in range(4):
            i = 8 * t + l
            c = tracer_ref[i]
            c_e = from_east(c, ce[:, 8 * t : 8 * t + 1])
            c_w = from_west(c, cw[:, 8 * t : 8 * t + 1])
            c_n = from_north(c, rows_ref[1, pl.ds(i, 1), :])
            c_s = from_south(c, rows_ref[0, pl.ds(i, 1), :])
            diag = mask_e * c_e - mask_w * c_w
            diag_n = from_north(diag, diag_ref[1, pl.ds(i, 1), :])
            diag_s = from_south(diag, diag_ref[0, pl.ds(i, 1), :])
            out_ref[i] = (
                keep * c + in_e * c_e + in_w * c_w + in_n * c_n + in_s * c_s + cross * (diag_n - diag_s)
            )
        return carry

    lax.fori_loop(0, 8, level_step, 0)
    for t in range(4):
        top_ref[t] = out_ref[8 * t]
    for t in range(48):
        done_ref[t] = code_ref[t]


def finish_kernel(points, code_ref, land_ref, back_ref, cross_ref, inner_ref, heat_ref, depth_ref,
                  top_ref, step_hbm, flux_ref, out_ref, wide_ref):
    odd = lax.rem(lax.axis_index("lat"), 2)
    cross_off = jnp.where(odd == 1, 2, 0)
    for t in range(48):
        code = code_ref[t]
        rank = lax.bitwise_and(code, 7)
        dlon = lax.bitwise_and(lax.shift_right_logical(code, 3), 7)
        off = lax.shift_right_logical(code, 6)
        at = dlon * PAIR + rank
        own = back_ref[dlon * SLOTS + PAIR + rank].astype(F32)
        cross = cross_ref[at].astype(F32)
        inner = inner_ref[at].astype(F32)
        value = jnp.where(off == 1, own, jnp.where(off == cross_off, cross, inner))
        value = jnp.where(land_ref[t] > 0, value, 0.0)
        flux_ref[t] = value.astype(BF16)
        wide_ref[8 * t : 8 * t + 8, :] = value
    heat = jnp.sum(jnp.sum(heat_ref[...], axis=0), axis=1, keepdims=True)
    correction = heat / points
    for j in range(3):
        cols = slice(128 * j, 128 * j + 128)
        wet = depth_ref[:, cols].astype(F32) * tile_column(land_ref, j)
        gain = jnp.where(wet > 0.0, 0.5, 0.0)
        for t in range(4):
            force = wide_ref[pl.ds(8 * j + t, 16, stride=24), :]
            if t == 0:
                force = force - correction
            out_ref[t, 0, :, cols] = top_ref[t, :, cols] + gain * force


def call(kernel, name, in_specs, out_shape, out_specs, scratch=(), limit=SMALL, **more):
    return pl.pallas_call(
        kernel,
        out_shape=out_shape,
        in_specs=in_specs,
        out_specs=out_specs,
        scratch_shapes=list(scratch),
        name=name,
        compiler_params=pltpu.CompilerParams(vmem_limit_bytes=limit),
        **more,
    )


def shape(dims, dtype):
    return jax.ShapeDtypeStruct(dims, dtype)


def shards(
    tracers,
    east_velocity,
    north_velocity,
    diffusivity,
    cross_diffusivity,
    depth_levels,
    land_mask,
    ocean_state,
    atm_state,
    exchange_coef,
    sunlight,
    mixing,
    o2a_dest,
    o2a_slot,
    a2o_source,
    a2o_tile,
):
    lats = lax.axis_size("lat")
    lons = lax.axis_size("lon")
    lat = lax.axis_index("lat")
    cross_pairs, inner_pairs = [], []
    for i in range(0, lats, 2):
        north, south = i + 1, (i + lats - 1) % lats
        inner_pairs += [(i, north), (north, i)]
        cross_pairs += [(i, south), (south, i)]
    flat = (8 * SLOTS, 8, 128)

    def turn(values):
        values = values.reshape(8, SLOTS, 8, 128)
        return lax.all_to_all(values, "lon", 0, 0, tiled=True).reshape(flat)

    tracers_l = tracers.reshape(32, 16, 384)

    outgoing, code = call(
        functools.partial(pack_kernel, lats),
        "pack",
        [HBM] * 7,
        (shape(flat, BF16), shape((48,), jnp.int32)),
        (VMEM, SMEM),
        [
            pltpu.SMEM((24,), jnp.int32),
            pltpu.SMEM((48,), jnp.int32),
            pltpu.SMEM((48,), jnp.int32),
            pltpu.VMEM((48, 8, 128), BF16),
            pltpu.VMEM((2, 32, 16, 128), F32),
            pltpu.VMEM((8, 16, 128), F32),
            pltpu.VMEM((2, 8, 16, 128), F32),
            pltpu.VMEM((16, 384), jnp.int32),
            pltpu.SemaphoreType.DMA((9,)),
        ],
        limit=60 * 1024 * 1024,
    )(o2a_dest, land_mask, ocean_state, tracers_l, east_velocity, diffusivity, depth_levels)

    source_off = (lat - a2o_source // lons + 1) % lats
    same = a2o_source[:, None] == a2o_source[None, :]
    earlier = a2o_tile[None, :] < a2o_tile[:, None]
    source_rank = jnp.sum((same & earlier).astype(jnp.int32), axis=1)
    place = source_off * 64 + (a2o_source % lons) * 8 + source_rank

    came = turn(outgoing)
    row_shape = shape((69, 8, 128), BF16)
    cross, inner = call(
        rows_kernel,
        "rows",
        [SMEM, VMEM, VMEM, VMEM, VMEM, VMEM],
        (row_shape, row_shape),
        (VMEM, VMEM),
    )(
        land_mask,
        came,
        tracers_l,
        north_velocity,
        diffusivity,
        depth_levels,
    )
    cross = lax.ppermute(cross, "lat", cross_pairs)
    inner = lax.ppermute(inner, "lat", inner_pairs)

    backward = call(
        couple_kernel,
        "couple",
        [SMEM] + [VMEM] * 7,
        shape(flat, BF16),
        VMEM,
        [pltpu.VMEM((48, 8, 128), F32)],
    )(place, came, cross, inner, atm_state, exchange_coef, sunlight, mixing)
    back = turn(backward)

    step, top, done = call(
        functools.partial(stencil_kernel, lats),
        "stencil",
        [SMEM] + [VMEM] * 9 + [SMEM, ANY],
        (shape((32, 16, 384), F32), shape((4, 16, 384), F32), shape((48,), jnp.int32)),
        (VMEM, VMEM, SMEM),
        [pltpu.VMEM((2, 56, 384), F32), pltpu.VMEM((2, 32, 384), F32), pltpu.VMEM((5, 16, 384), F32)],
        cost_estimate=pl.CostEstimate(flops=8000000, bytes_accessed=3000000, transcendentals=0),
    )(
        land_mask,
        came,
        cross,
        inner,
        tracers_l,
        east_velocity,
        north_velocity,
        diffusivity,
        cross_diffusivity,
        depth_levels,
        code,
        backward,
    )

    back_cross, back_inner, heat = call(
        functools.partial(split_kernel, lats),
        "split",
        [VMEM, ANY],
        (shape((48, 8, 128), BF16), shape((48, 8, 128), BF16), shape((lats, 1, 128), F32)),
        (VMEM, VMEM, VMEM),
    )(back, done)
    heat = lax.all_to_all(heat, "lat", 0, 0, tiled=True)
    back_cross = lax.ppermute(back_cross, "lat", cross_pairs)
    back_inner = lax.ppermute(back_inner, "lat", inner_pairs)

    points = float(48 * 128 * lats * lons)
    ocean_flux, new_tracers = call(
        functools.partial(finish_kernel, points),
        "finish",
        [SMEM, SMEM, VMEM, VMEM, VMEM, VMEM, VMEM, VMEM, ANY],
        (shape((48, 8, 128), BF16), shape((4, 8, 16, 384), F32)),
        (VMEM, pl.BlockSpec((4, 1, 16, 384), lambda i: (0, 0, 0, 0))),
        [pltpu.VMEM((416, 128), F32)],
        grid=(1,),
        input_output_aliases={8: 1},
    )(done, land_mask, back, back_cross, back_inner, heat, depth_levels, top, step.reshape(4, 8, 16, 384))
    return (new_tracers, ocean_flux)


def solution(mesh):
    return jax.shard_map(
        shards,
        mesh=mesh,
        in_specs=(
            P(None, None, "lat", "lon"),
            P(None, "lat", "lon"),
            P(None, "lat", "lon"),
            P(None, "lat", "lon"),
            P(None, "lat", "lon"),
            P("lat", "lon"),
            P(("lat", "lon")),
            P(("lat", "lon"), None, None),
            P(("lat", "lon"), None, None),
            P(("lat", "lon"), None),
            P(("lat", "lon"), None),
            P(),
            P(("lat", "lon")),
            P(("lat", "lon")),
            P(("lat", "lon")),
            P(("lat", "lon")),
        ),
        out_specs=(P(None, None, "lat", "lon"), P(("lat", "lon"), None, None)),
        check_vma=False,
    )
```

```python
import functools

import jax
import jax.numpy as jnp
from jax import lax
from jax.experimental import pallas as pl
from jax.experimental.pallas import tpu as pltpu
from jax.sharding import PartitionSpec as P

F32 = jnp.float32
BF16 = jnp.bfloat16
PAIR = 6
SLOTS = 20
LAND = 2.0**100
LAND_TEST = 2.0**90
VMEM = pl.BlockSpec(memory_space=pltpu.VMEM)
SMEM = pl.BlockSpec(memory_space=pltpu.SMEM)
ANY = pl.BlockSpec(memory_space=pl.ANY)
HBM = pl.BlockSpec(memory_space=pltpu.HBM)
SMALL = 16 * 1024 * 1024


def iota(shape, dim):
    return lax.broadcasted_iota(jnp.int32, shape, dim)


def block_of(ref, block):
    return ref[..., 128 * block : 128 * block + 128]


def tile_column(land_ref, block):
    rows = iota((16, 128), 0)
    out = jnp.zeros((16, 128), F32)
    for r in range(16):
        out = jnp.where(rows == r, land_ref[3 * r + block].astype(F32), out)
    return out


def pack_kernel(lats, dest_hbm, land_hbm, state_hbm, tracer_hbm, east_hbm, kappa_hbm, depth_hbm,
                out_ref, code_ref, count_ref, dest_ref, land_ref, state_ref, tracer_ref, east_ref,
                kappa_ref, depth_ref, sems):
    first, last = pl.ds(0, 128), pl.ds(256, 128)
    copies = [
        pltpu.make_async_copy(source, target, sems.at[n])
        for n, (source, target) in enumerate(
            (
                (dest_hbm, dest_ref),
                (land_hbm, land_ref),
                (state_hbm, state_ref),
                (depth_hbm, depth_ref),
                (tracer_hbm.at[:, :, last], tracer_ref.at[0]),
                (tracer_hbm.at[:, :, first], tracer_ref.at[1]),
                (kappa_hbm.at[:, :, last], kappa_ref.at[0]),
                (kappa_hbm.at[:, :, first], kappa_ref.at[1]),
                (east_hbm.at[:, :, last], east_ref),
            )
        )
    ]
    for copy in copies:
        copy.start()
    lat = lax.axis_index("lat")
    lon = lax.axis_index("lon")
    lons = 8
    for i in range(24):
        count_ref[i] = 0
    for copy in copies[:3]:
        copy.wait()
    for t in range(48):
        dest = dest_ref[t]
        off = lax.shift_right_logical(dest, 3) - lat + 1
        off = jnp.where(off < 0, off + lats, jnp.where(off >= lats, off - lats, off))
        dlon = lax.bitwise_and(dest, 7)
        key = off * 8 + dlon
        rank = count_ref[key]
        count_ref[key] = rank + 1
        code_ref[t] = key * 8 + rank
        value = state_ref[t].astype(F32)
        value = jnp.where(land_ref[t] > 0, value, LAND)
        out_ref[dlon * SLOTS + off * PAIR + rank] = value.astype(BF16)
    for copy in copies[3:]:
        copy.wait()
    lanes = iota((16, 128), 1)
    for side, block, lane, shift in ((0, 2, 127, 1), (1, 0, 0, lons - 1)):
        packed = jnp.zeros((16, 128), F32)
        for i in range(32):
            packed = jnp.where(lanes == i, tracer_ref[side, i][:, lane : lane + 1], packed)
        for i in range(8):
            if side == 0:
                packed = jnp.where(lanes == 32 + i, east_ref[i][:, lane : lane + 1], packed)
            packed = jnp.where(lanes == 40 + i, kappa_ref[side, i][:, lane : lane + 1], packed)
        bottom = block_of(depth_ref, block)[...].astype(F32) * tile_column(land_ref, block)
        packed = jnp.where(lanes == 48, bottom[:, lane : lane + 1], packed)
        target = lax.rem(lon + shift, lons)
        out_ref[target * SLOTS + 18] = packed[:8].astype(BF16)
        out_ref[target * SLOTS + 19] = packed[8:].astype(BF16)


def by_parity(body, cross, inner):
    odd = lax.rem(lax.axis_index("lat"), 2)

    @pl.when(odd == 1)
    def _():
        body(cross, inner)

    @pl.when(odd == 0)
    def _():
        body(inner, cross)


def rows_kernel(land_ref, came_ref, tracer_ref, north_ref, kappa_ref, depth_ref, cross_ref, inner_ref):
    inputs = (land_ref, came_ref, tracer_ref, north_ref, kappa_ref, depth_ref)
    by_parity(functools.partial(fill_rows, *inputs), cross_ref, inner_ref)


def fill_rows(land_ref, came_ref, tracer_ref, north_ref, kappa_ref, depth_ref, up_ref, down_ref):
    lon = lax.axis_index("lon")
    west = lax.rem(lon + 7, 8)
    east = lax.rem(lon + 1, 8)
    subs = iota((8, 128), 0)
    for out_ref, first, row in ((up_ref, 12, 15), (down_ref, 0, 0)):
        for s in range(8):
            for k in range(PAIR):
                out_ref[s * PAIR + k] = came_ref[s * SLOTS + first + k]
        half, sub = (19, 7) if row else (18, 0)
        corners = (
            came_ref[west * SLOTS + half].astype(F32)[sub : sub + 1],
            None,
            came_ref[east * SLOTS + half].astype(F32)[sub : sub + 1],
        )
        for j in range(3):
            cols = slice(128 * j, 128 * j + 128)
            for k in range(4):
                out_ref[48 + 3 * k + j] = tracer_ref[8 * k : 8 * k + 8, row, cols].astype(BF16)
            if row:
                out_ref[48 + 12 + j] = north_ref[:, row, cols].astype(BF16)
            else:
                out_ref[48 + 12 + j] = jnp.zeros((8, 128), BF16)
            out_ref[48 + 15 + j] = kappa_ref[:, row, cols].astype(BF16)
            bottom = depth_ref[row : row + 1, cols].astype(F32) * land_ref[3 * row + j].astype(F32)
            last = jnp.where(subs == 0, bottom, 0.0)
            if j != 1:
                last = jnp.where(subs == 1, corners[j], last)
            out_ref[48 + 18 + j] = last.astype(BF16)


def couple_kernel(place_ref, came_ref, inner_ref, cross_ref, atm_ref, coef_ref, sun_ref, mixing_ref,
                  out_ref, got_ref):
    odd = lax.rem(lax.axis_index("lat"), 2)
    cross_off = jnp.where(odd == 1, 0, 2)
    total = jnp.zeros((8, 128), F32)
    for q in range(48):
        code = place_ref[q]
        rank = lax.bitwise_and(code, 7)
        slon = lax.bitwise_and(lax.shift_right_logical(code, 3), 7)
        off = lax.shift_right_logical(code, 6)
        at = slon * PAIR + rank
        own = came_ref[slon * SLOTS + PAIR + rank].astype(F32)
        cross = cross_ref[at].astype(F32)
        inner = inner_ref[at].astype(F32)
        value = jnp.where(off == 1, own, jnp.where(off == cross_off, cross, inner))
        got_ref[q] = value
        total = total + coef_ref[q : q + 1, :] * jnp.where(value < LAND_TEST, value, 0.0)
    weight = jnp.sum(jnp.sum(coef_ref[...], axis=0, keepdims=True), axis=1, keepdims=True)
    band_mean = jnp.sum(total, axis=1, keepdims=True) / weight
    mixing = mixing_ref[...]
    columns = [jnp.broadcast_to(mixing[:, g : g + 1], (8, 128)) for g in range(8)]
    heat = jnp.zeros((8, 128), F32)
    first = iota((8, 128), 0) == 0
    for q in range(48):
        code = place_ref[q]
        rank = lax.bitwise_and(code, 7)
        slon = lax.bitwise_and(lax.shift_right_logical(code, 3), 7)
        off = lax.shift_right_logical(code, 6)
        value = got_ref[q]
        wet = value < LAND_TEST
        drive = atm_ref[q] + band_mean - 2.0 * jnp.where(wet, value, 0.0)
        mixed = columns[0] * drive[0:1]
        for g in range(1, 8):
            mixed = mixed + columns[g] * drive[g : g + 1]
        coef = coef_ref[q : q + 1, :]
        flux = coef * mixed
        flux = flux + jnp.where(first, coef * sun_ref[q : q + 1, :], 0.0)
        rounded = flux.astype(BF16)
        out_ref[slon * SLOTS + off * PAIR + rank] = rounded
        heat = heat + jnp.where(wet, rounded.astype(F32), 0.0)
    subs = iota((8, 128), 0)
    row = jnp.broadcast_to(heat[0:1], (8, 128))
    one = row.astype(BF16).astype(F32)
    two = (row - one).astype(BF16).astype(F32)
    three = row - one - two
    parts = jnp.where(subs == 0, one, jnp.where(subs == 1, two, jnp.where(subs == 2, three, 0.0)))
    for s in range(8):
        out_ref[s * SLOTS + 18] = parts.astype(BF16)


def split_kernel(lats, back_ref, done_ref, cross_ref, inner_ref, heat_ref):
    odd = lax.rem(lax.axis_index("lat"), 2)
    cross_at = jnp.where(odd == 1, 0, 12)
    inner_at = 12 - cross_at
    heat = jnp.zeros((8, 128), F32)
    for s in range(8):
        heat = heat + back_ref[s * SLOTS + 18].astype(F32)
        for k in range(PAIR):
            cross_ref[s * PAIR + k] = back_ref[s * SLOTS + cross_at + k]
            inner_ref[s * PAIR + k] = back_ref[s * SLOTS + inner_at + k]
    row = jnp.sum(heat, axis=0, keepdims=True)
    heat_ref[...] = jnp.broadcast_to(row[None], (lats, 1, 128))


def stencil_kernel(lats, land_ref, came_ref, inner_halo_ref, cross_halo_ref, tracer_ref, east_ref, north_ref,
                   kappa_ref, cross_ref, depth_ref, code_ref, after_ref, out_ref, top_ref, done_ref, rows_ref,
                   diag_ref, bottom_ref):
    lat = lax.axis_index("lat")
    lon = lax.axis_index("lon")
    west = lax.rem(lon + 7, 8)
    east = lax.rem(lon + 1, 8)
    full = (16, 384)
    lanes = iota(full, 1)
    subs = iota(full, 0)
    at_west, at_east = lanes == 0, lanes == 383
    at_south, at_north = subs == 0, subs == 15
    small = iota((8, 384), 1)
    lane8, sub8 = iota((8, 128), 1), iota((8, 128), 0)

    def columns_of(side):
        return jnp.concatenate(
            [came_ref[side * SLOTS + 18].astype(F32), came_ref[side * SLOTS + 19].astype(F32)], axis=0
        )

    def from_west(v, column):
        return jnp.where(at_west, column, pltpu.roll(v, 1, 1))

    def from_east(v, column):
        return jnp.where(at_east, column, pltpu.roll(v, 383, 1))

    def from_south(v, row):
        return jnp.where(at_south, row, pltpu.roll(v, 1, 0))

    def from_north(v, row):
        return jnp.where(at_north, row, pltpu.roll(v, 15, 0))

    col_west, col_east = columns_of(west), columns_of(east)

    def unpack_rows(high_ref, low_ref):
        for side, ref in enumerate((low_ref, high_ref)):
            inside = jnp.where(lat == (0, lats - 1)[side], 0.0, 1.0)
            for k in range(7):
                for j in range(3):
                    tile = ref[48 + 3 * k + j].astype(F32)
                    if k == 6:
                        tile = jnp.where(sub8 == 0, tile * inside, tile)
                    rows_ref[side, 8 * k : 8 * k + 8, 128 * j : 128 * j + 128] = tile

    by_parity(unpack_rows, cross_halo_ref, inner_halo_ref)
    for j in range(3):
        cols = slice(128 * j, 128 * j + 128)
        bottom_ref[0, :, cols] = depth_ref[:, cols].astype(F32) * tile_column(land_ref, j)
    bottom = bottom_ref[0]
    bottom_ref[1] = from_east(bottom, col_east[:, 48:49])
    bottom_ref[2] = from_west(bottom, col_west[:, 48:49])
    bottom_ref[3] = from_north(bottom, rows_ref[1, 48:49, :])
    bottom_ref[4] = from_south(bottom, rows_ref[0, 48:49, :])

    level8 = iota((8, 384), 0).astype(F32)
    for side in range(2):
        inside = jnp.where(lat == (0, lats - 1)[side], 0.0, 1.0)
        corner_w = jnp.broadcast_to(rows_ref[side, 49:50, 0:128], (8, 128))
        corner_e = jnp.broadcast_to(rows_ref[side, 49:50, 256:384], (8, 128))
        edge = jnp.broadcast_to(rows_ref[side, 48:49, :], (8, 384))
        edge_e = jnp.where(small == 383, corner_e[:, 48:49] * inside, pltpu.roll(edge, 383, 1))
        edge_w = jnp.where(small == 0, corner_w[:, 48:49] * inside, pltpu.roll(edge, 1, 1))
        for k in range(4):
            value = rows_ref[side, 8 * k : 8 * k + 8, :]
            pick = lane8 == sub8 + 8 * k
            value_e = jnp.sum(jnp.where(pick, corner_e, 0.0), axis=1, keepdims=True)
            value_w = jnp.sum(jnp.where(pick, corner_w, 0.0), axis=1, keepdims=True)
            value_e = jnp.where(small == 383, value_e, pltpu.roll(value, 383, 1))
            value_w = jnp.where(small == 0, value_w, pltpu.roll(value, 1, 1))
            diag_ref[side, 8 * k : 8 * k + 8, :] = jnp.where(level8 < edge_e, value_e, 0.0) - jnp.where(
                level8 < edge_w, value_w, 0.0
            )

    def level_step(l, carry):
        lf = l.astype(F32)
        cw = pltpu.roll(col_west, lax.rem(128 - l, 128), 1)
        ce = pltpu.roll(col_east, lax.rem(128 - l, 128), 1)
        masks = [(lf < bottom_ref[i]).astype(F32) for i in range(5)]
        mask, mask_e, mask_w, mask_n, mask_s = masks
        kappa = kappa_ref[l]
        velocity = east_ref[l]
        kap = 0.5 * (kappa + from_east(kappa, ce[:, 40:41]))
        open_face = mask * mask_e
        out_e = open_face * (jnp.maximum(velocity, 0.0) + kap)
        in_e = open_face * (kap - jnp.minimum(velocity, 0.0))
        velocity = from_west(velocity, cw[:, 32:33])
        kap = 0.5 * (kappa + from_west(kappa, cw[:, 40:41]))
        open_face = mask * mask_w
        in_w = open_face * (jnp.maximum(velocity, 0.0) + kap)
        out_w = open_face * (kap - jnp.minimum(velocity, 0.0))
        velocity = north_ref[l]
        kap = 0.5 * (kappa + from_north(kappa, rows_ref[1, pl.ds(40 + l, 1), :]))
        open_face = mask * mask_n
        out_n = open_face * (jnp.maximum(velocity, 0.0) + kap)
        in_n = open_face * (kap - jnp.minimum(velocity, 0.0))
        velocity = from_south(velocity, rows_ref[0, pl.ds(32 + l, 1), :])
        kap = 0.5 * (kappa + from_south(kappa, rows_ref[0, pl.ds(40 + l, 1), :]))
        open_face = mask * mask_s
        in_s = open_face * (jnp.maximum(velocity, 0.0) + kap)
        out_s = open_face * (kap - jnp.minimum(velocity, 0.0))
        keep = 1.0 - (out_e + out_w + out_n + out_s)
        cross = cross_ref[l] * mask
        for t in range(4):
            i = 8 * t + l
            c = tracer_ref[i]
            c_e = from_east(c, ce[:, 8 * t : 8 * t + 1])
            c_w = from_west(c, cw[:, 8 * t : 8 * t + 1])
            c_n = from_north(c, rows_ref[1, pl.ds(i, 1), :])
            c_s = from_south(c, rows_ref[0, pl.ds(i, 1), :])
            diag = mask_e * c_e - mask_w * c_w
            diag_n = from_north(diag, diag_ref[1, pl.ds(i, 1), :])
            diag_s = from_south(diag, diag_ref[0, pl.ds(i, 1), :])
            out_ref[i] = (
                keep * c + in_e * c_e + in_w * c_w + in_n * c_n + in_s * c_s + cross * (diag_n - diag_s)
            )
        return carry

    lax.fori_loop(0, 8, level_step, 0)
    for t in range(4):
        top_ref[t] = out_ref[8 * t]
    for t in range(48):
        done_ref[t] = code_ref[t]


def finish_kernel(points, code_ref, land_ref, back_ref, cross_ref, inner_ref, heat_ref, depth_ref,
                  top_ref, step_hbm, flux_ref, out_ref, wide_ref):
    odd = lax.rem(lax.axis_index("lat"), 2)
    cross_off = jnp.where(odd == 1, 2, 0)
    for t in range(48):
        code = code_ref[t]
        rank = lax.bitwise_and(code, 7)
        dlon = lax.bitwise_and(lax.shift_right_logical(code, 3), 7)
        off = lax.shift_right_logical(code, 6)
        at = dlon * PAIR + rank
        own = back_ref[dlon * SLOTS + PAIR + rank].astype(F32)
        cross = cross_ref[at].astype(F32)
        inner = inner_ref[at].astype(F32)
        value = jnp.where(off == 1, own, jnp.where(off == cross_off, cross, inner))
        value = jnp.where(land_ref[t] > 0, value, 0.0)
        flux_ref[t] = value.astype(BF16)
        wide_ref[8 * t : 8 * t + 8, :] = value
    heat = jnp.sum(jnp.sum(heat_ref[...], axis=0), axis=1, keepdims=True)
    correction = heat / points
    for j in range(3):
        cols = slice(128 * j, 128 * j + 128)
        wet = depth_ref[:, cols].astype(F32) * tile_column(land_ref, j)
        gain = jnp.where(wet > 0.0, 0.5, 0.0)
        for t in range(4):
            force = wide_ref[pl.ds(8 * j + t, 16, stride=24), :]
            if t == 0:
                force = force - correction
            out_ref[t, 0, :, cols] = top_ref[t, :, cols] + gain * force


def call(kernel, name, in_specs, out_shape, out_specs, scratch=(), limit=SMALL, **more):
    return pl.pallas_call(
        kernel,
        out_shape=out_shape,
        in_specs=in_specs,
        out_specs=out_specs,
        scratch_shapes=list(scratch),
        name=name,
        compiler_params=pltpu.CompilerParams(vmem_limit_bytes=limit),
        **more,
    )


def shape(dims, dtype):
    return jax.ShapeDtypeStruct(dims, dtype)


def shards(
    tracers,
    east_velocity,
    north_velocity,
    diffusivity,
    cross_diffusivity,
    depth_levels,
    land_mask,
    ocean_state,
    atm_state,
    exchange_coef,
    sunlight,
    mixing,
    o2a_dest,
    o2a_slot,
    a2o_source,
    a2o_tile,
):
    lats = lax.axis_size("lat")
    lons = lax.axis_size("lon")
    lat = lax.axis_index("lat")
    cross_pairs, inner_pairs = [], []
    for i in range(0, lats, 2):
        north, south = i + 1, (i + lats - 1) % lats
        inner_pairs += [(i, north), (north, i)]
        cross_pairs += [(i, south), (south, i)]
    flat = (8 * SLOTS, 8, 128)

    def turn(values):
        values = values.reshape(8, SLOTS, 8, 128)
        return lax.all_to_all(values, "lon", 0, 0, tiled=True).reshape(flat)

    tracers_l = tracers.reshape(32, 16, 384)

    outgoing, code = call(
        functools.partial(pack_kernel, lats),
        "pack",
        [HBM] * 7,
        (shape(flat, BF16), shape((48,), jnp.int32)),
        (VMEM, SMEM),
        [
            pltpu.SMEM((24,), jnp.int32),
            pltpu.SMEM((48,), jnp.int32),
            pltpu.SMEM((48,), jnp.int32),
            pltpu.VMEM((48, 8, 128), BF16),
            pltpu.VMEM((2, 32, 16, 128), F32),
            pltpu.VMEM((8, 16, 128), F32),
            pltpu.VMEM((2, 8, 16, 128), F32),
            pltpu.VMEM((16, 384), jnp.int32),
            pltpu.SemaphoreType.DMA((9,)),
        ],
        limit=60 * 1024 * 1024,
    )(o2a_dest, land_mask, ocean_state, tracers_l, east_velocity, diffusivity, depth_levels)

    source_off = (lat - a2o_source // lons + 1) % lats
    same = a2o_source[:, None] == a2o_source[None, :]
    earlier = a2o_tile[None, :] < a2o_tile[:, None]
    source_rank = jnp.sum((same & earlier).astype(jnp.int32), axis=1)
    place = source_off * 64 + (a2o_source % lons) * 8 + source_rank

    came = turn(outgoing)
    row_shape = shape((69, 8, 128), BF16)
    cross, inner = call(
        rows_kernel,
        "rows",
        [SMEM, VMEM, VMEM, VMEM, VMEM, VMEM],
        (row_shape, row_shape),
        (VMEM, VMEM),
    )(
        land_mask,
        came,
        tracers_l,
        north_velocity,
        diffusivity,
        depth_levels,
    )
    inner = lax.ppermute(inner, "lat", inner_pairs)
    cross = lax.ppermute(cross, "lat", cross_pairs)

    backward = call(
        couple_kernel,
        "couple",
        [SMEM] + [VMEM] * 7,
        shape(flat, BF16),
        VMEM,
        [pltpu.VMEM((48, 8, 128), F32)],
    )(place, came, inner, cross, atm_state, exchange_coef, sunlight, mixing)
    back = turn(backward)

    step, top, done = call(
        functools.partial(stencil_kernel, lats),
        "stencil",
        [SMEM] + [VMEM] * 9 + [SMEM, ANY],
        (shape((32, 16, 384), F32), shape((4, 16, 384), F32), shape((48,), jnp.int32)),
        (VMEM, VMEM, SMEM),
        [pltpu.VMEM((2, 56, 384), F32), pltpu.VMEM((2, 32, 384), F32), pltpu.VMEM((5, 16, 384), F32)],
        cost_estimate=pl.CostEstimate(flops=8000000, bytes_accessed=3000000, transcendentals=0),
    )(
        land_mask,
        came,
        inner,
        cross,
        tracers_l,
        east_velocity,
        north_velocity,
        diffusivity,
        cross_diffusivity,
        depth_levels,
        code,
        backward,
    )

    back_cross, back_inner, heat = call(
        functools.partial(split_kernel, lats),
        "split",
        [VMEM, ANY],
        (shape((48, 8, 128), BF16), shape((48, 8, 128), BF16), shape((lats, 1, 128), F32)),
        (VMEM, VMEM, VMEM),
    )(back, done)
    heat = lax.all_to_all(heat, "lat", 0, 0, tiled=True)
    back_cross = lax.ppermute(back_cross, "lat", cross_pairs)
    back_inner = lax.ppermute(back_inner, "lat", inner_pairs)

    points = float(48 * 128 * lats * lons)
    ocean_flux, new_tracers = call(
        functools.partial(finish_kernel, points),
        "finish",
        [SMEM, SMEM, VMEM, VMEM, VMEM, VMEM, VMEM, VMEM, ANY],
        (shape((48, 8, 128), BF16), shape((4, 8, 16, 384), F32)),
        (VMEM, pl.BlockSpec((4, 1, 16, 384), lambda i: (0, 0, 0, 0))),
        [pltpu.VMEM((416, 128), F32)],
        grid=(1,),
        input_output_aliases={8: 1},
    )(done, land_mask, back, back_cross, back_inner, heat, depth_levels, top, step.reshape(4, 8, 16, 384))
    return (new_tracers, ocean_flux)


def solution(mesh):
    return jax.shard_map(
        shards,
        mesh=mesh,
        in_specs=(
            P(None, None, "lat", "lon"),
            P(None, "lat", "lon"),
            P(None, "lat", "lon"),
            P(None, "lat", "lon"),
            P(None, "lat", "lon"),
            P("lat", "lon"),
            P(("lat", "lon")),
            P(("lat", "lon"), None, None),
            P(("lat", "lon"), None, None),
            P(("lat", "lon"), None),
            P(("lat", "lon"), None),
            P(),
            P(("lat", "lon")),
            P(("lat", "lon")),
            P(("lat", "lon")),
            P(("lat", "lon")),
        ),
        out_specs=(P(None, None, "lat", "lon"), P(("lat", "lon"), None, None)),
        check_vma=False,
    )
```

```python
import functools

import jax
import jax.numpy as jnp
from jax import lax
from jax.experimental import pallas as pl
from jax.experimental.pallas import tpu as pltpu
from jax.sharding import PartitionSpec as P

F32 = jnp.float32
BF16 = jnp.bfloat16
PAIR = 6
SLOTS = 20
LAND = 2.0**100
LAND_TEST = 2.0**90
VMEM = pl.BlockSpec(memory_space=pltpu.VMEM)
SMEM = pl.BlockSpec(memory_space=pltpu.SMEM)
ANY = pl.BlockSpec(memory_space=pl.ANY)
HBM = pl.BlockSpec(memory_space=pltpu.HBM)
SMALL = 16 * 1024 * 1024


def iota(shape, dim):
    return lax.broadcasted_iota(jnp.int32, shape, dim)


def block_of(ref, block):
    return ref[..., 128 * block : 128 * block + 128]


def tile_column(land_ref, block):
    rows = iota((16, 128), 0)
    out = jnp.zeros((16, 128), F32)
    for r in range(16):
        out = jnp.where(rows == r, land_ref[3 * r + block].astype(F32), out)
    return out


def pack_kernel(lats, dest_hbm, land_hbm, state_hbm, tracer_hbm, east_hbm, kappa_hbm, depth_hbm,
                out_ref, code_ref, count_ref, dest_ref, land_ref, state_ref, tracer_ref, east_ref,
                kappa_ref, depth_ref, sems):
    first, last = pl.ds(0, 128), pl.ds(256, 128)
    copies = [
        pltpu.make_async_copy(source, target, sems.at[n])
        for n, (source, target) in enumerate(
            (
                (dest_hbm, dest_ref),
                (land_hbm, land_ref),
                (state_hbm, state_ref),
                (depth_hbm, depth_ref),
                (tracer_hbm.at[:, :, last], tracer_ref.at[0]),
                (tracer_hbm.at[:, :, first], tracer_ref.at[1]),
                (kappa_hbm.at[:, :, last], kappa_ref.at[0]),
                (kappa_hbm.at[:, :, first], kappa_ref.at[1]),
                (east_hbm.at[:, :, last], east_ref),
            )
        )
    ]
    for copy in copies:
        copy.start()
    lat = lax.axis_index("lat")
    lon = lax.axis_index("lon")
    lons = 8
    for i in range(24):
        count_ref[i] = 0
    for copy in copies[:3]:
        copy.wait()
    for t in range(48):
        dest = dest_ref[t]
        off = lax.shift_right_logical(dest, 3) - lat + 1
        off = jnp.where(off < 0, off + lats, jnp.where(off >= lats, off - lats, off))
        dlon = lax.bitwise_and(dest, 7)
        key = off * 8 + dlon
        rank = count_ref[key]
        count_ref[key] = rank + 1
        code_ref[t] = key * 8 + rank
        value = state_ref[t].astype(F32)
        value = jnp.where(land_ref[t] > 0, value, LAND)
        out_ref[dlon * SLOTS + off * PAIR + rank] = value.astype(BF16)
    for copy in copies[3:]:
        copy.wait()
    lanes = iota((16, 128), 1)
    for side, block, lane, shift in ((0, 2, 127, 1), (1, 0, 0, lons - 1)):
        packed = jnp.zeros((16, 128), F32)
        for i in range(32):
            packed = jnp.where(lanes == i, tracer_ref[side, i][:, lane : lane + 1], packed)
        for i in range(8):
            if side == 0:
                packed = jnp.where(lanes == 32 + i, east_ref[i][:, lane : lane + 1], packed)
            packed = jnp.where(lanes == 40 + i, kappa_ref[side, i][:, lane : lane + 1], packed)
        bottom = block_of(depth_ref, block)[...].astype(F32) * tile_column(land_ref, block)
        packed = jnp.where(lanes == 48, bottom[:, lane : lane + 1], packed)
        target = lax.rem(lon + shift, lons)
        out_ref[target * SLOTS + 18] = packed[:8].astype(BF16)
        out_ref[target * SLOTS + 19] = packed[8:].astype(BF16)


def by_parity(body, cross, inner):
    odd = lax.rem(lax.axis_index("lat"), 2)

    @pl.when(odd == 1)
    def _():
        body(cross, inner)

    @pl.when(odd == 0)
    def _():
        body(inner, cross)


def rows_kernel(land_ref, came_ref, tracer_ref, north_ref, kappa_ref, depth_ref, cross_ref, inner_ref):
    inputs = (land_ref, came_ref, tracer_ref, north_ref, kappa_ref, depth_ref)
    by_parity(functools.partial(fill_rows, *inputs), cross_ref, inner_ref)


def fill_rows(land_ref, came_ref, tracer_ref, north_ref, kappa_ref, depth_ref, up_ref, down_ref):
    lon = lax.axis_index("lon")
    west = lax.rem(lon + 7, 8)
    east = lax.rem(lon + 1, 8)
    subs = iota((8, 128), 0)
    for out_ref, first, row in ((up_ref, 12, 15), (down_ref, 0, 0)):
        for s in range(8):
            for k in range(PAIR):
                out_ref[s * PAIR + k] = came_ref[s * SLOTS + first + k]
        half, sub = (19, 7) if row else (18, 0)
        corners = (
            came_ref[west * SLOTS + half].astype(F32)[sub : sub + 1],
            None,
            came_ref[east * SLOTS + half].astype(F32)[sub : sub + 1],
        )
        for j in range(3):
            cols = slice(128 * j, 128 * j + 128)
            for k in range(4):
                out_ref[48 + 3 * k + j] = tracer_ref[8 * k : 8 * k + 8, row, cols].astype(BF16)
            if row:
                out_ref[48 + 12 + j] = north_ref[:, row, cols].astype(BF16)
            else:
                out_ref[48 + 12 + j] = jnp.zeros((8, 128), BF16)
            out_ref[48 + 15 + j] = kappa_ref[:, row, cols].astype(BF16)
            bottom = depth_ref[row : row + 1, cols].astype(F32) * land_ref[3 * row + j].astype(F32)
            last = jnp.where(subs == 0, bottom, 0.0)
            if j != 1:
                last = jnp.where(subs == 1, corners[j], last)
            out_ref[48 + 18 + j] = last.astype(BF16)


def couple_kernel(place_ref, came_ref, cross_ref, inner_ref, atm_ref, coef_ref, sun_ref, mixing_ref,
                  out_ref, got_ref):
    odd = lax.rem(lax.axis_index("lat"), 2)
    cross_off = jnp.where(odd == 1, 0, 2)
    total = jnp.zeros((8, 128), F32)
    for q in range(48):
        code = place_ref[q]
        rank = lax.bitwise_and(code, 7)
        slon = lax.bitwise_and(lax.shift_right_logical(code, 3), 7)
        off = lax.shift_right_logical(code, 6)
        at = slon * PAIR + rank
        own = came_ref[slon * SLOTS + PAIR + rank].astype(F32)
        cross = cross_ref[at].astype(F32)
        inner = inner_ref[at].astype(F32)
        value = jnp.where(off == 1, own, jnp.where(off == cross_off, cross, inner))
        got_ref[q] = value
        total = total + coef_ref[q : q + 1, :] * jnp.where(value < LAND_TEST, value, 0.0)
    weight = jnp.sum(jnp.sum(coef_ref[...], axis=0, keepdims=True), axis=1, keepdims=True)
    band_mean = jnp.sum(total, axis=1, keepdims=True) / weight
    mixing = mixing_ref[...]
    columns = [jnp.broadcast_to(mixing[:, g : g + 1], (8, 128)) for g in range(8)]
    heat = jnp.zeros((8, 128), F32)
    first = iota((8, 128), 0) == 0
    for q in range(48):
        code = place_ref[q]
        rank = lax.bitwise_and(code, 7)
        slon = lax.bitwise_and(lax.shift_right_logical(code, 3), 7)
        off = lax.shift_right_logical(code, 6)
        value = got_ref[q]
        wet = value < LAND_TEST
        drive = atm_ref[q] + band_mean - 2.0 * jnp.where(wet, value, 0.0)
        mixed = columns[0] * drive[0:1]
        for g in range(1, 8):
            mixed = mixed + columns[g] * drive[g : g + 1]
        coef = coef_ref[q : q + 1, :]
        flux = coef * mixed
        flux = flux + jnp.where(first, coef * sun_ref[q : q + 1, :], 0.0)
        rounded = flux.astype(BF16)
        out_ref[slon * SLOTS + off * PAIR + rank] = rounded
        heat = heat + jnp.where(wet, rounded.astype(F32), 0.0)
    subs = iota((8, 128), 0)
    row = jnp.broadcast_to(heat[0:1], (8, 128))
    one = row.astype(BF16).astype(F32)
    two = (row - one).astype(BF16).astype(F32)
    three = row - one - two
    parts = jnp.where(subs == 0, one, jnp.where(subs == 1, two, jnp.where(subs == 2, three, 0.0)))
    for s in range(8):
        out_ref[s * SLOTS + 18] = parts.astype(BF16)


def split_kernel(lats, back_ref, done_ref, cross_ref, inner_ref, heat_ref):
    odd = lax.rem(lax.axis_index("lat"), 2)
    cross_at = jnp.where(odd == 1, 0, 12)
    inner_at = 12 - cross_at
    heat = jnp.zeros((8, 128), F32)
    for s in range(8):
        heat = heat + back_ref[s * SLOTS + 18].astype(F32)
        for k in range(PAIR):
            cross_ref[s * PAIR + k] = back_ref[s * SLOTS + cross_at + k]
            inner_ref[s * PAIR + k] = back_ref[s * SLOTS + inner_at + k]
    row = jnp.sum(heat, axis=0, keepdims=True)
    heat_ref[...] = jnp.broadcast_to(row[None], (lats, 1, 128))


def stencil_kernel(lats, land_ref, came_ref, cross_halo_ref, inner_halo_ref, tracer_ref, east_ref, north_ref,
                   kappa_ref, cross_ref, depth_ref, code_ref, after_ref, out_ref, top_ref, gain_ref, done_ref,
                   rows_ref,
                   diag_ref, bottom_ref):
    lat = lax.axis_index("lat")
    lon = lax.axis_index("lon")
    west = lax.rem(lon + 7, 8)
    east = lax.rem(lon + 1, 8)
    full = (16, 384)
    lanes = iota(full, 1)
    subs = iota(full, 0)
    at_west, at_east = lanes == 0, lanes == 383
    at_south, at_north = subs == 0, subs == 15
    small = iota((8, 384), 1)
    lane8, sub8 = iota((8, 128), 1), iota((8, 128), 0)

    def columns_of(side):
        return jnp.concatenate(
            [came_ref[side * SLOTS + 18].astype(F32), came_ref[side * SLOTS + 19].astype(F32)], axis=0
        )

    def from_west(v, column):
        return jnp.where(at_west, column, pltpu.roll(v, 1, 1))

    def from_east(v, column):
        return jnp.where(at_east, column, pltpu.roll(v, 383, 1))

    def from_south(v, row):
        return jnp.where(at_south, row, pltpu.roll(v, 1, 0))

    def from_north(v, row):
        return jnp.where(at_north, row, pltpu.roll(v, 15, 0))

    col_west, col_east = columns_of(west), columns_of(east)

    def unpack_rows(high_ref, low_ref):
        for side, ref in enumerate((low_ref, high_ref)):
            inside = jnp.where(lat == (0, lats - 1)[side], 0.0, 1.0)
            for k in range(7):
                for j in range(3):
                    tile = ref[48 + 3 * k + j].astype(F32)
                    if k == 6:
                        tile = jnp.where(sub8 == 0, tile * inside, tile)
                    rows_ref[side, 8 * k : 8 * k + 8, 128 * j : 128 * j + 128] = tile

    by_parity(unpack_rows, cross_halo_ref, inner_halo_ref)
    for j in range(3):
        cols = slice(128 * j, 128 * j + 128)
        bottom_ref[0, :, cols] = depth_ref[:, cols].astype(F32) * tile_column(land_ref, j)
    bottom = bottom_ref[0]
    bottom_ref[1] = from_east(bottom, col_east[:, 48:49])
    bottom_ref[2] = from_west(bottom, col_west[:, 48:49])
    bottom_ref[3] = from_north(bottom, rows_ref[1, 48:49, :])
    bottom_ref[4] = from_south(bottom, rows_ref[0, 48:49, :])

    level8 = iota((8, 384), 0).astype(F32)
    for side in range(2):
        inside = jnp.where(lat == (0, lats - 1)[side], 0.0, 1.0)
        corner_w = jnp.broadcast_to(rows_ref[side, 49:50, 0:128], (8, 128))
        corner_e = jnp.broadcast_to(rows_ref[side, 49:50, 256:384], (8, 128))
        edge = jnp.broadcast_to(rows_ref[side, 48:49, :], (8, 384))
        edge_e = jnp.where(small == 383, corner_e[:, 48:49] * inside, pltpu.roll(edge, 383, 1))
        edge_w = jnp.where(small == 0, corner_w[:, 48:49] * inside, pltpu.roll(edge, 1, 1))
        for k in range(4):
            value = rows_ref[side, 8 * k : 8 * k + 8, :]
            pick = lane8 == sub8 + 8 * k
            value_e = jnp.sum(jnp.where(pick, corner_e, 0.0), axis=1, keepdims=True)
            value_w = jnp.sum(jnp.where(pick, corner_w, 0.0), axis=1, keepdims=True)
            value_e = jnp.where(small == 383, value_e, pltpu.roll(value, 383, 1))
            value_w = jnp.where(small == 0, value_w, pltpu.roll(value, 1, 1))
            diag_ref[side, 8 * k : 8 * k + 8, :] = jnp.where(level8 < edge_e, value_e, 0.0) - jnp.where(
                level8 < edge_w, value_w, 0.0
            )

    def level_step(l, carry):
        lf = l.astype(F32)
        cw = pltpu.roll(col_west, lax.rem(128 - l, 128), 1)
        ce = pltpu.roll(col_east, lax.rem(128 - l, 128), 1)
        masks = [(lf < bottom_ref[i]).astype(F32) for i in range(5)]
        mask, mask_e, mask_w, mask_n, mask_s = masks
        kappa = kappa_ref[l]
        velocity = east_ref[l]
        kap = 0.5 * (kappa + from_east(kappa, ce[:, 40:41]))
        open_face = mask * mask_e
        out_e = open_face * (jnp.maximum(velocity, 0.0) + kap)
        in_e = open_face * (kap - jnp.minimum(velocity, 0.0))
        velocity = from_west(velocity, cw[:, 32:33])
        kap = 0.5 * (kappa + from_west(kappa, cw[:, 40:41]))
        open_face = mask * mask_w
        in_w = open_face * (jnp.maximum(velocity, 0.0) + kap)
        out_w = open_face * (kap - jnp.minimum(velocity, 0.0))
        velocity = north_ref[l]
        kap = 0.5 * (kappa + from_north(kappa, rows_ref[1, pl.ds(40 + l, 1), :]))
        open_face = mask * mask_n
        out_n = open_face * (jnp.maximum(velocity, 0.0) + kap)
        in_n = open_face * (kap - jnp.minimum(velocity, 0.0))
        velocity = from_south(velocity, rows_ref[0, pl.ds(32 + l, 1), :])
        kap = 0.5 * (kappa + from_south(kappa, rows_ref[0, pl.ds(40 + l, 1), :]))
        open_face = mask * mask_s
        in_s = open_face * (jnp.maximum(velocity, 0.0) + kap)
        out_s = open_face * (kap - jnp.minimum(velocity, 0.0))
        keep = 1.0 - (out_e + out_w + out_n + out_s)
        cross = cross_ref[l] * mask
        for t in range(4):
            i = 8 * t + l
            c = tracer_ref[i]
            c_e = from_east(c, ce[:, 8 * t : 8 * t + 1])
            c_w = from_west(c, cw[:, 8 * t : 8 * t + 1])
            c_n = from_north(c, rows_ref[1, pl.ds(i, 1), :])
            c_s = from_south(c, rows_ref[0, pl.ds(i, 1), :])
            diag = mask_e * c_e - mask_w * c_w
            diag_n = from_north(diag, diag_ref[1, pl.ds(i, 1), :])
            diag_s = from_south(diag, diag_ref[0, pl.ds(i, 1), :])
            out_ref[i] = (
                keep * c + in_e * c_e + in_w * c_w + in_n * c_n + in_s * c_s + cross * (diag_n - diag_s)
            )
        return carry

    lax.fori_loop(0, 8, level_step, 0)
    for t in range(4):
        top_ref[t] = out_ref[8 * t]
    gain_ref[...] = jnp.where(bottom > 0.0, 0.5, 0.0)
    for t in range(48):
        done_ref[t] = code_ref[t] + 256 * land_ref[t]


def finish_kernel(points, code_ref, back_ref, cross_ref, inner_ref, heat_ref, gain_ref,
                  top_ref, step_hbm, flux_ref, out_ref, wide_ref):
    odd = lax.rem(lax.axis_index("lat"), 2)
    cross_off = jnp.where(odd == 1, 2, 0)
    for t in range(48):
        code = code_ref[t]
        rank = lax.bitwise_and(code, 7)
        dlon = lax.bitwise_and(lax.shift_right_logical(code, 3), 7)
        off = lax.bitwise_and(lax.shift_right_logical(code, 6), 3)
        at = dlon * PAIR + rank
        own = back_ref[dlon * SLOTS + PAIR + rank].astype(F32)
        cross = cross_ref[at].astype(F32)
        inner = inner_ref[at].astype(F32)
        value = jnp.where(off == 1, own, jnp.where(off == cross_off, cross, inner))
        value = jnp.where(code >= 256, value, 0.0)
        flux_ref[t] = value.astype(BF16)
        wide_ref[8 * t : 8 * t + 8, :] = value
    heat = jnp.sum(jnp.sum(heat_ref[...], axis=0), axis=1, keepdims=True)
    correction = heat / points
    for j in range(3):
        cols = slice(128 * j, 128 * j + 128)
        gain = gain_ref[:, cols]
        for t in range(4):
            force = wide_ref[pl.ds(8 * j + t, 16, stride=24), :]
            if t == 0:
                force = force - correction
            out_ref[t, 0, :, cols] = top_ref[t, :, cols] + gain * force


def call(kernel, name, in_specs, out_shape, out_specs, scratch=(), limit=SMALL, **more):
    return pl.pallas_call(
        kernel,
        out_shape=out_shape,
        in_specs=in_specs,
        out_specs=out_specs,
        scratch_shapes=list(scratch),
        name=name,
        compiler_params=pltpu.CompilerParams(vmem_limit_bytes=limit),
        **more,
    )


def shape(dims, dtype):
    return jax.ShapeDtypeStruct(dims, dtype)


def shards(
    tracers,
    east_velocity,
    north_velocity,
    diffusivity,
    cross_diffusivity,
    depth_levels,
    land_mask,
    ocean_state,
    atm_state,
    exchange_coef,
    sunlight,
    mixing,
    o2a_dest,
    o2a_slot,
    a2o_source,
    a2o_tile,
):
    lats = lax.axis_size("lat")
    lons = lax.axis_size("lon")
    lat = lax.axis_index("lat")
    cross_pairs, inner_pairs = [], []
    for i in range(0, lats, 2):
        north, south = i + 1, (i + lats - 1) % lats
        inner_pairs += [(i, north), (north, i)]
        cross_pairs += [(i, south), (south, i)]
    flat = (8 * SLOTS, 8, 128)

    def turn(values):
        values = values.reshape(8, SLOTS, 8, 128)
        return lax.all_to_all(values, "lon", 0, 0, tiled=True).reshape(flat)

    tracers_l = tracers.reshape(32, 16, 384)

    outgoing, code = call(
        functools.partial(pack_kernel, lats),
        "pack",
        [HBM] * 7,
        (shape(flat, BF16), shape((48,), jnp.int32)),
        (VMEM, SMEM),
        [
            pltpu.SMEM((24,), jnp.int32),
            pltpu.SMEM((48,), jnp.int32),
            pltpu.SMEM((48,), jnp.int32),
            pltpu.VMEM((48, 8, 128), BF16),
            pltpu.VMEM((2, 32, 16, 128), F32),
            pltpu.VMEM((8, 16, 128), F32),
            pltpu.VMEM((2, 8, 16, 128), F32),
            pltpu.VMEM((16, 384), jnp.int32),
            pltpu.SemaphoreType.DMA((9,)),
        ],
        limit=60 * 1024 * 1024,
    )(o2a_dest, land_mask, ocean_state, tracers_l, east_velocity, diffusivity, depth_levels)

    source_off = (lat - a2o_source // lons + 1) % lats
    same = a2o_source[:, None] == a2o_source[None, :]
    earlier = a2o_tile[None, :] < a2o_tile[:, None]
    source_rank = jnp.sum((same & earlier).astype(jnp.int32), axis=1)
    place = source_off * 64 + (a2o_source % lons) * 8 + source_rank

    came = turn(outgoing)
    row_shape = shape((69, 8, 128), BF16)
    cross, inner = call(
        rows_kernel,
        "rows",
        [SMEM, VMEM, VMEM, VMEM, VMEM, VMEM],
        (row_shape, row_shape),
        (VMEM, VMEM),
    )(
        land_mask,
        came,
        tracers_l,
        north_velocity,
        diffusivity,
        depth_levels,
    )
    cross = lax.ppermute(cross, "lat", cross_pairs)
    inner = lax.ppermute(inner, "lat", inner_pairs)

    backward = call(
        couple_kernel,
        "couple",
        [SMEM] + [VMEM] * 7,
        shape(flat, BF16),
        VMEM,
        [pltpu.VMEM((48, 8, 128), F32)],
    )(place, came, cross, inner, atm_state, exchange_coef, sunlight, mixing)
    back = turn(backward)

    step, top, gain, done = call(
        functools.partial(stencil_kernel, lats),
        "stencil",
        [SMEM] + [VMEM] * 9 + [SMEM, ANY],
        (shape((32, 16, 384), F32), shape((4, 16, 384), F32), shape((16, 384), F32), shape((48,), jnp.int32)),
        (VMEM, VMEM, VMEM, SMEM),
        [pltpu.VMEM((2, 56, 384), F32), pltpu.VMEM((2, 32, 384), F32), pltpu.VMEM((5, 16, 384), F32)],
        cost_estimate=pl.CostEstimate(flops=8000000, bytes_accessed=3000000, transcendentals=0),
    )(
        land_mask,
        came,
        cross,
        inner,
        tracers_l,
        east_velocity,
        north_velocity,
        diffusivity,
        cross_diffusivity,
        depth_levels,
        code,
        backward,
    )

    back_cross, back_inner, heat = call(
        functools.partial(split_kernel, lats),
        "split",
        [VMEM, ANY],
        (shape((48, 8, 128), BF16), shape((48, 8, 128), BF16), shape((lats, 1, 128), F32)),
        (VMEM, VMEM, VMEM),
    )(back, done)
    heat = lax.all_to_all(heat, "lat", 0, 0, tiled=True)
    back_cross = lax.ppermute(back_cross, "lat", cross_pairs)
    back_inner = lax.ppermute(back_inner, "lat", inner_pairs)

    points = float(48 * 128 * lats * lons)
    ocean_flux, new_tracers = call(
        functools.partial(finish_kernel, points),
        "finish",
        [SMEM, VMEM, VMEM, VMEM, VMEM, VMEM, VMEM, ANY],
        (shape((48, 8, 128), BF16), shape((4, 8, 16, 384), F32)),
        (VMEM, pl.BlockSpec((4, 1, 16, 384), lambda i: (0, 0, 0, 0))),
        [pltpu.VMEM((416, 128), F32)],
        grid=(1,),
        input_output_aliases={7: 1},
    )(done, back, back_cross, back_inner, heat, gain, top, step.reshape(4, 8, 16, 384))
    return (new_tracers, ocean_flux)


def solution(mesh):
    return jax.shard_map(
        shards,
        mesh=mesh,
        in_specs=(
            P(None, None, "lat", "lon"),
            P(None, "lat", "lon"),
            P(None, "lat", "lon"),
            P(None, "lat", "lon"),
            P(None, "lat", "lon"),
            P("lat", "lon"),
            P(("lat", "lon")),
            P(("lat", "lon"), None, None),
            P(("lat", "lon"), None, None),
            P(("lat", "lon"), None),
            P(("lat", "lon"), None),
            P(),
            P(("lat", "lon")),
            P(("lat", "lon")),
            P(("lat", "lon")),
            P(("lat", "lon")),
        ),
        out_specs=(P(None, None, "lat", "lon"), P(("lat", "lon"), None, None)),
        check_vma=False,
    )
```
